128 devices in a mesh: section: 2 (over core), expert: 16 (over y, z), tensor: 4 (over x).
Axes of the slice: x: 4, y: 4, z: 4, core: 2. Of those that a mesh axis runs over, the one named last changes fastest.
Arguments:
- inputs: bfloat16 [2, 2048, 1536], P(None, 'expert'), may hold values from -6 to 6
- cotangent: bfloat16 [2, 2048, 1536], P(None, 'expert'), may hold values from -6 to 6
- documents: int32 [2, 16, 128], P(None, 'expert'), may hold values from 0 to 3, never falling along the last dimension, each value on 1 to 64 neighbouring positions
- routes: int32 [2, 2048, 8], P(None, 'expert'), may hold values from 0 to 31, all different within a row; in each aligned block of 128 rows (0 to 127, 128 to 255, ..., all dimensions but the last counted through in order) at most 48 rows name the same one
- gain_attn: bfloat16 [2, 1536], P('section'), may hold values from 0.25 to 1.75
- w_query: bfloat16 [2, 1536, 1536], P('section', None, 'tensor'), may hold values from -0.15625 to 0.15625
- w_key: bfloat16 [2, 1536, 512], P('section', None, 'tensor'), may hold values from -0.15625 to 0.15625
- w_value: bfloat16 [2, 1536, 512], P('section', None, 'tensor'), may hold values from -0.15625 to 0.15625
- w_out: bfloat16 [2, 1536, 1536], P('section', 'tensor'), may hold values from -0.625 to 0.625
- gain_moe: bfloat16 [2, 1536], P('section'), may hold values from 0.25 to 1.75
- w_router: bfloat16 [2, 1536, 32], P('section'), may hold values from -0.078125 to 0.078125
- w_gate: bfloat16 [2, 32, 1536, 512], P('section', 'expert', None, 'tensor'), may hold values from -0.15625 to 0.15625
- w_up: bfloat16 [2, 32, 1536, 512], P('section', 'expert', None, 'tensor'), may hold values from -0.15625 to 0.15625
- w_down: bfloat16 [2, 32, 512, 1536], P('section', 'expert', 'tensor'), may hold values from -1 to 1
Outputs:
- activations: bfloat16 [2, 2, 2048, 1536], P('section', None, 'expert')
- input_grads: bfloat16 [2, 2, 2048, 1536], P('section', None, 'expert')
- grad_gain_attn: float32 [2, 1536], P('section')
- grad_query: float32 [2, 1536, 1536], P('section', None, 'tensor')
- grad_key: float32 [2, 1536, 512], P('section', None, 'tensor')
- grad_value: float32 [2, 1536, 512], P('section', None, 'tensor')
- grad_out: float32 [2, 1536, 1536], P('section', 'tensor')
- grad_gain_moe: float32 [2, 1536], P('section')
- grad_router: float32 [2, 1536, 32], P('section')
- grad_gate: float32 [2, 32, 1536, 512], P('section', 'expert', None, 'tensor')
- grad_up: float32 [2, 32, 1536, 512], P('section', 'expert', None, 'tensor')
- grad_down: float32 [2, 32, 512, 1536], P('section', 'expert', 'tensor')
The draws below stay inside these ranges and needn't reach their ends.
Inputs may be any that keep to these rules, and one draw needn't show every extreme that they name: `documents`: document numbers never fall within a sequence; a document has at most half of 128 tokens, and some document has exactly that many. `routes`: each token names 8 different experts. Among the tokens of one sequence no expert is named more than 48 times, and in every draw some expert is named exactly 48 times by the tokens of some sequence.
All inputs are finite; a program needn't handle non-finite values.
Results may differ from the reference program's by a relative error of at most 0.038.
Values may be sent and summed in bfloat16 or wider, within the bound.
No kernel may reach another device: no remote copies, remote signals or barrier semaphores. Data moves between devices by JAX's collectives and lax.ppermute only.
A program may use at most 256 MiB of HBM per device.

```python
import math
from functools import partial
import jax
import jax.numpy as jnp
import numpy as np
from jax import lax

D = 1536
HEADS = 24
KV_HEADS = 8
HEAD_DIM = 64
FF = 512
TOP = 8
ROWS = 128
MB = 2
DOCS = 4
EXPERTS = 32
SEQS = 16
TOKENS = 2048
CAP = 48


def level_of(key, extent, shards, smallest, largest):
    level, own = 1.0, jax.random.fold_in(key, 6)
    for dim, shards_of in shards:
        steps = jnp.exp(jax.random.uniform(jax.random.fold_in(own, dim), (shards_of,), jnp.float32, smallest / len(shards), largest / len(shards)))
        level = level * jnp.repeat(steps, extent[dim] // shards_of).reshape([-1 if axis == dim else 1 for axis in range(len(extent))])
    return level


def length_profile(count, total, most, slope):
    portions = [(1 << 20) // math.isqrt(standing ** slope) + 1 for standing in range(2, count + 1)]
    surplus, counts = total - most - (count - 1), [1] * (count - 1)
    while surplus > 0:
        free = [i for i in range(count - 1) if counts[i] < most]
        pool, remaining = sum([portions[i] for i in free]), surplus
        for i in free:
            more = min(most - counts[i], max(1, remaining * portions[i] // pool), surplus)
            counts[i] = counts[i] + more
            surplus = surplus - more
    return np.array([most] + counts)


def uneven_parts(rng, number_of, total, reach, lean):
    if number_of == 2:
        one = jax.random.randint(rng, (), max(1, total - reach), min(reach, total - 1) + 1)
        return jnp.stack([one, total - one])
    lengths = jnp.asarray(length_profile(number_of, total, reach, lean), jnp.int32)
    couples = (number_of - 1) // 2
    source_of, taker = lengths[1:1 + 2 * couples:2], lengths[2:2 + 2 * couples:2]
    margin = jnp.minimum(source_of - 1, reach - taker)
    shifted = jax.random.randint(jax.random.fold_in(rng, 1), (couples,), 0, 1 << 20) % (margin + 1)
    lengths = lengths.at[1:1 + 2 * couples:2].set(source_of - shifted).at[2:2 + 2 * couples:2].set(taker + shifted)
    return lengths[jax.random.permutation(jax.random.fold_in(rng, 2), number_of)]


def shared_out(own_key, own, number, rows, number_of, top, reach, slope):
    sequence = jax.random.permutation(own_key, number_of)
    packed, usual = shares(number_of, rows * top, reach, slope, True), shares(number_of, rows * top, reach, slope, False)
    places = jnp.arange(number_of)

    def named(tallies, turn):
        used = int((tallies > 0).sum())
        fixed = max(1, used // 4)
        moved = fixed + (places - fixed + turn * (used - fixed)) % max(1, number_of - fixed)
        return jnp.zeros((number_of,), jnp.int32).at[sequence[jnp.where(places < fixed, places, moved)]].set(jnp.asarray(tallies, jnp.int32))

    tallies = jnp.where(number % 4 == 0, named(packed, number // 4), named(usual, number - number // 4 - 1))
    mixed = jax.random.permutation(jax.random.fold_in(own, 3), number_of)
    source_of, taker = mixed[0:number_of // 2 * 2:2], mixed[1:number_of // 2 * 2:2]
    margin = jnp.minimum(tallies[source_of] - 1, reach - tallies[taker]) // 2
    margin = jnp.where((source_of == sequence[0]) | (taker == sequence[0]) | (tallies[taker] == 0), 0, jnp.maximum(margin, 0))
    moved = jax.random.randint(jax.random.fold_in(own, 4), (number_of // 2,), 0, 1 << 20) % (margin + 1)
    tallies = tallies.at[source_of].add(-moved).at[taker].add(moved)
    labels = jnp.searchsorted(jnp.cumsum(tallies), jnp.arange(rows * top), side="right").astype(jnp.int32)
    listing = labels.reshape(top, rows).T
    listing = listing[jax.random.permutation(jax.random.fold_in(own, 1), rows)]
    turn = jax.random.randint(jax.random.fold_in(own, 2), (rows, 1), 0, top)
    return jnp.take_along_axis(listing, (jnp.arange(top)[None, :] + turn) % top, axis=1)


def shares(number_of, total, bound, skew, full):
    portions = [(1 << 20) // math.isqrt(standing ** skew) + 1 for standing in range(1, number_of + 1)]
    largest = bound if full else min(bound, max(-(-total // number_of), total * portions[0] // sum(portions)))
    least = 1 if total - largest >= number_of - 1 else 0
    given, rest = [largest] + [least] * (number_of - 1), total - largest - least * (number_of - 1)
    while rest > 0:
        candidates = [i for i in range(1, number_of) if given[i] < largest] or [i for i in range(1, number_of) if given[i] < bound]
        mass, budget = sum([portions[i] for i in candidates]), rest
        for i in candidates:
            extra = min(bound - given[i], max(1, budget * portions[i] // mass), rest)
            given[i] = given[i] + extra
            rest = rest - extra
    return np.array(given)


def bell_draw(own_key, dims, width, most, shards=(), held_as=jnp.bfloat16):
    level = level_of(own_key, dims, shards, -0.22, 0.18) if shards else 1.0
    entries = jax.random.normal(own_key, dims, jnp.float32) * width * level
    return jnp.minimum(jnp.maximum(entries, -most), most).astype(held_as)


def setup_inputs(seed: int = 0) -> dict:
    streams_of = jax.random.split(jax.random.key(seed), 15)
    inputs = bell_draw(streams_of[0], (MB, TOKENS, D), 1.0, 6.0, ((1, 16),))
    cotangent = bell_draw(streams_of[1], (MB, TOKENS, D), 1.0, 6.0, ((1, 16),))
    documents = jax.vmap(lambda own: jnp.searchsorted(jnp.cumsum(uneven_parts(own, DOCS, ROWS, ROWS // 2, 0)), jnp.arange(ROWS), side="right"))(jax.random.split(streams_of[2], MB * SEQS)).reshape((MB, SEQS, ROWS)).astype(jnp.int32)
    routes_keys = jax.random.split(jax.random.fold_in(streams_of[3], 1), MB * TOKENS // ROWS)
    routes_turns = jax.random.permutation(jax.random.fold_in(streams_of[3], 3), MB * TOKENS // ROWS)
    routes = jax.vmap(lambda own, number: shared_out(jax.random.fold_in(streams_of[3], 2), own, number, ROWS, EXPERTS, TOP, CAP, 2))(routes_keys, routes_turns).reshape((MB, TOKENS, TOP))
    gain_attn = jnp.clip(1.0 + 0.15 * jax.random.normal(streams_of[4], (2, D), jnp.float32), 0.25, 1.75).astype(jnp.bfloat16)
    w_query = bell_draw(streams_of[5], (2, D, HEADS * HEAD_DIM), D ** -0.5, 0.15625, ((0, 2), (2, 4)))
    w_key = bell_draw(streams_of[6], (2, D, KV_HEADS * HEAD_DIM), D ** -0.5, 0.15625, ((0, 2), (2, 4)))
    w_value = bell_draw(streams_of[7], (2, D, KV_HEADS * HEAD_DIM), D ** -0.5, 0.15625, ((0, 2), (2, 4)))
    w_out = bell_draw(streams_of[8], (2, HEADS * HEAD_DIM, D), (HEADS * HEAD_DIM // 16) ** -0.5, 0.625, ((0, 2), (1, 4)))
    gain_moe = jnp.clip(1.0 + 0.15 * jax.random.normal(streams_of[9], (2, D), jnp.float32), 0.25, 1.75).astype(jnp.bfloat16)
    w_router = bell_draw(streams_of[10], (2, D, EXPERTS), (4 * D) ** -0.5, 0.078125, ((0, 2),))
    w_gate = bell_draw(streams_of[11], (2, EXPERTS, D, FF), D ** -0.5, 0.15625, ((0, 2), (1, 16), (3, 4)))
    w_up = bell_draw(streams_of[12], (2, EXPERTS, D, FF), D ** -0.5, 0.15625, ((0, 2), (1, 16), (3, 4)))
    w_down = bell_draw(streams_of[13], (2, EXPERTS, FF, D), (FF // 16) ** -0.5, 1.0, ((0, 2), (1, 16), (2, 4)))
    return {"inputs": inputs, "cotangent": cotangent, "documents": documents, "routes": routes, "gain_attn": gain_attn, "w_query": w_query, "w_key": w_key, "w_value": w_value, "w_out": w_out, "gain_moe": gain_moe, "w_router": w_router, "w_gate": w_gate, "w_up": w_up, "w_down": w_down}


@jax.custom_vjp
def low(v):
    return lax.optimization_barrier(v.astype(jnp.bfloat16)).astype(jnp.float32)

@jax.custom_vjp
def low_back(v):
    return v

def low_keep(v):
    return (low(v), None)

def low_pass(kept, grad):
    return (grad,)

def back_keep(v):
    return (v, None)

def back_low(kept, grad):
    return (low(grad),)
low.defvjp(low_keep, low_pass)
low_back.defvjp(back_keep, back_low)
EPSILON = 1e-06
HIGHEST = lax.Precision.HIGHEST

def rms_scaled(values, gain):
    return values * lax.rsqrt(lax.optimization_barrier(jnp.mean(values * values, axis=-1, keepdims=True)) + EPSILON) * gain

def rotate_half(values, cosine_table, sine_table):
    middle_at = values.shape[-1] // 2
    turned = jnp.concatenate([-values[..., middle_at:], values[..., :middle_at]], axis=-1)
    return values * cosine_table + turned * sine_table

def rope_tables(document):
    places = jnp.arange(document.shape[0], dtype=jnp.int32)
    starts = lax.optimization_barrier(jnp.sum((document[None, :] < document[:, None]).astype(jnp.int32), axis=1))
    offsets = (places - starts).astype(jnp.float32)
    frequency = jnp.exp(jnp.arange(HEAD_DIM // 2, dtype=jnp.float32) * (-2.0 * math.log(10000.0) / HEAD_DIM))
    angle_table = offsets[:, None] * frequency[None, :]
    angle_table = jnp.concatenate([angle_table, angle_table], axis=-1)
    return (jnp.cos(angle_table), jnp.sin(angle_table))

def allowed_pairs(document):
    places = jnp.arange(document.shape[0], dtype=jnp.int32)
    return (document[:, None] == document[None, :]) & (places[None, :] <= places[:, None])

def slot_numbers(route_rows, expert_count):
    flat_routes = route_rows.reshape(-1)
    onehot_hits = (flat_routes[:, None] == jnp.arange(expert_count, dtype=jnp.int32)[None, :]).astype(jnp.int32)
    earlier = jnp.cumsum(onehot_hits, axis=0) - onehot_hits
    return lax.optimization_barrier(jnp.sum(earlier * onehot_hits, axis=1)).reshape(route_rows.shape)

def attend_sequence(queries, key_rows, value_rows, document):
    cosine_table, sine_table = rope_tables(document)
    queries = low(rotate_half(queries, cosine_table[:, None, None, :], sine_table[:, None, None, :]))
    key_rows = low(rotate_half(key_rows, cosine_table[:, None, :], sine_table[:, None, :]))
    scores = low_back(jnp.einsum('qkgd,pkd->kgqp', queries, key_rows, precision=HIGHEST) * HEAD_DIM ** (-0.5))
    scores = jnp.where(allowed_pairs(document)[None, None], scores, -1e+30)
    row_peak = lax.optimization_barrier(jnp.max(scores, axis=-1, keepdims=True))
    exp_scores = jnp.exp(scores - row_peak)
    probability = exp_scores / lax.optimization_barrier(jnp.sum(exp_scores, axis=-1, keepdims=True))
    attended = jnp.einsum('kgqp,pkd->qkgd', low(probability), value_rows, precision=HIGHEST)
    return low(low_back(attended))

def layer(level_rows, params, document, route_ids, slot_ids):
    gain_attn, w_query, w_key, w_value, w_out, gain_moe, w_router, w_gate, w_up, w_down = params
    normed = low(rms_scaled(level_rows, gain_attn))
    queries = low_back(jnp.dot(normed, w_query, precision=HIGHEST)).reshape(SEQS, ROWS, KV_HEADS, HEADS // KV_HEADS, HEAD_DIM)
    key_rows = low_back(jnp.dot(normed, w_key, precision=HIGHEST)).reshape(SEQS, ROWS, KV_HEADS, HEAD_DIM)
    value_rows = low(low_back(jnp.dot(normed, w_value, precision=HIGHEST))).reshape(SEQS, ROWS, KV_HEADS, HEAD_DIM)
    attended = lax.map(lambda pieces: jax.checkpoint(attend_sequence)(*pieces), (queries, key_rows, value_rows, document))
    branch = low_back(jnp.dot(attended.reshape(TOKENS, HEADS * HEAD_DIM), w_out, precision=HIGHEST))
    middle = level_rows + branch
    shaped = low(rms_scaled(middle, gain_moe))
    logits = low_back(jnp.dot(shaped, w_router, precision=HIGHEST))
    gate_weights = jax.nn.softmax(jnp.take_along_axis(logits, route_ids, axis=1), axis=-1)
    blocks = jnp.arange(TOKENS, dtype=jnp.int32) // ROWS
    position = ((blocks[:, None] * EXPERTS + route_ids) * CAP + slot_ids).reshape(-1)
    buffer = jnp.zeros((SEQS * EXPERTS * CAP, D), jnp.float32).at[position].set(jnp.repeat(shaped, TOP, axis=0))
    arrived = low_back(buffer).reshape(SEQS, EXPERTS, CAP, D)
    gate_act = low_back(jnp.einsum('secd,edf->secf', arrived, w_gate, precision=HIGHEST))
    up_act = low_back(jnp.einsum('secd,edf->secf', arrived, w_up, precision=HIGHEST))
    hidden = low(jax.nn.silu(gate_act) * up_act)
    result = low(low_back(jnp.einsum('secf,efd->secd', hidden, w_down, precision=HIGHEST))).reshape(SEQS * EXPERTS * CAP, D)
    picked = result[position].reshape(TOKENS, TOP, D)
    return middle + lax.optimization_barrier(jnp.sum(gate_weights[..., None] * picked, axis=1))

def reference(inputs, cotangent, documents, routes, gain_attn, w_query, w_key, w_value, w_out, gain_moe, w_router, w_gate, w_up, w_down):
    stacked = (gain_attn, w_query, w_key, w_value, w_out, gain_moe, w_router, w_gate, w_up, w_down)
    slots_all = jax.vmap(lambda block_routes: slot_numbers(block_routes, EXPERTS))(routes.reshape(MB * SEQS, ROWS, TOP)).reshape(MB, TOKENS, TOP)
    outputs = [[], []]
    in_grads = [[], []]
    totals = [[jnp.zeros(weight_array.shape[1:], jnp.float32) for weight_array in stacked] for section_number in range(2)]
    for micro_index in range(MB):
        level_rows = inputs[micro_index].astype(jnp.float32)
        pullers = []
        for section_number in range(2):
            params = tuple((weight_array[section_number].astype(jnp.float32) for weight_array in stacked))
            bound_layer = partial(layer, document=documents[micro_index], route_ids=routes[micro_index], slot_ids=slots_all[micro_index])
            layer_out, puller = jax.vjp(bound_layer, level_rows, params)
            pullers.append(puller)
            rounded = layer_out.astype(jnp.bfloat16)
            outputs[section_number].append(rounded)
            level_rows = rounded.astype(jnp.float32)
        flowing = cotangent[micro_index].astype(jnp.float32)
        for section_number in (1, 0):
            input_grad, param_grads = pullers[section_number](flowing)
            rounded = input_grad.astype(jnp.bfloat16)
            in_grads[section_number].append(rounded)
            flowing = rounded.astype(jnp.float32)
            totals[section_number] = [running + piece_grad for running, piece_grad in zip(totals[section_number], param_grads)]
    activations = jnp.stack([jnp.stack(outputs[0]), jnp.stack(outputs[1])])
    input_grads = jnp.stack([jnp.stack(in_grads[0]), jnp.stack(in_grads[1])])
    joined = [jnp.stack([totals[0][number], totals[1][number]]) for number in range(10)]
    return (activations, input_grads, joined[0], joined[1], joined[2], joined[3], joined[4], joined[5], joined[6], joined[7], joined[8], joined[9])
```

```python
import math

import jax
import jax.numpy as jnp
from jax import lax
from jax.sharding import PartitionSpec as P

HEADS = 24
KV_HEADS = 8
HEAD_DIM = 64
EPSILON = 1e-06
BF = jnp.bfloat16
F32 = jnp.float32


def shifted(array, axis, by):
    length = lax.axis_size(axis)
    return lax.ppermute(array, axis, [(i, (i + by) % length) for i in range(length)])


def sibling(array):
    return shifted(array, "section", 1)


def gather_x(block):
    ahead = {k: shifted(block, "tensor", -k) for k in (1, 3, 2)}
    return [block, ahead[1], ahead[2], ahead[3]]


def gather_x_ring(block, dim):
    one, three = shifted(block, "tensor", -1), shifted(block, "tensor", 1)
    half = block.shape[dim] // 2
    low = shifted(lax.slice_in_dim(one, 0, half, axis=dim), "tensor", -1)
    high = shifted(lax.slice_in_dim(three, half, 2 * half, axis=dim), "tensor", 1)
    return [block, one, jnp.concatenate([low, high], dim), three]


def scatter_x(blocks):
    total = blocks[0].astype(F32)
    for k in (1, 3, 2):
        total = total + shifted(blocks[k].astype(BF), "tensor", k).astype(F32)
    return total


def spread_e(block):
    copies = jnp.broadcast_to(block[None], (lax.axis_size("expert"), *block.shape))
    return lax.all_to_all(copies, "expert", 0, 0, tiled=True)


def collect_e(blocks):
    pieces = lax.all_to_all(blocks, "expert", 0, 0, tiled=True)
    return jnp.sum(pieces.astype(F32), axis=0)


def rotate_half(values, cosine_table, sine_table):
    middle_at = values.shape[-1] // 2
    turned = jnp.concatenate([-values[..., middle_at:], values[..., :middle_at]], axis=-1)
    return values * cosine_table + turned * sine_table


def rotate_back(values, cosine_table, sine_table):
    middle_at = values.shape[-1] // 2
    scaled = values * sine_table
    return values * cosine_table + jnp.concatenate(
        [scaled[..., middle_at:], -scaled[..., :middle_at]], axis=-1
    )


def rope_tables(document, places):
    starts = jnp.sum((document[None, :] < document[:, None]).astype(jnp.int32), axis=1)
    offsets = (places - starts).astype(F32)
    frequency = jnp.exp(
        jnp.arange(HEAD_DIM // 2, dtype=F32) * (-2.0 * math.log(10000.0) / HEAD_DIM)
    )
    angle_table = offsets[:, None] * frequency[None, :]
    angle_table = jnp.concatenate([angle_table, angle_table], axis=-1)
    return (jnp.cos(angle_table), jnp.sin(angle_table))


def norm_parts(level_rows, gain):
    inverse = lax.rsqrt(jnp.mean(level_rows * level_rows, axis=-1, keepdims=True) + EPSILON)
    unit_rows = level_rows * inverse
    return (inverse, unit_rows, unit_rows * gain.astype(F32))


def norm_back(back_scaled, inverse, unit_rows, gain):
    back_unit = back_scaled * gain.astype(F32)
    back_level = inverse * (
        back_unit - unit_rows * jnp.mean(back_unit * unit_rows, axis=-1, keepdims=True)
    )
    return (back_level, jnp.sum(back_scaled * unit_rows, axis=0))


def dot(left, right):
    return jnp.dot(left, right, preferred_element_type=F32)


def contract_rows(left_rows, right_rows):
    return lax.dot_general(
        left_rows, right_rows, (((0,), (0,)), ((), ())), preferred_element_type=F32
    )


def contract_cols(left_rows, right_rows):
    return lax.dot_general(
        left_rows, right_rows, (((1,), (1,)), ((), ())), preferred_element_type=F32
    )


def score_table(queries, key_rows, allowed):
    raw_scores = jnp.einsum(
        "qkgd,pkd->kgqp", queries, key_rows, preferred_element_type=F32
    ) * HEAD_DIM ** (-0.5)
    return jnp.where(allowed[None, None], raw_scores, -1e30)


def attention_forward(entry, tables, allowed, w_qkv, w_out, gain):
    cosine_table, sine_table = tables
    rows = entry.shape[0]
    normed = norm_parts(entry.astype(F32), gain)[2].astype(BF)
    q_cols, kv_cols = w_out.shape[0], (w_qkv.shape[1] - w_out.shape[0]) // 2
    groups = kv_cols // HEAD_DIM
    raw = dot(normed, w_qkv)
    queries = rotate_half(
        raw[:, :q_cols].reshape(rows, groups, -1, HEAD_DIM),
        cosine_table[:, None, None, :],
        sine_table[:, None, None, :],
    ).astype(BF)
    keys = rotate_half(
        raw[:, q_cols : q_cols + kv_cols].reshape(rows, groups, HEAD_DIM),
        cosine_table[:, None, :],
        sine_table[:, None, :],
    ).astype(BF)
    values = raw[:, q_cols + kv_cols :].astype(BF).reshape(rows, groups, HEAD_DIM)
    scores = score_table(queries, keys, allowed)
    row_peak = jnp.max(scores, axis=-1, keepdims=True)
    exp_scores = jnp.exp(scores - row_peak)
    row_total = jnp.sum(exp_scores, axis=-1, keepdims=True)
    probability = exp_scores / row_total
    log_total = row_peak + jnp.log(row_total)
    attended = jnp.einsum(
        "kgqp,pkd->qkgd", probability.astype(BF), values, preferred_element_type=F32
    )
    attended = attended.astype(BF).reshape(rows, q_cols)
    partial = dot(attended, w_out)
    return partial, (normed, queries, keys, values, log_total, attended)


def attention_backward(back_branch, saved, tables, allowed, w_qkv, w_out):
    normed, queries, keys, values, log_total, attended = saved
    cosine_table, sine_table = tables
    rows = back_branch.shape[0]
    grad_out = contract_rows(attended, back_branch)
    back_attended = contract_cols(back_branch, w_out).astype(BF).reshape(queries.shape)
    scores = score_table(queries, keys, allowed)
    probability = jnp.exp(scores - log_total)
    back_probs = jnp.einsum("qkgd,pkd->kgqp", back_attended, values, preferred_element_type=F32)
    back_values = jnp.einsum(
        "kgqp,qkgd->pkd", probability.astype(BF), back_attended, preferred_element_type=F32
    )
    row_delta = jnp.sum(back_probs * probability, axis=-1, keepdims=True)
    back_scores = (probability * (back_probs - row_delta)).astype(BF)
    scale_factor = HEAD_DIM ** (-0.5)
    back_queries = (
        jnp.einsum("kgqp,pkd->qkgd", back_scores, keys, preferred_element_type=F32) * scale_factor
    )
    back_keys = (
        jnp.einsum("kgqp,qkgd->pkd", back_scores, queries, preferred_element_type=F32)
        * scale_factor
    )
    back_queries = rotate_back(
        back_queries, cosine_table[:, None, None, :], sine_table[:, None, None, :]
    ).reshape(rows, -1)
    back_keys = rotate_back(
        back_keys, cosine_table[:, None, :], sine_table[:, None, :]
    ).reshape(rows, -1)
    back_qkv = jnp.concatenate(
        [back_queries.astype(BF), back_keys.astype(BF), back_values.reshape(rows, -1).astype(BF)],
        axis=1,
    )
    grad_qkv = contract_rows(back_qkv, normed)
    partial = contract_cols(back_qkv, w_qkv)
    return partial, jnp.concatenate([grad_qkv, grad_out], axis=0)


def gate_table(rows, named, w_router, mine):
    logits = dot(rows, w_router)
    masked = jnp.where(named, logits, -1e30)
    peak = jnp.max(masked, axis=-1, keepdims=True)
    raised = jnp.where(named, jnp.exp(masked - peak), 0.0)
    gates = raised / jnp.sum(raised, axis=-1, keepdims=True)
    return jnp.einsum("re,ke->kr", gates, mine, precision=lax.Precision.HIGHEST)


def experts_forward(rows, gates, w_gu, w_down):
    total = 0.0
    kept = []
    for k in range(2):
        width = w_gu[k][0].shape[1] // 2
        for gate_up, down in zip(w_gu[k], w_down[k]):
            pre = dot(rows, gate_up)
            gate_act, up_act = pre[:, :width], pre[:, width:]
            hidden = (jax.nn.silu(gate_act) * up_act).astype(BF)
            kept.append((gate_act, up_act, hidden))
            total = total + gates[k][:, None] * dot(hidden, down)
    return total, kept


def experts_backward(rows, back, slope, gates, kept, w_gu, w_down):
    total = 0.0
    grads = []
    back_logits = []
    for k in range(2):
        kept_k = kept[4 * k : 4 * k + 4]
        raw = [contract_cols(back, down) for down in w_down[k]]
        back_gate = sum(
            jnp.sum(r * hidden.astype(F32), axis=1) for r, (_, _, hidden) in zip(raw, kept_k)
        )
        back_logits.append(gates[k] * (back_gate - slope))
        gate = gates[k][:, None]
        blocks = []
        for r, (gate_act, up_act, hidden), gate_up in zip(raw, kept_k, w_gu[k]):
            back_hidden = gate * r
            sigmoid = jax.nn.sigmoid(gate_act)
            back_pre = jnp.concatenate(
                [
                    (back_hidden * up_act * sigmoid * (1.0 + gate_act * (1.0 - sigmoid))).astype(BF),
                    (back_hidden * gate_act * sigmoid).astype(BF),
                ],
                axis=1,
            )
            total = total + contract_cols(back_pre, gate_up)
            grad_gu = contract_rows(rows, back_pre)
            grad_down = contract_rows((gate * hidden.astype(F32)).astype(BF), back)
            blocks.append((grad_gu, grad_down))
        grads.append(blocks)
    return total, grads, jnp.stack(back_logits)


def per_device(
    inputs,
    cotangent,
    documents,
    routes,
    gain_attn,
    w_query,
    w_key,
    w_value,
    w_out,
    gain_moe,
    w_router,
    w_gate,
    w_up,
    w_down,
):
    section = lax.axis_index("section")
    expert = lax.axis_index("expert")
    tensor = lax.axis_index("tensor")
    first = section == 0
    rows, width = inputs.shape[1:]
    own_rows = rows // 4
    expert_count = w_router.shape[2]

    def turned(array):
        array = lax.dynamic_index_in_dim(array, section, 0, keepdims=False)
        return jnp.roll(array, -own_rows * tensor, axis=0)

    def both_layers(own):
        other = sibling(own)
        return jnp.where(first, own, other), jnp.where(first, other, own)

    w_qkv = jnp.concatenate([w_query[0], w_key[0], w_value[0]], axis=1)
    w_qkvs = both_layers(w_qkv)
    w_outs = both_layers(w_out[0])
    small = jnp.concatenate([gain_attn, gain_moe, w_router[0].T], axis=0)
    smalls = both_layers(small)

    w_gu = jnp.concatenate([w_gate[0], w_up[0]], axis=2)
    quarter = []
    for array in (w_gu, w_down[0]):
        kept = lax.dynamic_index_in_dim(array, section, 0, keepdims=False)
        given = sibling(lax.dynamic_index_in_dim(array, 1 - section, 0, keepdims=False))
        quarter.append((jnp.where(first, kept, given), jnp.where(first, given, kept)))
    w_gus, w_downs = [], []
    for layer in range(2):
        mine = gather_x_ring(quarter[0][layer], 0)
        w_gus.append((mine, [sibling(block) for block in mine]))
        mine = gather_x_ring(quarter[1][layer], 0)
        w_downs.append((mine, [sibling(block) for block in mine]))

    places = (jnp.arange(rows, dtype=jnp.int32) + own_rows * tensor) % rows
    document = turned(documents[:, 0])
    allowed = (document[:, None] == document[None, :]) & (places[None, :] <= places[:, None])
    tables = rope_tables(document, places)
    names = spread_e(turned(routes)[:own_rows]).reshape(-1, routes.shape[2])
    named = jnp.any(
        names[:, :, None] == jnp.arange(expert_count, dtype=jnp.int32)[None, None, :], axis=1
    )
    mine = jnp.stack(
        [
            (jnp.arange(expert_count) == 2 * expert + section).astype(F32),
            (jnp.arange(expert_count) == 2 * expert + 1 - section).astype(F32),
        ]
    )

    state = []
    outputs = []
    entry = turned(inputs)
    for layer in range(2):
        gain_a, gain_m, router = smalls[layer][0], smalls[layer][1], smalls[layer][2:].T
        partial, attn_saved = attention_forward(
            entry, tables, allowed, w_qkvs[layer], w_outs[layer], gain_a
        )
        entry_own = entry[:own_rows].astype(F32)
        middle = entry_own + scatter_x([partial[own_rows * k : own_rows * (k + 1)] for k in range(4)])
        shaped = norm_parts(middle, gain_m)[2].astype(BF)
        arrived = spread_e(shaped).reshape(-1, width)
        gates = gate_table(arrived, named, router, mine)
        terms, kept = experts_forward(arrived, gates, w_gus[layer], w_downs[layer])
        moe = collect_e(terms.astype(BF).reshape(-1, own_rows, width))
        out_own = (middle + moe).astype(BF)
        entry_saved = entry_own
        entry = jnp.concatenate(gather_x(out_own), axis=0)
        outputs.append(entry)
        state.append((entry_saved, attn_saved, middle, arrived, gates, kept, moe))

    flow = turned(cotangent)[:own_rows]
    in_grads = [None, None]
    expert_grads = [None, None]
    packs = [None, None]
    small_grads = [None, None]
    for layer in (1, 0):
        gain_a, gain_m, router = smalls[layer][0], smalls[layer][1], smalls[layer][2:].T
        entry_own, attn_saved, middle, arrived, gates, kept, moe = state[layer]
        flowing = flow.astype(F32)
        slope = jnp.sum(flowing * moe, axis=-1, keepdims=True)
        slope_high = slope.astype(BF)
        slope_low = (slope - slope_high.astype(F32)).astype(BF)
        extra = jnp.concatenate(
            [slope_high, slope_low, jnp.zeros((own_rows, 126), BF)], axis=1
        )
        moved = spread_e(jnp.concatenate([flow, extra], axis=1)).reshape(-1, width + 128)
        back = moved[:, :width]
        slope_all = moved[:, width].astype(F32) + moved[:, width + 1].astype(F32)
        terms, grads, back_logits = experts_backward(
            arrived, back, slope_all, gates, kept, w_gus[layer], w_downs[layer]
        )
        back_table = dot(back_logits.T, mine).astype(BF)
        terms = terms + contract_cols(back_table, router)
        grad_router = contract_rows(back_table, arrived)
        back_shaped = collect_e(terms.astype(BF).reshape(-1, own_rows, width))
        inverse, unit, _ = norm_parts(middle, gain_m)
        back_norm, grad_gain_m = norm_back(back_shaped, inverse, unit, gain_m)
        back_middle = flowing + back_norm
        branch = jnp.concatenate(gather_x(back_middle.astype(BF)), axis=0)
        partial, packs[layer] = attention_backward(
            branch, attn_saved, tables, allowed, w_qkvs[layer], w_outs[layer]
        )
        back_normed = scatter_x([partial[own_rows * k : own_rows * (k + 1)] for k in range(4)])
        inverse, unit, _ = norm_parts(entry_own, gain_a)
        back_norm, grad_gain_a = norm_back(back_normed, inverse, unit, gain_a)
        flow = (back_middle + back_norm).astype(BF)
        in_grads[layer] = jnp.concatenate(gather_x(flow), axis=0)
        padding = jnp.zeros((64 - 2 - expert_count, width), F32)
        small_grads[layer] = jnp.concatenate(
            [grad_gain_a[None], grad_gain_m[None], grad_router, padding], axis=0
        )
        sums = []
        for number in range(2):
            own = [block[number] for block in grads[0]]
            other = [sibling(block[number].astype(BF)).astype(F32) for block in grads[1]]
            sums.append(scatter_x([a + b for a, b in zip(own, other)]))
        expert_grads[layer] = sums

    def owners(of_first, of_second):
        own = jnp.where(first, of_first, of_second)
        other = sibling(jnp.where(first, of_second, of_first).astype(BF)).astype(F32)
        return own, other

    def in_order(own, other):
        return jnp.where(first, jnp.stack([own, other]), jnp.stack([other, own]))

    whole = []
    for number in range(2):
        whole.append(in_order(*owners(expert_grads[0][number], expert_grads[1][number])))
    half_width = w_gate.shape[3]
    grad_gate, grad_up = whole[0][:, :, :half_width], whole[0][:, :, half_width:]
    grad_down = whole[1]

    halves = []
    for layer in range(2):
        half = packs[layer].shape[0] // 2
        kept_half = lax.dynamic_slice_in_dim(packs[layer], section * half, half, 0)
        given = lax.dynamic_slice_in_dim(packs[layer], (1 - section) * half, half, 0)
        joined = kept_half + sibling(given.astype(BF)).astype(F32)
        piece = collect_e(joined.astype(BF).reshape(16, -1, width))
        halves.append(spread_e(piece.astype(BF)).reshape(half, width).astype(F32))
    pack = in_order(*owners(halves[0], halves[1])).reshape(-1, width)
    q_cols, kv_cols = w_query.shape[2], w_key.shape[2]
    bounds = [0, q_cols, q_cols + kv_cols, q_cols + 2 * kv_cols, pack.shape[0]]
    grad_query, grad_key, grad_value, grad_out = (
        pack[a:b] for a, b in zip(bounds[:-1], bounds[1:])
    )

    small_own, small_other = owners(small_grads[0], small_grads[1])
    small_sum = jnp.roll(small_own + small_other, -16 * tensor, axis=0)
    small_sum = scatter_x([small_sum[16 * k : 16 * (k + 1)] for k in range(4)])
    small_sum = jnp.sum(spread_e(small_sum.astype(BF)).astype(F32), axis=0)
    small_total = jnp.concatenate(gather_x(small_sum.astype(BF)), axis=0)
    small_total = jnp.roll(small_total, 16 * tensor, axis=0).astype(F32)

    def straight(array):
        return jnp.roll(array, own_rows * tensor, axis=0)

    def by_batch(of_first, of_second):
        own = straight(jnp.where(first, of_first, of_second))
        other = sibling(straight(jnp.where(first, of_second, of_first)))
        return jnp.where(first, jnp.stack([own, other]), jnp.stack([other, own]))

    activations = by_batch(outputs[0], outputs[1])
    input_grads = by_batch(in_grads[0], in_grads[1])
    return (
        activations[None],
        input_grads[None],
        small_total[:1],
        grad_query.T[None],
        grad_key.T[None],
        grad_value.T[None],
        grad_out[None],
        small_total[1:2],
        small_total[2 : 2 + expert_count].T[None],
        grad_gate[None],
        grad_up[None],
        grad_down[None],
    )


def solution(mesh):
    in_specs = (
        P(None, "expert", None),
        P(None, "expert", None),
        P(None, "expert", None),
        P(None, "expert", None),
        P("section", None),
        P("section", None, "tensor"),
        P("section", None, "tensor"),
        P("section", None, "tensor"),
        P("section", "tensor", None),
        P("section", None),
        P("section", None, None),
        P("section", "expert", None, "tensor"),
        P("section", "expert", None, "tensor"),
        P("section", "expert", "tensor", None),
    )
    out_specs = (
        P("section", None, "expert", None),
        P("section", None, "expert", None),
        P("section", None),
        P("section", None, "tensor"),
        P("section", None, "tensor"),
        P("section", None, "tensor"),
        P("section", "tensor", None),
        P("section", None),
        P("section", None, None),
        P("section", "expert", None, "tensor"),
        P("section", "expert", None, "tensor"),
        P("section", "expert", "tensor", None),
    )
    return jax.shard_map(
        per_device, mesh=mesh, in_specs=in_specs, out_specs=out_specs, check_vma=False
    )
```

```python
import math

import jax
import jax.numpy as jnp
from jax import lax
from jax.experimental import pallas as pl
from jax.experimental.pallas import tpu as pltpu
from jax.sharding import PartitionSpec as P

HEADS = 24
KV_HEADS = 8
HEAD_DIM = 64
SHARING = HEADS // KV_HEADS
EPSILON = 1e-06
LOWEST = -1e30
BF = jnp.bfloat16
F32 = jnp.float32
ANY = pl.BlockSpec(memory_space=pl.ANY)
WHOLE = pl.BlockSpec(memory_space=pltpu.VMEM)
SCALARS = pl.BlockSpec(memory_space=pltpu.SMEM)
BESIDE = 128


def shifted(array, axis, by):
    length = lax.axis_size(axis)
    return lax.ppermute(array, axis, [(i, (i + by) % length) for i in range(length)])


def sibling(array):
    return shifted(array, "section", 1)


def to_core(array, core):
    return lax.ppermute(array, "section", [(1 - core, core)])


def after(value, *others):
    return lax.optimization_barrier((value, *others))[0]


def gather_x(block):
    ahead = {k: shifted(block, "tensor", -k) for k in (1, 3, 2)}
    return [block, ahead[1], ahead[2], ahead[3]]


def arrivals(blocks):
    return [blocks[0]] + [shifted(blocks[k], "tensor", k) for k in (1, 2, 3)]


def sum_of(blocks):
    return sum(block.astype(F32) for block in blocks).astype(BF)


def spread_e(block):
    return exchange_e(jnp.broadcast_to(block[None], (lax.axis_size("expert"), *block.shape)))


def exchange_e(blocks):
    return lax.all_to_all(blocks, "expert", 0, 0, tiled=True)


def collect_e(blocks):
    return jnp.sum(exchange_e(blocks).astype(F32), axis=0).astype(BF)


def dot(left, right):
    return jnp.dot(left, right, preferred_element_type=F32)


def contract_rows(left, right):
    return lax.dot_general(left, right, (((0,), (0,)), ((), ())), preferred_element_type=F32)


def contract_cols(left, right):
    return lax.dot_general(left, right, (((1,), (1,)), ((), ())), preferred_element_type=F32)


def call(kernel, outs, args, specs, scratch=(), grid=None, out_specs=None):
    extra = {} if grid is None else {"grid": grid}
    return pl.pallas_call(
        kernel,
        out_shape=[jax.ShapeDtypeStruct(shape, kind) for shape, kind in outs],
        in_specs=specs,
        out_specs=out_specs or [WHOLE] * len(outs),
        scratch_shapes=list(scratch),
        compiler_params=pltpu.CompilerParams(vmem_limit_bytes=60 * 2**20),
        cost_estimate=pl.CostEstimate(flops=1, bytes_accessed=1, transcendentals=0),
        **extra,
    )(*args)


def inverse_level(rows):
    return lax.rsqrt(jnp.mean(rows * rows, axis=-1, keepdims=True) + EPSILON)


def norm_back(back_scaled, rows, gain):
    inverse = inverse_level(rows)
    unit = rows * inverse
    back_unit = back_scaled * gain
    level = inverse * (back_unit - unit * jnp.mean(back_unit * unit, axis=-1, keepdims=True))
    return level, jnp.sum(back_scaled * unit, axis=0, keepdims=True)


def of_layer(layer, section, own, other):
    return jnp.where(section == layer, own[...].astype(F32), other[...].astype(F32))


def prepare_tables(place, documents, columns):
    rows = documents.shape[2]
    share = rows // 4

    def kernel(at, doc_ref, cos, sin, mask):
        turn = share * at[1]
        doc = pltpu.roll(doc_ref[at[0]].astype(F32), lax.rem(rows - turn, rows), 1)
        along = jnp.broadcast_to(doc, (rows, rows))
        down = along.T
        place_along = lax.rem(lax.broadcasted_iota(jnp.int32, (rows, rows), 1) + turn, rows)
        place_down = lax.rem(lax.broadcasted_iota(jnp.int32, (rows, rows), 0) + turn, rows)
        mask[...] = jnp.where((along == down) & (place_along <= place_down), 0.0, LOWEST)
        starts = jnp.sum(jnp.where(along < down, 1.0, 0.0), axis=1, keepdims=True)
        lane = lax.broadcasted_iota(jnp.int32, (rows, 128), 1)
        frequency = jnp.exp(lax.rem(lane, HEAD_DIM // 2).astype(F32) * (-2.0 * math.log(10000.0) / HEAD_DIM))
        offset = place_down[:, :1].astype(F32) - starts
        angle = offset * frequency
        for ref, table in ((cos, jnp.cos(angle)), (sin, jnp.sin(angle))):
            for a in range(0, columns, 128):
                ref[:, a : a + 128] = table

    return call(
        kernel,
        [((rows, columns), F32), ((rows, columns), F32), ((rows, rows), F32)],
        [place, documents],
        [SCALARS, WHOLE],
    )


def half_turn(values):
    lane = lax.broadcasted_iota(jnp.int32, values.shape, 1)
    width = values.shape[1]
    behind = pltpu.roll(values, width - HEAD_DIM // 2, 1)
    before = pltpu.roll(values, HEAD_DIM // 2, 1)
    return jnp.where(lane % HEAD_DIM < HEAD_DIM // 2, -behind, before)


def pick(layer, section, own, other, target, sem, start):
    for here, source in ((True, own), (False, other)):

        @pl.when((section == layer) == here)
        def _():
            copy = pltpu.make_async_copy(source, target, sem)
            copy.start() if start else copy.wait()


def pick_all(layer, section, weights, qkv, out, sems, which, start):
    at = 0
    for i in range(4):
        width = weights[i].shape[1]
        target = out if i == 3 else qkv.at[:, at : at + width]
        at += width
        if i in which:
            pick(layer, section, weights[i], weights[4 + i], target, sems.at[i], start)


def attention_forward(source, tables, weights, gains, place, layer):
    width, q_cols = weights[0].shape
    kv_cols = weights[1].shape[1]
    all_cols = q_cols + 2 * kv_cols
    heads = q_cols // HEAD_DIM
    rows = tables[0].shape[0]
    share = rows // 4
    entries = len(source)

    def kernel(at, *refs):
        entry, refs = refs[:entries], refs[entries:]
        (cos, sin, allowed, gain_own, gain_other), refs = refs[:5], refs[5:]
        parts, refs = refs[:8], refs[8:]
        (p0, p1, p2, p3, normed, qkv, lse, attended, w_qkv, w_out, staged, sems) = refs
        section = at[0]
        if entries == 1:
            copies = [
                pltpu.make_async_copy(
                    entry[0].at[section, pl.ds(pl.multiple_of(share * lax.rem(at[1] + k, 4), share), share)],
                    staged.at[share * k : share * (k + 1)],
                    sems.at[4 + k],
                )
                for k in range(4)
            ]
            for copy in copies:
                copy.start()
        pick_all(layer, section, parts, w_qkv, w_out, sems, range(4), True)
        gain = of_layer(layer, section, gain_own, gain_other)
        for k in range(4):
            if entries == 1:
                copies[k].wait()
                x = staged[share * k : share * (k + 1), :].astype(F32)
            else:
                x = entry[k][...].astype(F32)
            normed[share * k : share * (k + 1), :] = (x * inverse_level(x) * gain).astype(BF)
        pick_all(layer, section, parts, w_qkv, w_out, sems, range(3), False)
        raw = dot(normed[...], w_qkv[...])
        turned = raw[:, : q_cols + kv_cols]
        turned = turned * cos[...] + half_turn(turned) * sin[...]
        qkv[:, : q_cols + kv_cols] = turned.astype(BF)
        qkv[:, q_cols + kv_cols :] = raw[:, q_cols + kv_cols :].astype(BF)
        sums = jnp.zeros((rows, 128), F32)
        lane = lax.broadcasted_iota(jnp.int32, (rows, 128), 1)
        for h in range(heads):
            g = h // SHARING
            q = qkv[:, HEAD_DIM * h : HEAD_DIM * (h + 1)]
            key = qkv[:, q_cols + HEAD_DIM * g : q_cols + HEAD_DIM * (g + 1)]
            value = qkv[:, q_cols + kv_cols + HEAD_DIM * g : q_cols + kv_cols + HEAD_DIM * (g + 1)]
            scores = contract_cols(q, key) * HEAD_DIM**-0.5 + allowed[...]
            peak = jnp.max(scores, axis=-1, keepdims=True)
            raised = jnp.exp(scores - peak)
            total = jnp.sum(raised, axis=-1, keepdims=True)
            sums = jnp.where(lane == h, peak + jnp.log(total), sums)
            probability = (raised / total).astype(BF)
            attended[:, HEAD_DIM * h : HEAD_DIM * (h + 1)] = dot(probability, value).astype(BF)
        lse[...] = sums
        pick_all(layer, section, parts, w_qkv, w_out, sems, (3,), False)
        for k, ref in enumerate((p0, p1, p2, p3)):
            ref[...] = dot(attended[share * k : share * (k + 1), :], w_out[...]).astype(BF)

    results = call(
        kernel,
        [((share, width), BF)] * 4
        + [((rows, width), BF), ((rows, all_cols), BF), ((rows, 128), F32), ((rows, q_cols), BF)],
        [place, *source, *tables, *gains, *weights],
        [SCALARS] + [ANY if entries == 1 else WHOLE] * entries + [WHOLE] * 5 + [ANY] * 8,
        [
            pltpu.VMEM((width, all_cols), BF),
            pltpu.VMEM((q_cols, width), BF),
            pltpu.VMEM((rows, width), BF),
            pltpu.SemaphoreType.DMA((8,)),
        ],
    )
    return results[:4], results[4:]


def attention_backward(blocks, saved, tables, weights, place, layer):
    normed, qkv, lse, attended = saved
    rows, width = normed.shape
    q_cols = weights[0].shape[1]
    kv_cols = weights[1].shape[1]
    all_cols = q_cols + 2 * kv_cols
    groups = kv_cols // HEAD_DIM
    share = rows // 4

    def kernel(at, b0, b1, b2, b3, qkv_ref, lse_ref, cos, sin, allowed, *refs):
        parts, refs = refs[:8], refs[8:]
        p0, p1, p2, p3, branch, back_qkv, w_qkv, w_out, back_o, back_qk, sems = refs
        section = at[0]
        pick_all(layer, section, parts, w_qkv, w_out, sems, (3, 0, 1, 2), True)
        for k, ref in enumerate((b0, b1, b2, b3)):
            branch[share * k : share * (k + 1), :] = ref[...]
        pick_all(layer, section, parts, w_qkv, w_out, sems, (3,), False)
        back_o[...] = contract_cols(branch[...], w_out[...]).astype(BF)
        for g in range(groups):
            at_k = q_cols + HEAD_DIM * g
            at_v = q_cols + kv_cols + HEAD_DIM * g
            key = qkv_ref[:, at_k : at_k + HEAD_DIM]
            value = qkv_ref[:, at_v : at_v + HEAD_DIM]
            back_value = jnp.zeros((rows, HEAD_DIM), F32)
            back_key = jnp.zeros((rows, HEAD_DIM), F32)
            for h in range(SHARING * g, SHARING * (g + 1)):
                q = qkv_ref[:, HEAD_DIM * h : HEAD_DIM * (h + 1)]
                back = back_o[:, HEAD_DIM * h : HEAD_DIM * (h + 1)]
                scores = contract_cols(q, key) * HEAD_DIM**-0.5 + allowed[...]
                probability = jnp.exp(scores - lse_ref[:, h : h + 1])
                back_p = contract_cols(back, value)
                back_value = back_value + contract_rows(probability.astype(BF), back)
                delta = jnp.sum(back_p * probability, axis=-1, keepdims=True)
                back_s = (probability * (back_p - delta)).astype(BF)
                back_qk[:, HEAD_DIM * h : HEAD_DIM * (h + 1)] = dot(back_s, key)
                back_key = back_key + contract_rows(back_s, q)
            back_qk[:, at_k : at_k + HEAD_DIM] = back_key
            back_qkv[:, at_v : at_v + HEAD_DIM] = back_value.astype(BF)
        scaled = back_qk[...] * HEAD_DIM**-0.5
        turned = scaled * cos[...] - half_turn(scaled * sin[...])
        back_qkv[:, : q_cols + kv_cols] = turned.astype(BF)
        pick_all(layer, section, parts, w_qkv, w_out, sems, range(3), False)
        for k, ref in enumerate((p0, p1, p2, p3)):
            ref[...] = contract_cols(back_qkv[share * k : share * (k + 1), :], w_qkv[...]).astype(BF)

    results = call(
        kernel,
        [((share, width), BF)] * 4 + [((rows, width), BF), ((rows, all_cols), BF)],
        [place, *blocks, qkv, lse, *tables, *weights],
        [SCALARS] + [WHOLE] * 9 + [ANY] * 8,
        [
            pltpu.VMEM((width, all_cols), BF),
            pltpu.VMEM((q_cols, width), BF),
            pltpu.VMEM((rows, q_cols), BF),
            pltpu.VMEM((rows, q_cols + kv_cols), F32),
            pltpu.SemaphoreType.DMA((4,)),
        ],
    )
    return results[:4], results[4], results[5]


def attention_grads(place, back_qkv, saved, branch):
    normed, attended = saved[0], saved[3]
    rows, width = normed.shape
    all_cols, q_cols = back_qkv.shape[1], attended.shape[1]
    half = width // 2

    def kernel(at, back_ref, normed_ref, attended_ref, branch_ref, mine, other):
        for out, which in ((other, 1 - at[0]), (mine, at[0])):
            for a in range(0, half, 256):
                columns = pl.ds(pl.multiple_of(half * which + a, 256), 256)
                out[a : a + 256, :all_cols] = contract_rows(normed_ref[:, columns], back_ref[...]).astype(BF)
                out[a : a + 256, all_cols:] = contract_rows(branch_ref[:, columns], attended_ref[...]).astype(BF)

    return call(
        kernel,
        [((half, all_cols + q_cols), BF)] * 2,
        [place, back_qkv, normed, attended, branch],
        [SCALARS] + [WHOLE] * 4,
    )


def attention_finish(place, halves, widths):
    half = halves[0].shape[0]
    q_cols = widths[0]
    ends = [sum(widths[:k]) for k in range(4)]

    def kernel(at, h0, h1, h2, h3, grad_q, grad_k, grad_v, grad_o):
        def store(ref, which):
            rows = pl.ds(half * which, half)
            for out, start, width in zip((grad_q, grad_k, grad_v), ends, widths):
                out[0, rows, :] = ref[:, start : start + width].astype(F32)
            grad_o[0, :, rows] = ref[:, ends[3] : ends[3] + q_cols].astype(F32).T

        @pl.when(at[0] == 0)
        def _():
            store(h0, 0)
            store(h2, 1)

        @pl.when(at[0] == 1)
        def _():
            store(h1, 1)
            store(h3, 0)

    return call(
        kernel,
        [((1, 2 * half, w), F32) for w in widths] + [((1, q_cols, 2 * half), F32)],
        [place, *halves],
        [SCALARS] + [WHOLE] * 4,
    )


def small_finish(blocks, count):
    chunks = blocks[0].shape[0] // 65
    width = chunks * 128

    def kernel(a, b, c, d, router, gain_m, gain_a):
        total = a[...].astype(F32) + b[...].astype(F32) + c[...].astype(F32) + d[...].astype(F32)
        for i in range(chunks):
            columns = slice(128 * i, 128 * (i + 1))
            router[:, columns] = total[64 * i : 64 * i + count, :]
            gain_m[:, columns] = total[64 * i + count : 64 * i + count + 1, :]
            gain_a[:, columns] = total[64 * chunks + i : 64 * chunks + i + 1, :]

    return call(
        kernel,
        [((count, width), F32), ((1, width), F32), ((1, width), F32)],
        blocks,
        [WHOLE] * 4,
    )


def prepare_experts(place, w_gate, w_up, w_down):
    _, width, deep = w_gate.shape
    half = width // 2

    def kernel(at, gate, up, down, kept_low, kept_high, given_low, given_high):
        for outs, which in (((given_low, given_high), 1 - at[0]), ((kept_low, kept_high), at[0])):
            for out, start in zip(outs, (0, half)):
                out[:, :deep] = gate[which, start : start + half, :]
                out[:, deep : 2 * deep] = up[which, start : start + half, :]
                out[:, 2 * deep :] = down[which, :, start : start + half].T

    results = call(
        kernel,
        [((half, 3 * deep), BF)] * 4,
        [place, w_gate, w_up, w_down],
        [SCALARS] + [WHOLE] * 3,
    )
    return results[:2], results[2:]


def load_experts(refs, gate_up, down, sems):
    each = len(refs) // 2
    width, deep = down.shape[0], refs[0].shape[1] // 3
    half = width // 2
    spots = [(block, low, low + half) for block in (0, 1, 3, 2) for low in (0, half)]
    up_copies, down_copies = [[], []], [[], []]
    sem = 0
    for k in range(2):
        for ref, (block, low, high) in zip(refs[each * k : each * (k + 1)], spots):
            at = 4 * k + block
            if gate_up is not None:
                target = gate_up.at[low:high, 2 * deep * at : 2 * deep * (at + 1)]
                up_copies[k].append(pltpu.make_async_copy(ref.at[:, : 2 * deep], target, sems.at[sem]))
            target = down.at[low:high, deep * at : deep * (at + 1)]
            down_copies[k].append(pltpu.make_async_copy(ref.at[:, 2 * deep :], target, sems.at[sem + 1]))
            sem += 2
    return up_copies, down_copies


def start_all(*groups):
    for group in groups:
        for copies in group:
            for copy in copies:
                copy.start()


def wait_all(copies):
    for copy in copies:
        copy.wait()


def gate_table(rows, names, router):
    count, width = rows.shape[0], router.shape[0]
    number = lax.broadcasted_iota(jnp.int32, (count, width), 1).astype(F32)
    chosen = jnp.zeros((count, width), F32)
    for j in range(names.shape[1]):
        chosen = jnp.where(number == names[:, j : j + 1], 1.0, chosen)
    logits = jnp.where(chosen > 0, contract_cols(rows, router), LOWEST)
    raised = jnp.where(chosen > 0, jnp.exp(logits - jnp.max(logits, axis=-1, keepdims=True)), 0.0)
    return raised / jnp.sum(raised, axis=-1, keepdims=True)


def expert_gates(x, names, router, at):
    table = gate_table(x, names, router)
    number = lax.broadcasted_iota(jnp.int32, table.shape, 1)
    wanted = (2 * at[2] + at[0], 2 * at[2] + 1 - at[0])
    return [jnp.sum(jnp.where(number == e, table, 0.0), axis=-1, keepdims=True) for e in wanted]


def keep_gates(gates, own):
    lane = lax.broadcasted_iota(jnp.int32, gates.shape, 1)
    gates[...] = jnp.where(lane == 0, own[0], jnp.where(lane == 1, own[1], 0.0))


def expert_down(hidden, down, out):
    width = down.shape[0]
    for a in range(0, width, 256):
        out[:, a : a + 256] = contract_cols(hidden[...], down[a : a + 256, :]).astype(BF)


def expert_backs(back, gate_up, down, waits, pre, gates, out, back_pre, hidden):
    count, width = back.shape
    deep = hidden.shape[1] // 8
    lane = lax.broadcasted_iota(jnp.int32, (count, BESIDE), 1)
    beside = jnp.zeros((count, BESIDE), F32)
    for k in range(2):
        wait_all(waits[0][k])
        gate_weight = gates[:, k : k + 1]
        inner = jnp.zeros((count, 1), F32)
        for b in range(0, 4, 2):
            first = deep * (4 * k + b)
            raw = dot(back[...], down[:, first : first + 2 * deep])
            for c in range(2):
                gate, up = pre(k, b + c)
                piece = raw[:, deep * c : deep * (c + 1)]
                sigma = 1.0 / (1.0 + jnp.exp(-gate))
                smooth = gate * sigma
                full = smooth * up
                inner = inner + jnp.sum(piece * full, axis=-1, keepdims=True)
                at = first + deep * c
                hidden[:, at : at + deep] = (gate_weight * full).astype(BF)
                flow = gate_weight * piece
                back_pre[:, 2 * at : 2 * at + deep] = (
                    flow * up * sigma * (1.0 + gate * (1.0 - sigma))
                ).astype(BF)
                back_pre[:, 2 * at + deep : 2 * at + 2 * deep] = (flow * smooth).astype(BF)
        high = inner.astype(BF).astype(F32)
        beside = jnp.where(lane == 2 * k, high, jnp.where(lane == 2 * k + 1, inner - high, beside))
    out[:, width:] = beside.astype(BF)
    for k in range(2):
        wait_all(waits[1][k])
    for a in range(0, width, 256):
        out[:, a : a + 256] = contract_cols(back_pre[...], gate_up[a : a + 256, :]).astype(BF)


def experts_forward(rows, top, router, weights, place, layer):
    count, width = rows.shape[0], rows.shape[1] - BESIDE
    deep = weights[0].shape[1] // 3
    used = len(weights)

    def kernel(at, x, router_own, router_other, *refs):
        parts, outs, scratch = refs[:used], refs[used : used + 4], refs[used + 4 :]
        (out, pre, gates, names), (gate_up, down, hidden, sems) = outs, scratch
        up_copies, down_copies = load_experts(parts, gate_up, down, sems)
        start_all(up_copies, down_copies)
        table = of_layer(layer, at[0], router_own, router_other).astype(BF)
        names[...] = x[:, width:]
        numbers = x[:, width:].astype(F32)[:, :top]
        keep_gates(gates, expert_gates(x[:, :width], numbers, table, at))
        for k in range(2):
            wait_all(up_copies[k])
            for b in range(4):
                at_b = deep * (4 * k + b)
                both = dot(x[:, :width], gate_up[:, 2 * at_b : 2 * at_b + 2 * deep])
                pre[:, 2 * at_b : 2 * at_b + 2 * deep] = both.astype(BF)
                gate, up = both[:, :deep], both[:, deep:]
                value = gates[:, k : k + 1] * gate * up / (1.0 + jnp.exp(-gate))
                hidden[:, at_b : at_b + deep] = value.astype(BF)
        for k in range(2):
            wait_all(down_copies[k])
        expert_down(hidden, down, out)

    return call(
        kernel,
        [((count, width), BF), ((count, 16 * deep), BF), ((count, 128), F32), ((count, BESIDE), BF)],
        [place, rows, *router, *weights],
        [SCALARS] + [WHOLE] * 3 + [ANY] * used,
        [
            pltpu.VMEM((width, 16 * deep), BF),
            pltpu.VMEM((width, 8 * deep), BF),
            pltpu.VMEM((count, 8 * deep), BF),
            pltpu.SemaphoreType.DMA((2 * used,)),
        ],
    )


def experts_backward(back, pre, gates, weights):
    count, width = back.shape
    deep = weights[0].shape[1] // 3
    used = len(weights)

    def kernel(back_ref, pre_ref, gates_ref, *refs):
        parts, (out, back_pre, hidden), (gate_up, down, sems) = refs[:used], refs[used : used + 3], refs[used + 3 :]
        up_copies, down_copies = load_experts(parts, gate_up, down, sems)
        start_all(down_copies, up_copies)

        def acts(k, b):
            at = 2 * deep * (4 * k + b)
            both = pre_ref[:, at : at + 2 * deep].astype(F32)
            return both[:, :deep], both[:, deep:]

        expert_backs(back_ref, gate_up, down, (down_copies, up_copies), acts, gates_ref, out, back_pre, hidden)

    return call(
        kernel,
        [((count, width + BESIDE), BF), ((count, 16 * deep), BF), ((count, 8 * deep), BF)],
        [back, pre, gates, *weights],
        [WHOLE] * 3 + [ANY] * used,
        [
            pltpu.VMEM((width, 16 * deep), BF),
            pltpu.VMEM((width, 8 * deep), BF),
            pltpu.SemaphoreType.DMA((2 * used,)),
        ],
    )


def experts_both(rows, names, top, router, back, weights, place, layer):
    count, width = rows.shape
    deep = weights[0].shape[1] // 3
    used = len(weights)

    def kernel(at, x, names_ref, router_own, router_other, back_ref, *refs):
        parts, (out, back_pre, hidden), (gate_up, down, pre, gates, sems) = (
            refs[:used],
            refs[used : used + 3],
            refs[used + 3 :],
        )
        up_copies, down_copies = load_experts(parts, gate_up, down, sems)
        start_all(up_copies, down_copies)
        table = of_layer(layer, at[0], router_own, router_other).astype(BF)
        numbers = names_ref[...].astype(F32)[:, :top]
        keep_gates(gates, expert_gates(x[...], numbers, table, at))
        for k in range(2):
            wait_all(up_copies[k])
            for b in range(4):
                at_b = 2 * deep * (4 * k + b)
                pre[:, at_b : at_b + 2 * deep] = dot(x[...], gate_up[:, at_b : at_b + 2 * deep])

        def acts(k, b):
            at_b = 2 * deep * (4 * k + b)
            return pre[:, at_b : at_b + deep], pre[:, at_b + deep : at_b + 2 * deep]

        expert_backs(back_ref, gate_up, down, (down_copies, ([], [])), acts, gates, out, back_pre, hidden)

    return call(
        kernel,
        [((count, width + BESIDE), BF), ((count, 16 * deep), BF), ((count, 8 * deep), BF)],
        [place, rows, names, *router, back, *weights],
        [SCALARS] + [WHOLE] * 5 + [ANY] * used,
        [
            pltpu.VMEM((width, 16 * deep), BF),
            pltpu.VMEM((width, 8 * deep), BF),
            pltpu.VMEM((count, 16 * deep), F32),
            pltpu.VMEM((count, 128), F32),
            pltpu.SemaphoreType.DMA((2 * used,)),
        ],
    )


def experts_out(hidden, weights):
    count = hidden.shape[0]
    width, deep = 2 * weights[0].shape[0], weights[0].shape[1] // 3
    used = len(weights)

    def kernel(hidden_ref, *refs):
        parts, out, down, sems = refs[:used], *refs[used:]
        _, down_copies = load_experts(parts, None, down, sems)
        start_all(down_copies)
        wait_all(down_copies[0] + down_copies[1])
        expert_down(hidden_ref, down, out)

    return call(
        kernel,
        [((count, width), BF)],
        [hidden, *weights],
        [WHOLE] + [ANY] * used,
        [pltpu.VMEM((width, 8 * deep), BF), pltpu.SemaphoreType.DMA((2 * used,))],
    )[0]


def experts_grads(rows, back, back_pre, hidden, which):
    count, width = back.shape
    deep = hidden.shape[1] // 8

    def kernel(x, back_ref, pre_ref, hidden_ref, out, rows_turned, back_turned):
        @pl.when(pl.program_id(0) == 0)
        def _():
            rows_turned[...] = x[:, :width].T
            back_turned[...] = back_ref[...].T

        for a in range(0, width, 512):
            out[0, a : a + 512, : 2 * deep] = dot(rows_turned[a : a + 512, :], pre_ref[...]).astype(BF)
            out[0, a : a + 512, 2 * deep :] = dot(back_turned[a : a + 512, :], hidden_ref[...]).astype(BF)

    return call(
        kernel,
        [((4, width, 3 * deep), BF)],
        [rows, back, back_pre, hidden],
        [
            WHOLE,
            WHOLE,
            pl.BlockSpec((count, 2 * deep), lambda i: (0, i + 4 * which)),
            pl.BlockSpec((count, deep), lambda i: (0, i + 4 * which)),
        ],
        [pltpu.VMEM((width, count), BF)] * 2,
        grid=(4,),
        out_specs=[pl.BlockSpec((1, width, 3 * deep), lambda i: (i, 0, 0))],
    )[0]


def experts_finish(place, sums):
    half, deep = sums[0].shape[0], sums[0].shape[1] // 3

    def kernel(at, *refs):
        sums, (grad_gate, grad_up, grad_down) = refs[:8], refs[8:]

        def store(halves, which):
            for ref, rows in zip(halves, (slice(0, half), slice(half, 2 * half))):
                grad_gate[0, which, rows, :] = ref[:, :deep].astype(F32)
                grad_up[0, which, rows, :] = ref[:, deep : 2 * deep].astype(F32)
                grad_down[0, which, :, rows] = ref[:, 2 * deep :].astype(F32).T

        @pl.when(at[0] == 0)
        def _():
            store(sums[0:2], 0)
            store(sums[4:6], 1)

        @pl.when(at[0] == 1)
        def _():
            store(sums[2:4], 1)
            store(sums[6:8], 0)

    return call(
        kernel,
        [((1, 2, 2 * half, deep), F32)] * 2 + [((1, 2, deep, 2 * half), F32)],
        [place, *sums],
        [SCALARS] + [WHOLE] * 8,
    )


def middle_rows(entry, pieces, gain, names, router, place, layer, copies):
    share, width = entry.shape
    top = names.shape[1]
    beside = 0 if layer else BESIDE
    count = router[0].shape[0]

    def kernel(at, entry_ref, a, b, c, d, gain_own, gain_other, names_ref, router_own, router_other,
               middle, out, shaped, gates):
        total = entry_ref[...].astype(F32)
        for ref in (a, b, c, d):
            total = total + ref[...].astype(F32)
        middle[...] = total
        rows = (total * inverse_level(total) * of_layer(layer, at[0], gain_own, gain_other)).astype(BF)
        shaped[...] = rows
        numbers = names_ref[...].astype(F32)
        lane = lax.broadcasted_iota(jnp.int32, (share, BESIDE), 1)
        extra = jnp.zeros((share, BESIDE), F32)
        for j in range(top):
            extra = jnp.where(lane == j, numbers[:, j : j + 1], extra)
        for k in range(copies):
            out[k, :, :width] = rows
            if beside:
                out[k, :, width:] = extra.astype(BF)
        table = of_layer(layer, at[0], router_own, router_other).astype(BF)
        gates[...] = gate_table(rows, numbers, table)

    return call(
        kernel,
        [((share, width), F32), ((copies, share, width + beside), BF), ((share, width), BF), ((share, count), F32)],
        [place, entry, *pieces, *gain, names, *router],
        [SCALARS] + [WHOLE] * 10,
    )


def leave_rows(middle, pieces):
    share, width = middle.shape

    def kernel(middle_ref, pieces_ref, out):
        total = middle_ref[...]
        for k in range(pieces_ref.shape[0]):
            total = total + pieces_ref[k].astype(F32)
        out[...] = total.astype(BF)

    return call(kernel, [((share, width), BF)], [middle, pieces], [WHOLE] * 2)[0]


def back_middle_rows(flow, pieces, middle, shaped, gates, gain, router, place, layer):
    share, width = middle.shape
    count = gates.shape[1]

    def kernel(at, flow_ref, pieces_ref, middle_ref, shaped_ref, gates_ref, gain_own, gain_other, router_own,
               router_other, back, rounded, small):
        total = jnp.zeros((share, width), F32)
        inner = jnp.zeros((share, count), F32)
        number = lax.broadcasted_iota(jnp.int32, (share, count), 1)
        for p in range(pieces_ref.shape[0]):
            total = total + pieces_ref[p, :, :width].astype(F32)
            beside = pieces_ref[p, :, width:].astype(F32)
            for k, e in enumerate((2 * p + at[0], 2 * p + 1 - at[0])):
                value = beside[:, 2 * k : 2 * k + 1] + beside[:, 2 * k + 1 : 2 * k + 2]
                inner = jnp.where(number == e, value, inner)
        own = gates_ref[...]
        slope = jnp.sum(own * inner, axis=-1, keepdims=True)
        logits = (own * (inner - slope)).astype(BF)
        table = of_layer(layer, at[0], router_own, router_other).astype(BF)
        total = total + dot(logits, table)
        gain_row = of_layer(layer, at[0], gain_own, gain_other)
        level, grad = norm_back(total, middle_ref[...], gain_row)
        total = flow_ref[...].astype(F32) + level
        back[...] = total
        rounded[...] = total.astype(BF)
        grad_router = contract_rows(logits, shaped_ref[...])
        row = lax.broadcasted_iota(jnp.int32, (64 - count, 128), 0)
        for i in range(width // 128):
            columns = slice(128 * i, 128 * (i + 1))
            small[64 * i : 64 * i + count, :] = grad_router[:, columns]
            small[64 * i + count : 64 * (i + 1), :] = jnp.where(row == 0, grad[:, columns], 0.0)

    return call(
        kernel,
        [((share, width), F32), ((share, width), BF), ((width // 2, 128), F32)],
        [place, flow, pieces, middle, shaped, gates, *gain, *router],
        [SCALARS] + [WHOLE] * 9,
    )


def back_entry_rows(back, pieces, entry, gain, place, layer, copies):
    share, width = back.shape

    def kernel(at, back_ref, a, b, c, d, entry_ref, gain_own, gain_other, out, grad_gain, *more):
        total = a[...].astype(F32) + b[...].astype(F32) + c[...].astype(F32) + d[...].astype(F32)
        level, grad = norm_back(
            total, entry_ref[...].astype(F32), of_layer(layer, at[0], gain_own, gain_other)
        )
        flow = (back_ref[...] + level).astype(BF)
        out[...] = flow
        grad_gain[...] = grad
        for ref in more:
            for k in range(copies):
                ref[k] = flow

    outs = [((share, width), BF), ((1, width), F32)]
    if copies:
        outs.append(((copies, share, width), BF))
    return call(
        kernel, outs, [place, back, *pieces, entry, *gain], [SCALARS] + [WHOLE] * 8
    )


def straight_rows(place, of_first, of_second):
    share, width = of_first[0].shape

    def kernel(at, *refs):
        blocks, (own, other) = refs[:8], refs[8:]
        for k in range(4):
            rows = pl.ds(pl.multiple_of(share * lax.rem(at[1] + k, 4), share), share)
            here = at[0] == 0
            own[rows, :] = jnp.where(here, blocks[k][...].astype(F32), blocks[4 + k][...].astype(F32)).astype(BF)
            other[rows, :] = jnp.where(here, blocks[4 + k][...].astype(F32), blocks[k][...].astype(F32)).astype(BF)

    return call(
        kernel,
        [((4 * share, width), BF)] * 2,
        [place, *of_first, *of_second],
        [SCALARS] + [WHOLE] * 8,
    )


def by_batch(place, own, other):
    rows, width = own.shape

    def kernel(at, own_ref, other_ref, out):
        out[0, at[0]] = own_ref[...]
        out[0, 1 - at[0]] = other_ref[...]

    return call(kernel, [((1, 2, rows, width), BF)], [place, own, other], [SCALARS] + [WHOLE] * 2)[0]


def per_device(
    inputs,
    cotangent,
    documents,
    routes,
    gain_attn,
    w_query,
    w_key,
    w_value,
    w_out,
    gain_moe,
    w_router,
    w_gate,
    w_up,
    w_down,
):
    section = lax.axis_index("section")
    expert = lax.axis_index("expert")
    tensor = lax.axis_index("tensor")
    sequences = lax.axis_size("expert")
    first = section == 0
    place = jnp.stack([section, tensor, expert]).astype(jnp.int32)
    rows, width = inputs.shape[1:]
    share = rows // 4
    expert_count = w_router.shape[2]
    own_weights = [w_query[0], w_key[0], w_value[0], w_out[0]]

    def own_rows(array):
        start = (section, share * tensor, 0)
        return lax.dynamic_slice(array, start, (1, share, array.shape[2]))[0]

    kept, given = prepare_experts(place, w_gate[0], w_up[0], w_down[0])
    given = [sibling(half) for half in given]
    low, high = (jnp.where(first, a, b) for a, b in zip(kept, given))
    one_low, three_high = shifted(low, "tensor", -1), shifted(high, "tensor", 1)
    weights = own_weights + [sibling(w) for w in own_weights]

    gains_a = [gain_attn, sibling(gain_attn)]
    gains_m = [gain_moe, sibling(gain_moe)]
    routers = [w_router[0].T, sibling(w_router[0].T)]
    tables = prepare_tables(place, documents, w_query.shape[2] + w_key.shape[2])
    names_own = own_rows(routes)
    top = routes.shape[2]
    flow = after(own_rows(cotangent), low, high)
    backs = [None, spread_e(flow).reshape(-1, width)]

    entry = [own_rows(inputs), None]
    attn_saved, middles, shapeds, gates_own, arrived = ([None, None] for _ in range(5))
    pieces, attn_saved[0] = attention_forward([after(inputs, low, high)], tables, weights, gains_a, place, 0)
    pieces = arrivals(pieces)
    middles[0], copies, shapeds[0], gates_own[0] = middle_rows(
        entry[0], pieces, gains_m, names_own, routers, place, 0, sequences
    )
    one_high = shifted(after(high, *pieces), "tensor", -1)
    three_low = shifted(after(low, *pieces), "tensor", 1)
    two_low = shifted(after(one_low, *pieces), "tensor", -1)
    two_high = shifted(after(three_high, *pieces), "tensor", 1)
    mine = [low, high, one_low, one_high, three_low, three_high, two_low, two_high]
    expert_weights = [[*mine, *[sibling(block) for block in mine]], None]
    copies = after(copies, backs[1])
    arrived[0] = exchange_e(copies).reshape(-1, width + BESIDE)
    low, high = (jnp.where(first, b, a) for a, b in zip(kept, given))
    low, high = after((low, high), two_low, two_high)
    one_low, three_low = shifted(low, "tensor", -1), shifted(low, "tensor", 1)
    terms, pre, gates, names = experts_forward(arrived[0], top, routers, expert_weights[0], place, 0)
    terms = after(terms, one_low, three_low)
    pieces = exchange_e(terms.reshape(-1, share, width))
    one_high, three_high = shifted(high, "tensor", -1), shifted(high, "tensor", 1)
    entry[1] = leave_rows(middles[0], after(pieces, one_high, three_high))

    blocks = gather_x(entry[1])
    outputs = [blocks, None]
    pieces, attn_saved[1] = attention_forward(blocks, tables, weights, gains_a, place, 1)
    pieces = arrivals(pieces)
    two_low = shifted(after(low, *pieces), "tensor", -2)
    two_high = shifted(after(high, *pieces), "tensor", -2)
    mine = [low, high, one_low, one_high, three_low, three_high, two_low, two_high]
    expert_weights[1] = [*mine, *[sibling(block) for block in mine]]
    middles[1], copies, shapeds[1], gates_own[1] = middle_rows(
        entry[1], pieces, gains_m, names_own, routers, place, 1, sequences
    )
    arrived[1] = exchange_e(copies).reshape(-1, width)
    terms, back_pre, hidden = experts_both(
        arrived[1], names, top, routers, backs[1], expert_weights[1], place, 1
    )

    def join(mines, others):
        half = width // 2
        return [
            [sum_of([mines[k, a : a + half], others[k, a : a + half]]) for a in (0, half)]
            for k in range(4)
        ]

    in_blocks, smalls, grads_gain = ([None, None] for _ in range(3))
    pieces = exchange_e(terms.reshape(-1, share, width + BESIDE))
    others = experts_grads(arrived[1], backs[1], back_pre, hidden, 1)
    mines = experts_grads(arrived[1], backs[1], back_pre, hidden, 0)
    outs = experts_out(hidden, expert_weights[1])
    back_middle, rounded, smalls[1] = back_middle_rows(
        flow, after(pieces, mines, others, outs), middles[1], shapeds[1], gates_own[1], gains_m, routers, place, 1
    )
    others = sibling(after(others, rounded))
    out_pieces = exchange_e(after(outs, rounded).reshape(-1, share, width))
    partial, branch, back_qkv = attention_backward(
        gather_x(rounded), attn_saved[1], tables, weights, place, 1
    )
    flow, grads_gain[1], copies = back_entry_rows(
        back_middle, arrivals(partial), entry[1], gains_a, place, 1, sequences
    )
    in_blocks[1] = gather_x(flow)
    mine_half, other_half = attention_grads(place, back_qkv, attn_saved[1], branch)
    copies = after(copies, out_pieces)
    backs[0] = exchange_e(copies).reshape(-1, width)
    last = leave_rows(middles[1], after(out_pieces, flow))
    outputs[1] = gather_x(last)
    joined = join(after(mines, last), others)
    half_one = sum_of([mine_half, sibling(other_half)])
    lows = after(tuple(block[0] for block in joined), *outputs[1], *in_blocks[1])
    highs = tuple(block[1] for block in joined)
    first_low, third_low = shifted(lows[1], "tensor", 1), shifted(lows[3], "tensor", 3)
    backs[0] = after(backs[0], half_one, first_low, third_low)
    highs = after(highs, first_low, third_low)
    first_high, third_high = shifted(highs[1], "tensor", 1), shifted(highs[3], "tensor", 3)

    piece = collect_e(after(half_one, backs[0]).reshape(sequences, -1, half_one.shape[1]))
    terms, back_pre, hidden = experts_backward(backs[0], pre, gates, expert_weights[0])
    terms = after(terms, piece, first_high, third_high)
    second_low, second_high = (
        shifted(after(block, first_high, third_high), "tensor", 2) for block in joined[2]
    )
    pieces = exchange_e(terms.reshape(-1, share, width + BESIDE))
    others = experts_grads(arrived[0], backs[0], back_pre, hidden, 1)
    mines = experts_grads(arrived[0], backs[0], back_pre, hidden, 0)
    sums = [
        None,
        [
            sum_of([lows[0], first_low, second_low, third_low]),
            sum_of([highs[0], first_high, second_high, third_high]),
        ],
    ]
    own, other = straight_rows(place, outputs[0], outputs[1])
    activations = by_batch(place, own, sibling(other))
    pieces = after(pieces, mines, others, sums[1][0], sums[1][1], activations)
    back_middle, rounded, smalls[0] = back_middle_rows(
        flow, pieces, middles[0], shapeds[0], gates_own[0], gains_m, routers, place, 0
    )
    others = sibling(after(others, rounded))
    columns = half_one.shape[1] // 2
    piece = after(piece, rounded)
    done_one = [spread_e(piece[:, a : a + columns]).reshape(-1, columns) for a in (0, columns)]
    gathered = gather_x(rounded)
    partial, branch, back_qkv = attention_backward(gathered, attn_saved[0], tables, weights, place, 0)
    mine_half, other_half = attention_grads(
        place, after(back_qkv, done_one[0]), attn_saved[0], branch
    )
    pieces = arrivals(partial)
    flow, grads_gain[0] = back_entry_rows(back_middle, pieces, entry[0], gains_a, place, 0, 0)

    def own_layer(of_first, of_second):
        own = jnp.where(first, of_first, of_second)
        return own + sibling(jnp.where(first, of_second, of_first).astype(BF)).astype(F32)

    small = own_layer(smalls[0], smalls[1]).astype(BF)
    half_zero = jnp.concatenate([sum_of([mine_half, sibling(other_half)]), small], axis=1)
    half_zero = after(half_zero, done_one[1])
    joined = join(after(mines, half_zero), others)
    first_zero = [shifted(half, "tensor", 1) for half in joined[1]]
    third_zero = [shifted(half, "tensor", 3) for half in joined[3]]
    piece = collect_e(half_zero.reshape(sequences, -1, half_zero.shape[1]))
    gain = own_layer(grads_gain[0], grads_gain[1]).reshape(width // 128, 128).astype(BF)
    gain = jnp.pad(gain, ((0, piece.shape[0] - width // 128), (0, 0)))
    piece = jnp.concatenate([piece, gain], axis=1)
    piece = after(piece, *first_zero, *third_zero)
    second_zero = [
        shifted(after(half, *first_zero, *third_zero), "tensor", 2) for half in joined[2]
    ]
    spread = spread_e(piece)
    gain = jnp.sum(spread[:, : width // 128, -128:].astype(F32), axis=0).astype(BF)
    done_zero = after(spread, *second_zero).reshape(half_one.shape[0], -1)
    small = jnp.concatenate([done_zero[:, -256:-128], gain], axis=0)
    grad_router, grad_gain_m, gain = small_finish(gather_x(small), expert_count)
    sums[0] = [
        sum_of([joined[0][n], first_zero[n], second_zero[n], third_zero[n]]) for n in range(2)
    ]
    grad_gate, grad_up, grad_down = experts_finish(
        place,
        [*sums[0], *sums[1], *[to_core(half, 0) for half in sums[0]], *[to_core(half, 1) for half in sums[1]]],
    )
    done_one = jnp.concatenate(done_one, axis=1)
    grad_query, grad_key, grad_value, grad_out = attention_finish(
        place,
        [done_zero, done_one, to_core(done_zero, 0), to_core(done_one, 1)],
        [w_query.shape[2], w_key.shape[2], w_value.shape[2]],
    )

    own, other = straight_rows(place, gather_x(flow), in_blocks[1])
    input_grads = by_batch(place, own, sibling(other))
    return (
        activations,
        input_grads,
        gain,
        grad_query,
        grad_key,
        grad_value,
        grad_out,
        grad_gain_m,
        grad_router.T[None],
        grad_gate,
        grad_up,
        grad_down,
    )


def solution(mesh):
    in_specs = (
        P(None, "expert", None),
        P(None, "expert", None),
        P(None, "expert", None),
        P(None, "expert", None),
        P("section", None),
        P("section", None, "tensor"),
        P("section", None, "tensor"),
        P("section", None, "tensor"),
        P("section", "tensor", None),
        P("section", None),
        P("section", None, None),
        P("section", "expert", None, "tensor"),
        P("section", "expert", None, "tensor"),
        P("section", "expert", "tensor", None),
    )
    out_specs = (
        P("section", None, "expert", None),
        P("section", None, "expert", None),
        P("section", None),
        P("section", None, "tensor"),
        P("section", None, "tensor"),
        P("section", None, "tensor"),
        P("section", "tensor", None),
        P("section", None),
        P("section", None, None),
        P("section", "expert", None, "tensor"),
        P("section", "expert", None, "tensor"),
        P("section", "expert", "tensor", None),
    )
    return jax.shard_map(
        per_device, mesh=mesh, in_specs=in_specs, out_specs=out_specs, check_vma=False
    )
```

```python
import math

import jax
import jax.numpy as jnp
from jax import lax
from jax.experimental import pallas as pl
from jax.experimental.pallas import tpu as pltpu
from jax.sharding import PartitionSpec as P

HEADS = 24
KV_HEADS = 8
HEAD_DIM = 64
SHARING = HEADS // KV_HEADS
EPSILON = 1e-06
LOWEST = -1e30
BF = jnp.bfloat16
F32 = jnp.float32
ANY = pl.BlockSpec(memory_space=pl.ANY)
WHOLE = pl.BlockSpec(memory_space=pltpu.VMEM)
SCALARS = pl.BlockSpec(memory_space=pltpu.SMEM)
BESIDE = 128


def shifted(array, axis, by):
    length = lax.axis_size(axis)
    return lax.ppermute(array, axis, [(i, (i + by) % length) for i in range(length)])


def sibling(array):
    return shifted(array, "section", 1)


def to_core(array, core):
    return lax.ppermute(array, "section", [(1 - core, core)])


def after(value, *others):
    return lax.optimization_barrier((value, *others))[0]


def gather_x(block):
    ahead = {k: shifted(block, "tensor", -k) for k in (1, 3, 2)}
    return [block, ahead[1], ahead[2], ahead[3]]


def start_gather(upper, lower):
    return shifted(upper, "tensor", -1), shifted(lower, "tensor", 1)


def end_gather(block, one, three):
    part = block.shape[0] // 4
    return (
        shifted(jnp.concatenate([block[3 * part :], one[: 2 * part]], axis=0), "tensor", -1),
        shifted(jnp.concatenate([block[:part], three[part:]], axis=0), "tensor", 1),
    )


def arrivals(blocks):
    return [blocks[0]] + [shifted(blocks[k], "tensor", k) for k in (1, 2, 3)]


def sum_of(blocks):
    return sum(block.astype(F32) for block in blocks).astype(BF)


def spread_e(block):
    return exchange_e(jnp.broadcast_to(block[None], (lax.axis_size("expert"), *block.shape)))


def exchange_e(blocks):
    return lax.all_to_all(blocks, "expert", 0, 0, tiled=True)


def collect_e(blocks):
    return jnp.sum(exchange_e(blocks).astype(F32), axis=0).astype(BF)


def dot(left, right):
    return jnp.dot(left, right, preferred_element_type=F32)


def contract_rows(left, right):
    return lax.dot_general(left, right, (((0,), (0,)), ((), ())), preferred_element_type=F32)


def contract_cols(left, right):
    return lax.dot_general(left, right, (((1,), (1,)), ((), ())), preferred_element_type=F32)


def call(kernel, outs, args, specs, scratch=(), grid=None, out_specs=None):
    extra = {} if grid is None else {"grid": grid}
    return pl.pallas_call(
        kernel,
        out_shape=[jax.ShapeDtypeStruct(shape, kind) for shape, kind in outs],
        in_specs=specs,
        out_specs=out_specs or [WHOLE] * len(outs),
        scratch_shapes=list(scratch),
        compiler_params=pltpu.CompilerParams(vmem_limit_bytes=60 * 2**20),
        cost_estimate=pl.CostEstimate(flops=1, bytes_accessed=1, transcendentals=0),
        **extra,
    )(*args)


def inverse_level(rows):
    return lax.rsqrt(jnp.mean(rows * rows, axis=-1, keepdims=True) + EPSILON)


def norm_back(back_scaled, rows, gain):
    inverse = inverse_level(rows)
    unit = rows * inverse
    back_unit = back_scaled * gain
    level = inverse * (back_unit - unit * jnp.mean(back_unit * unit, axis=-1, keepdims=True))
    return level, jnp.sum(back_scaled * unit, axis=0, keepdims=True)


def of_layer(layer, section, own, other):
    return jnp.where(section == layer, own[...].astype(F32), other[...].astype(F32))


def prepare_tables(place, documents, columns):
    rows = documents.shape[2]
    share = rows // 4

    def kernel(at, doc_ref, cos, sin, mask):
        turn = share * at[1]
        doc = pltpu.roll(doc_ref[at[0]].astype(F32), lax.rem(rows - turn, rows), 1)
        along = jnp.broadcast_to(doc, (rows, rows))
        down = along.T
        place_along = lax.rem(lax.broadcasted_iota(jnp.int32, (rows, rows), 1) + turn, rows)
        place_down = lax.rem(lax.broadcasted_iota(jnp.int32, (rows, rows), 0) + turn, rows)
        mask[...] = jnp.where((along == down) & (place_along <= place_down), 0.0, LOWEST)
        starts = jnp.sum(jnp.where(along < down, 1.0, 0.0), axis=1, keepdims=True)
        lane = lax.broadcasted_iota(jnp.int32, (rows, 128), 1)
        frequency = jnp.exp(lax.rem(lane, HEAD_DIM // 2).astype(F32) * (-2.0 * math.log(10000.0) / HEAD_DIM))
        offset = place_down[:, :1].astype(F32) - starts
        angle = offset * frequency
        for ref, table in ((cos, jnp.cos(angle)), (sin, jnp.sin(angle))):
            for a in range(0, columns, 128):
                ref[:, a : a + 128] = table

    return call(
        kernel,
        [((rows, columns), F32), ((rows, columns), F32), ((rows, rows), F32)],
        [place, documents],
        [SCALARS, WHOLE],
    )


def half_turn(values):
    lane = lax.broadcasted_iota(jnp.int32, values.shape, 1)
    width = values.shape[1]
    behind = pltpu.roll(values, width - HEAD_DIM // 2, 1)
    before = pltpu.roll(values, HEAD_DIM // 2, 1)
    return jnp.where(lane % HEAD_DIM < HEAD_DIM // 2, -behind, before)


def pick(layer, section, own, other, target, sem, start):
    for here, source in ((True, own), (False, other)):

        @pl.when((section == layer) == here)
        def _():
            copy = pltpu.make_async_copy(source, target, sem)
            copy.start() if start else copy.wait()


def pick_all(layer, section, weights, qkv, out, sems, which, start):
    at = 0
    for i in range(4):
        width = weights[i].shape[1]
        target = out if i == 3 else qkv.at[:, at : at + width]
        at += width
        if i in which:
            pick(layer, section, weights[i], weights[4 + i], target, sems.at[i], start)


def attention_forward(source, tables, weights, gains, place, layer):
    width, q_cols = weights[0].shape
    kv_cols = weights[1].shape[1]
    all_cols = q_cols + 2 * kv_cols
    heads = q_cols // HEAD_DIM
    rows = tables[0].shape[0]
    share = rows // 4
    entries = len(source)

    def kernel(at, *refs):
        entry, refs = refs[:entries], refs[entries:]
        (cos, sin, allowed, gain_own, gain_other), refs = refs[:5], refs[5:]
        parts, refs = refs[:8], refs[8:]
        (p0, p1, p2, p3, normed, qkv, lse, attended, w_qkv, w_out, staged, sems) = refs
        section = at[0]
        if entries == 1:
            copies = [
                pltpu.make_async_copy(
                    entry[0].at[section, pl.ds(pl.multiple_of(share * lax.rem(at[1] + k, 4), share), share)],
                    staged.at[share * k : share * (k + 1)],
                    sems.at[4 + k],
                )
                for k in range(4)
            ]
            for copy in copies:
                copy.start()
        pick_all(layer, section, parts, w_qkv, w_out, sems, range(4), True)
        gain = of_layer(layer, section, gain_own, gain_other)
        for k in range(4):
            if entries == 1:
                copies[k].wait()
                x = staged[share * k : share * (k + 1), :].astype(F32)
            else:
                x = entry[k][...].astype(F32)
            normed[share * k : share * (k + 1), :] = (x * inverse_level(x) * gain).astype(BF)
        pick_all(layer, section, parts, w_qkv, w_out, sems, range(3), False)
        raw = dot(normed[...], w_qkv[...])
        turned = raw[:, : q_cols + kv_cols]
        turned = turned * cos[...] + half_turn(turned) * sin[...]
        qkv[:, : q_cols + kv_cols] = turned.astype(BF)
        qkv[:, q_cols + kv_cols :] = raw[:, q_cols + kv_cols :].astype(BF)
        sums = jnp.zeros((rows, 128), F32)
        lane = lax.broadcasted_iota(jnp.int32, (rows, 128), 1)
        for h in range(heads):
            g = h // SHARING
            q = qkv[:, HEAD_DIM * h : HEAD_DIM * (h + 1)]
            key = qkv[:, q_cols + HEAD_DIM * g : q_cols + HEAD_DIM * (g + 1)]
            value = qkv[:, q_cols + kv_cols + HEAD_DIM * g : q_cols + kv_cols + HEAD_DIM * (g + 1)]
            scores = contract_cols(q, key) * HEAD_DIM**-0.5 + allowed[...]
            peak = jnp.max(scores, axis=-1, keepdims=True)
            raised = jnp.exp(scores - peak)
            total = jnp.sum(raised, axis=-1, keepdims=True)
            sums = jnp.where(lane == h, peak + jnp.log(total), sums)
            probability = (raised / total).astype(BF)
            attended[:, HEAD_DIM * h : HEAD_DIM * (h + 1)] = dot(probability, value).astype(BF)
        lse[...] = sums
        pick_all(layer, section, parts, w_qkv, w_out, sems, (3,), False)
        for k, ref in enumerate((p0, p1, p2, p3)):
            ref[...] = dot(attended[share * k : share * (k + 1), :], w_out[...]).astype(BF)

    results = call(
        kernel,
        [((share, width), BF)] * 4
        + [((rows, width), BF), ((rows, all_cols), BF), ((rows, 128), F32), ((rows, q_cols), BF)],
        [place, *source, *tables, *gains, *weights],
        [SCALARS] + [ANY if entries == 1 else WHOLE] * entries + [WHOLE] * 5 + [ANY] * 8,
        [
            pltpu.VMEM((width, all_cols), BF),
            pltpu.VMEM((q_cols, width), BF),
            pltpu.VMEM((rows, width), BF),
            pltpu.SemaphoreType.DMA((8,)),
        ],
    )
    return results[:4], results[4:]


def attention_backward(blocks, saved, tables, weights, place, layer):
    normed, qkv, lse, attended = saved
    rows, width = normed.shape
    q_cols = weights[0].shape[1]
    kv_cols = weights[1].shape[1]
    all_cols = q_cols + 2 * kv_cols
    groups = kv_cols // HEAD_DIM
    share = rows // 4

    def kernel(at, b0, b1, b2, b3, qkv_ref, lse_ref, cos, sin, allowed, *refs):
        parts, refs = refs[:8], refs[8:]
        p0, p1, p2, p3, branch, back_qkv, w_qkv, w_out, back_o, back_qk, sems = refs
        section = at[0]
        pick_all(layer, section, parts, w_qkv, w_out, sems, (3, 0, 1, 2), True)
        for k, ref in enumerate((b0, b1, b2, b3)):
            branch[share * k : share * (k + 1), :] = ref[...]
        pick_all(layer, section, parts, w_qkv, w_out, sems, (3,), False)
        back_o[...] = contract_cols(branch[...], w_out[...]).astype(BF)
        for g in range(groups):
            at_k = q_cols + HEAD_DIM * g
            at_v = q_cols + kv_cols + HEAD_DIM * g
            key = qkv_ref[:, at_k : at_k + HEAD_DIM]
            value = qkv_ref[:, at_v : at_v + HEAD_DIM]
            back_value = jnp.zeros((rows, HEAD_DIM), F32)
            back_key = jnp.zeros((rows, HEAD_DIM), F32)
            for h in range(SHARING * g, SHARING * (g + 1)):
                q = qkv_ref[:, HEAD_DIM * h : HEAD_DIM * (h + 1)]
                back = back_o[:, HEAD_DIM * h : HEAD_DIM * (h + 1)]
                scores = contract_cols(q, key) * HEAD_DIM**-0.5 + allowed[...]
                probability = jnp.exp(scores - lse_ref[:, h : h + 1])
                back_p = contract_cols(back, value)
                back_value = back_value + contract_rows(probability.astype(BF), back)
                delta = jnp.sum(back_p * probability, axis=-1, keepdims=True)
                back_s = (probability * (back_p - delta)).astype(BF)
                back_qk[:, HEAD_DIM * h : HEAD_DIM * (h + 1)] = dot(back_s, key)
                back_key = back_key + contract_rows(back_s, q)
            back_qk[:, at_k : at_k + HEAD_DIM] = back_key
            back_qkv[:, at_v : at_v + HEAD_DIM] = back_value.astype(BF)
        scaled = back_qk[...] * HEAD_DIM**-0.5
        turned = scaled * cos[...] - half_turn(scaled * sin[...])
        back_qkv[:, : q_cols + kv_cols] = turned.astype(BF)
        pick_all(layer, section, parts, w_qkv, w_out, sems, range(3), False)
        for k, ref in enumerate((p0, p1, p2, p3)):
            ref[...] = contract_cols(back_qkv[share * k : share * (k + 1), :], w_qkv[...]).astype(BF)

    results = call(
        kernel,
        [((share, width), BF)] * 4 + [((rows, width), BF), ((rows, all_cols), BF)],
        [place, *blocks, qkv, lse, *tables, *weights],
        [SCALARS] + [WHOLE] * 9 + [ANY] * 8,
        [
            pltpu.VMEM((width, all_cols), BF),
            pltpu.VMEM((q_cols, width), BF),
            pltpu.VMEM((rows, q_cols), BF),
            pltpu.VMEM((rows, q_cols + kv_cols), F32),
            pltpu.SemaphoreType.DMA((4,)),
        ],
    )
    return results[:4], results[4], results[5]


def attention_grads(place, back_qkv, saved, branch):
    normed, attended = saved[0], saved[3]
    rows, width = normed.shape
    all_cols, q_cols = back_qkv.shape[1], attended.shape[1]
    half = width // 2

    def kernel(at, back_ref, normed_ref, attended_ref, branch_ref, mine, other):
        for out, which in ((other, 1 - at[0]), (mine, at[0])):
            for a in range(0, half, 256):
                columns = pl.ds(pl.multiple_of(half * which + a, 256), 256)
                out[a : a + 256, :all_cols] = contract_rows(normed_ref[:, columns], back_ref[...]).astype(BF)
                out[a : a + 256, all_cols:] = contract_rows(branch_ref[:, columns], attended_ref[...]).astype(BF)

    return call(
        kernel,
        [((half, all_cols + q_cols), BF)] * 2,
        [place, back_qkv, normed, attended, branch],
        [SCALARS] + [WHOLE] * 4,
    )


def attention_finish(place, halves, widths):
    half = halves[0].shape[0]
    q_cols = widths[0]
    ends = [sum(widths[:k]) for k in range(4)]

    def kernel(at, h0, h1, h2, h3, grad_q, grad_k, grad_v, grad_o):
        def store(ref, which):
            rows = pl.ds(half * which, half)
            for out, start, width in zip((grad_q, grad_k, grad_v), ends, widths):
                out[0, rows, :] = ref[:, start : start + width].astype(F32)
            grad_o[0, :, rows] = ref[:, ends[3] : ends[3] + q_cols].astype(F32).T

        @pl.when(at[0] == 0)
        def _():
            store(h0, 0)
            store(h2, 1)

        @pl.when(at[0] == 1)
        def _():
            store(h1, 1)
            store(h3, 0)

    return call(
        kernel,
        [((1, 2 * half, w), F32) for w in widths] + [((1, q_cols, 2 * half), F32)],
        [place, *halves],
        [SCALARS] + [WHOLE] * 4,
    )


def small_finish(blocks, count):
    chunks = blocks[0].shape[0] // 65
    width = chunks * 128

    def kernel(a, b, c, d, router, gain_m, gain_a):
        total = a[...].astype(F32) + b[...].astype(F32) + c[...].astype(F32) + d[...].astype(F32)
        for i in range(chunks):
            columns = slice(128 * i, 128 * (i + 1))
            router[:, columns] = total[64 * i : 64 * i + count, :]
            gain_m[:, columns] = total[64 * i + count : 64 * i + count + 1, :]
            gain_a[:, columns] = total[64 * chunks + i : 64 * chunks + i + 1, :]

    return call(
        kernel,
        [((count, width), F32), ((1, width), F32), ((1, width), F32)],
        blocks,
        [WHOLE] * 4,
    )


def prepare_experts(place, w_gate, w_up, w_down):
    _, width, deep = w_gate.shape

    def kernel(at, gate, up, down, kept, given):
        for out, which in ((given, 1 - at[0]), (kept, at[0])):
            out[:, :deep] = gate[which]
            out[:, deep : 2 * deep] = up[which]
            out[:, 2 * deep :] = down[which].T

    return call(
        kernel,
        [((width, 3 * deep), BF)] * 2,
        [place, w_gate, w_up, w_down],
        [SCALARS] + [WHOLE] * 3,
    )


def choose_experts(place, kept, given, layer):
    width, cols = kept.shape
    part = width // 4

    def kernel(at, kept_ref, given_ref, whole, upper, lower):
        def store(ref):
            whole[...] = ref[...]
            upper[...] = ref[: 3 * part, :]
            lower[...] = ref[part:, :]

        pl.when(at[0] == layer)(lambda: store(kept_ref))
        pl.when(at[0] != layer)(lambda: store(given_ref))

    return call(
        kernel,
        [((width, cols), BF), ((3 * part, cols), BF), ((3 * part, cols), BF)],
        [place, kept, given],
        [SCALARS] + [WHOLE] * 2,
    )


def load_experts(refs, gate_up, down, sems):
    each = len(refs) // 2
    width, deep = down.shape[0], refs[0].shape[1] // 3
    part = width // 4
    spots = [
        [(0, (0, width), 0)],
        [(1, (0, 3 * part), 0)],
        [(3, (part, 3 * part), 0)],
        [(1, (3 * part, part), 0), (2, (0, 2 * part), part)],
        [(3, (0, part), 0), (2, (2 * part, 2 * part), part)],
    ]
    up_copies, down_copies = [[], []], [[], []]
    sem = 0
    for k in range(2):
        for ref, pieces in zip(refs[each * k : each * (k + 1)], spots):
            for block, (start, count), source in pieces:
                at = 4 * k + block
                rows, taken = slice(start, start + count), slice(source, source + count)
                if gate_up is not None:
                    target = gate_up.at[rows, 2 * deep * at : 2 * deep * (at + 1)]
                    up_copies[k].append(
                        pltpu.make_async_copy(ref.at[taken, : 2 * deep], target, sems.at[sem])
                    )
                target = down.at[rows, deep * at : deep * (at + 1)]
                down_copies[k].append(
                    pltpu.make_async_copy(ref.at[taken, 2 * deep :], target, sems.at[sem + 1])
                )
                sem += 2
    return up_copies, down_copies


def start_all(*groups):
    for group in groups:
        for copies in group:
            for copy in copies:
                copy.start()


def wait_all(copies):
    for copy in copies:
        copy.wait()


def gate_table(rows, names, router):
    count, width = rows.shape[0], router.shape[0]
    number = lax.broadcasted_iota(jnp.int32, (count, width), 1).astype(F32)
    chosen = jnp.zeros((count, width), F32)
    for j in range(names.shape[1]):
        chosen = jnp.where(number == names[:, j : j + 1], 1.0, chosen)
    logits = jnp.where(chosen > 0, contract_cols(rows, router), LOWEST)
    raised = jnp.where(chosen > 0, jnp.exp(logits - jnp.max(logits, axis=-1, keepdims=True)), 0.0)
    return raised / jnp.sum(raised, axis=-1, keepdims=True)


def expert_gates(x, names, router, at):
    table = gate_table(x, names, router)
    number = lax.broadcasted_iota(jnp.int32, table.shape, 1)
    wanted = (2 * at[2] + at[0], 2 * at[2] + 1 - at[0])
    return [jnp.sum(jnp.where(number == e, table, 0.0), axis=-1, keepdims=True) for e in wanted]


def keep_gates(gates, own):
    lane = lax.broadcasted_iota(jnp.int32, gates.shape, 1)
    gates[...] = jnp.where(lane == 0, own[0], jnp.where(lane == 1, own[1], 0.0))


def expert_down(hidden, down, out):
    width = down.shape[0]
    for a in range(0, width, 256):
        out[:, a : a + 256] = contract_cols(hidden[...], down[a : a + 256, :]).astype(BF)


def expert_backs(back, gate_up, down, waits, pre, gates, out, back_pre, hidden):
    count, width = back.shape
    deep = hidden.shape[1] // 8
    lane = lax.broadcasted_iota(jnp.int32, (count, BESIDE), 1)
    beside = jnp.zeros((count, BESIDE), F32)
    for k in range(2):
        wait_all(waits[0][k])
        gate_weight = gates[:, k : k + 1]
        inner = jnp.zeros((count, 1), F32)
        for b in range(0, 4, 2):
            first = deep * (4 * k + b)
            raw = dot(back[...], down[:, first : first + 2 * deep])
            for c in range(2):
                gate, up = pre(k, b + c)
                piece = raw[:, deep * c : deep * (c + 1)]
                sigma = 1.0 / (1.0 + jnp.exp(-gate))
                smooth = gate * sigma
                full = smooth * up
                inner = inner + jnp.sum(piece * full, axis=-1, keepdims=True)
                at = first + deep * c
                hidden[:, at : at + deep] = (gate_weight * full).astype(BF)
                flow = gate_weight * piece
                back_pre[:, 2 * at : 2 * at + deep] = (
                    flow * up * sigma * (1.0 + gate * (1.0 - sigma))
                ).astype(BF)
                back_pre[:, 2 * at + deep : 2 * at + 2 * deep] = (flow * smooth).astype(BF)
        high = inner.astype(BF).astype(F32)
        beside = jnp.where(lane == 2 * k, high, jnp.where(lane == 2 * k + 1, inner - high, beside))
    out[:, width:] = beside.astype(BF)
    for k in range(2):
        wait_all(waits[1][k])
    for a in range(0, width, 256):
        out[:, a : a + 256] = contract_cols(back_pre[...], gate_up[a : a + 256, :]).astype(BF)


def experts_forward(rows, top, router, weights, place, layer):
    count, width = rows.shape[0], rows.shape[1] - BESIDE
    deep = weights[0].shape[1] // 3
    used = len(weights)

    def kernel(at, x, router_own, router_other, *refs):
        parts, outs, scratch = refs[:used], refs[used : used + 4], refs[used + 4 :]
        (out, pre, gates, names), (gate_up, down, hidden, sems) = outs, scratch
        up_copies, down_copies = load_experts(parts, gate_up, down, sems)
        start_all(up_copies, down_copies)
        table = of_layer(layer, at[0], router_own, router_other).astype(BF)
        names[...] = x[:, width:]
        numbers = x[:, width:].astype(F32)[:, :top]
        keep_gates(gates, expert_gates(x[:, :width], numbers, table, at))
        for k in range(2):
            wait_all(up_copies[k])
            for b in range(4):
                at_b = deep * (4 * k + b)
                both = dot(x[:, :width], gate_up[:, 2 * at_b : 2 * at_b + 2 * deep])
                pre[:, 2 * at_b : 2 * at_b + 2 * deep] = both.astype(BF)
                gate, up = both[:, :deep], both[:, deep:]
                value = gates[:, k : k + 1] * gate * up / (1.0 + jnp.exp(-gate))
                hidden[:, at_b : at_b + deep] = value.astype(BF)
        for k in range(2):
            wait_all(down_copies[k])
        expert_down(hidden, down, out)

    return call(
        kernel,
        [((count, width), BF), ((count, 16 * deep), BF), ((count, 128), F32), ((count, BESIDE), BF)],
        [place, rows, *router, *weights],
        [SCALARS] + [WHOLE] * 3 + [ANY] * used,
        [
            pltpu.VMEM((width, 16 * deep), BF),
            pltpu.VMEM((width, 8 * deep), BF),
            pltpu.VMEM((count, 8 * deep), BF),
            pltpu.SemaphoreType.DMA((28,)),
        ],
    )


def experts_backward(back, pre, gates, weights):
    count, width = back.shape
    deep = weights[0].shape[1] // 3
    used = len(weights)

    def kernel(back_ref, pre_ref, gates_ref, *refs):
        parts, (out, back_pre, hidden), (gate_up, down, sems) = refs[:used], refs[used : used + 3], refs[used + 3 :]
        up_copies, down_copies = load_experts(parts, gate_up, down, sems)
        start_all(down_copies, up_copies)

        def acts(k, b):
            at = 2 * deep * (4 * k + b)
            both = pre_ref[:, at : at + 2 * deep].astype(F32)
            return both[:, :deep], both[:, deep:]

        expert_backs(back_ref, gate_up, down, (down_copies, up_copies), acts, gates_ref, out, back_pre, hidden)

    return call(
        kernel,
        [((count, width + BESIDE), BF), ((count, 16 * deep), BF), ((count, 8 * deep), BF)],
        [back, pre, gates, *weights],
        [WHOLE] * 3 + [ANY] * used,
        [
            pltpu.VMEM((width, 16 * deep), BF),
            pltpu.VMEM((width, 8 * deep), BF),
            pltpu.SemaphoreType.DMA((28,)),
        ],
    )


def experts_both(rows, names, top, router, back, weights, place, layer):
    count, width = rows.shape
    deep = weights[0].shape[1] // 3
    used = len(weights)

    def kernel(at, x, names_ref, router_own, router_other, back_ref, *refs):
        parts, (out, back_pre, hidden), (gate_up, down, pre, gates, sems) = (
            refs[:used],
            refs[used : used + 3],
            refs[used + 3 :],
        )
        up_copies, down_copies = load_experts(parts, gate_up, down, sems)
        start_all(up_copies, down_copies)
        table = of_layer(layer, at[0], router_own, router_other).astype(BF)
        numbers = names_ref[...].astype(F32)[:, :top]
        keep_gates(gates, expert_gates(x[...], numbers, table, at))
        for k in range(2):
            wait_all(up_copies[k])
            for b in range(4):
                at_b = 2 * deep * (4 * k + b)
                pre[:, at_b : at_b + 2 * deep] = dot(x[...], gate_up[:, at_b : at_b + 2 * deep])

        def acts(k, b):
            at_b = 2 * deep * (4 * k + b)
            return pre[:, at_b : at_b + deep], pre[:, at_b + deep : at_b + 2 * deep]

        expert_backs(back_ref, gate_up, down, (down_copies, ([], [])), acts, gates, out, back_pre, hidden)

    return call(
        kernel,
        [((count, width + BESIDE), BF), ((count, 16 * deep), BF), ((count, 8 * deep), BF)],
        [place, rows, names, *router, back, *weights],
        [SCALARS] + [WHOLE] * 5 + [ANY] * used,
        [
            pltpu.VMEM((width, 16 * deep), BF),
            pltpu.VMEM((width, 8 * deep), BF),
            pltpu.VMEM((count, 16 * deep), F32),
            pltpu.VMEM((count, 128), F32),
            pltpu.SemaphoreType.DMA((28,)),
        ],
    )


def experts_out(hidden, weights):
    count = hidden.shape[0]
    width, deep = weights[0].shape[0], weights[0].shape[1] // 3
    used = len(weights)

    def kernel(hidden_ref, *refs):
        parts, out, down, sems = refs[:used], *refs[used:]
        _, down_copies = load_experts(parts, None, down, sems)
        start_all(down_copies)
        wait_all(down_copies[0] + down_copies[1])
        expert_down(hidden_ref, down, out)

    return call(
        kernel,
        [((count, width), BF)],
        [hidden, *weights],
        [WHOLE] + [ANY] * used,
        [pltpu.VMEM((width, 8 * deep), BF), pltpu.SemaphoreType.DMA((28,))],
    )[0]


def experts_grads(rows, back, back_pre, hidden):
    count, width = back.shape
    deep = hidden.shape[1] // 8

    def kernel(x, back_ref, pre_ref, hidden_ref, mine, other, rows_turned, back_turned):
        step = pl.program_id(0)

        @pl.when(step == 0)
        def _():
            rows_turned[...] = x[:, :width].T
            back_turned[...] = back_ref[...].T

        def store(out):
            for a in range(0, width, 512):
                out[0, a : a + 512, : 2 * deep] = dot(rows_turned[a : a + 512, :], pre_ref[...]).astype(BF)
                out[0, a : a + 512, 2 * deep :] = dot(back_turned[a : a + 512, :], hidden_ref[...]).astype(BF)

        pl.when(step < 4)(lambda: store(other))
        pl.when(step >= 4)(lambda: store(mine))

    return call(
        kernel,
        [((4, width, 3 * deep), BF)] * 2,
        [rows, back, back_pre, hidden],
        [
            WHOLE,
            WHOLE,
            pl.BlockSpec((count, 2 * deep), lambda i: (0, (i + 4) % 8)),
            pl.BlockSpec((count, deep), lambda i: (0, (i + 4) % 8)),
        ],
        [pltpu.VMEM((width, count), BF)] * 2,
        grid=(8,),
        out_specs=[
            pl.BlockSpec((1, width, 3 * deep), lambda i: (jnp.maximum(i - 4, 0), 0, 0)),
            pl.BlockSpec((1, width, 3 * deep), lambda i: (jnp.minimum(i, 3), 0, 0)),
        ],
    )


def experts_finish(place, sums):
    width, deep = sums[0].shape[0], sums[0].shape[1] // 3

    def kernel(at, s0, s1, s2, s3, grad_gate, grad_up, grad_down):
        def store(ref, which):
            grad_gate[0, which] = ref[:, :deep].astype(F32)
            grad_up[0, which] = ref[:, deep : 2 * deep].astype(F32)
            grad_down[0, which] = ref[:, 2 * deep :].astype(F32).T

        @pl.when(at[0] == 0)
        def _():
            store(s0, 0)
            store(s2, 1)

        @pl.when(at[0] == 1)
        def _():
            store(s1, 1)
            store(s3, 0)

    return call(
        kernel,
        [((1, 2, width, deep), F32)] * 2 + [((1, 2, deep, width), F32)],
        [place, *sums],
        [SCALARS] + [WHOLE] * 4,
    )


def middle_rows(entry, pieces, gain, names, router, place, layer, copies):
    share, width = entry.shape
    top = names.shape[1]
    beside = 0 if layer else BESIDE
    count = router[0].shape[0]

    def kernel(at, entry_ref, a, b, c, d, gain_own, gain_other, names_ref, router_own, router_other,
               middle, out, shaped, gates):
        total = entry_ref[...].astype(F32)
        for ref in (a, b, c, d):
            total = total + ref[...].astype(F32)
        middle[...] = total
        rows = (total * inverse_level(total) * of_layer(layer, at[0], gain_own, gain_other)).astype(BF)
        shaped[...] = rows
        numbers = names_ref[...].astype(F32)
        lane = lax.broadcasted_iota(jnp.int32, (share, BESIDE), 1)
        extra = jnp.zeros((share, BESIDE), F32)
        for j in range(top):
            extra = jnp.where(lane == j, numbers[:, j : j + 1], extra)
        for k in range(copies):
            out[k, :, :width] = rows
            if beside:
                out[k, :, width:] = extra.astype(BF)
        table = of_layer(layer, at[0], router_own, router_other).astype(BF)
        gates[...] = gate_table(rows, numbers, table)

    return call(
        kernel,
        [((share, width), F32), ((copies, share, width + beside), BF), ((share, width), BF), ((share, count), F32)],
        [place, entry, *pieces, *gain, names, *router],
        [SCALARS] + [WHOLE] * 10,
    )


def leave_rows(middle, pieces, beside=()):
    share, width = middle.shape
    extra = len(beside)

    def kernel(middle_ref, pieces_ref, *refs):
        total = middle_ref[...]
        for k in range(pieces_ref.shape[0]):
            total = total + pieces_ref[k].astype(F32)
        refs[-1][:share, :] = total.astype(BF)
        for k in range(extra):
            refs[-1][share * (k + 1) : share * (k + 2), :] = refs[k][...]

    return call(
        kernel, [((share * (1 + extra), width), BF)], [middle, pieces, *beside], [WHOLE] * (2 + extra)
    )[0]


def back_middle_rows(flow, pieces, middle, shaped, gates, gain, router, place, layer):
    share, width = middle.shape
    count = gates.shape[1]

    def kernel(at, flow_ref, pieces_ref, middle_ref, shaped_ref, gates_ref, gain_own, gain_other, router_own,
               router_other, back, rounded, small):
        total = jnp.zeros((share, width), F32)
        inner = jnp.zeros((share, count), F32)
        number = lax.broadcasted_iota(jnp.int32, (share, count), 1)
        for p in range(pieces_ref.shape[0]):
            total = total + pieces_ref[p, :, :width].astype(F32)
            beside = pieces_ref[p, :, width:].astype(F32)
            for k, e in enumerate((2 * p + at[0], 2 * p + 1 - at[0])):
                value = beside[:, 2 * k : 2 * k + 1] + beside[:, 2 * k + 1 : 2 * k + 2]
                inner = jnp.where(number == e, value, inner)
        own = gates_ref[...]
        slope = jnp.sum(own * inner, axis=-1, keepdims=True)
        logits = (own * (inner - slope)).astype(BF)
        table = of_layer(layer, at[0], router_own, router_other).astype(BF)
        total = total + dot(logits, table)
        gain_row = of_layer(layer, at[0], gain_own, gain_other)
        level, grad = norm_back(total, middle_ref[...], gain_row)
        total = flow_ref[...].astype(F32) + level
        back[...] = total
        rounded[...] = total.astype(BF)
        grad_router = contract_rows(logits, shaped_ref[...])
        row = lax.broadcasted_iota(jnp.int32, (64 - count, 128), 0)
        for i in range(width // 128):
            columns = slice(128 * i, 128 * (i + 1))
            small[64 * i : 64 * i + count, :] = grad_router[:, columns]
            small[64 * i + count : 64 * (i + 1), :] = jnp.where(row == 0, grad[:, columns], 0.0)

    return call(
        kernel,
        [((share, width), F32), ((share, width), BF), ((width // 2, 128), F32)],
        [place, flow, pieces, middle, shaped, gates, *gain, *router],
        [SCALARS] + [WHOLE] * 9,
    )


def back_entry_rows(back, pieces, entry, gain, place, layer, copies, beside=()):
    share, width = back.shape
    extra = sum(rows.shape[0] for rows in beside)

    def kernel(at, back_ref, a, b, c, d, entry_ref, gain_own, gain_other, *refs):
        more, (out, grad_gain, *spread) = refs[: len(beside)], refs[len(beside) :]
        total = a[...].astype(F32) + b[...].astype(F32) + c[...].astype(F32) + d[...].astype(F32)
        level, grad = norm_back(
            total, entry_ref[...].astype(F32), of_layer(layer, at[0], gain_own, gain_other)
        )
        flow = (back_ref[...] + level).astype(BF)
        out[:share, :] = flow
        start = share
        for ref in more:
            out[start : start + ref.shape[0], :] = ref[...]
            start += ref.shape[0]
        grad_gain[...] = grad
        for ref in spread:
            for k in range(copies):
                ref[k] = flow

    outs = [((share + extra, width), BF), ((1, width), F32)]
    if copies:
        outs.append(((copies, share, width), BF))
    return call(
        kernel,
        outs,
        [place, back, *pieces, entry, *gain, *beside],
        [SCALARS] + [WHOLE] * (8 + len(beside)),
    )


def straight_rows(place, entered, final):
    share, width = entered[0].shape
    rows = 4 * share

    def kernel(at, *refs):
        blocks, finals, (own, other) = refs[:4], refs[4:8], refs[8:]
        here = at[0] == 0
        for k in range(4):
            start = share * lax.rem(at[1] + k, 4)
            values = blocks[k][...].astype(F32), finals[k][...].astype(F32)
            pairs = (
                (values[0], values[1][share : 2 * share]),
                (values[1][:share], values[1][2 * share :]),
            )
            for n, (zero, one) in enumerate(pairs):
                spot = pl.ds(pl.multiple_of(rows * n + start, share), share)
                own[spot, :] = jnp.where(here, zero, one).astype(BF)
                other[spot, :] = jnp.where(here, one, zero).astype(BF)

    return call(
        kernel,
        [((2 * rows, width), BF)] * 2,
        [place, *entered, *final],
        [SCALARS] + [WHOLE] * 8,
    )


def by_batch(place, own, other):
    rows, width = own.shape[0] // 2, own.shape[1]

    def kernel(at, own_ref, other_ref, activations, input_grads):
        for n, out in enumerate((activations, input_grads)):
            out[0, at[0]] = own_ref[rows * n : rows * (n + 1), :]
            out[0, 1 - at[0]] = other_ref[rows * n : rows * (n + 1), :]

    return call(
        kernel, [((1, 2, rows, width), BF)] * 2, [place, own, other], [SCALARS] + [WHOLE] * 2
    )


def per_device(
    inputs,
    cotangent,
    documents,
    routes,
    gain_attn,
    w_query,
    w_key,
    w_value,
    w_out,
    gain_moe,
    w_router,
    w_gate,
    w_up,
    w_down,
):
    section = lax.axis_index("section")
    expert = lax.axis_index("expert")
    tensor = lax.axis_index("tensor")
    sequences = lax.axis_size("expert")
    first = section == 0
    place = jnp.stack([section, tensor, expert]).astype(jnp.int32)
    rows, width = inputs.shape[1:]
    share = rows // 4
    expert_count = w_router.shape[2]
    own_weights = [w_query[0], w_key[0], w_value[0], w_out[0]]

    def own_rows(array):
        start = (section, share * tensor, 0)
        return lax.dynamic_slice(array, start, (1, share, array.shape[2]))[0]

    kept, given = prepare_experts(place, w_gate[0], w_up[0], w_down[0])
    given = sibling(given)
    quarter, *parts = choose_experts(place, kept, given, 0)
    sides = start_gather(*parts)
    weights = own_weights + [sibling(w) for w in own_weights]

    gains_a = [gain_attn, sibling(gain_attn)]
    gains_m = [gain_moe, sibling(gain_moe)]
    routers = [w_router[0].T, sibling(w_router[0].T)]
    tables = prepare_tables(place, documents, w_query.shape[2] + w_key.shape[2])
    names_own = own_rows(routes)
    top = routes.shape[2]
    flow = own_rows(cotangent)

    entry = [own_rows(inputs), None]
    attn_saved, middles, shapeds, gates_own, arrived = ([None, None] for _ in range(5))
    pieces, attn_saved[0] = attention_forward([after(inputs, quarter)], tables, weights, gains_a, place, 0)
    pieces = arrivals(after(pieces, *sides))
    middles[0], copies, shapeds[0], gates_own[0] = middle_rows(
        entry[0], pieces, gains_m, names_own, routers, place, 0, sequences
    )
    mine = [quarter, *sides, *end_gather(after(quarter, *pieces), *sides)]
    expert_weights = [[*mine, *[sibling(block) for block in mine]], None]
    arrived[0] = exchange_e(copies).reshape(-1, width + BESIDE)
    backs = [None, spread_e(after(flow, copies)).reshape(-1, width)]
    arrived[0] = after(arrived[0], *mine[3:])
    quarter, *parts = choose_experts(place, kept, after(given, *mine[3:]), 1)
    sides = start_gather(*parts)
    terms, pre, gates, names = experts_forward(arrived[0], top, routers, expert_weights[0], place, 0)
    terms = after(terms, backs[1])
    pieces = exchange_e(terms.reshape(-1, share, width))
    mine = [quarter, *sides, *end_gather(quarter, *sides)]
    expert_weights[1] = [*mine, *[sibling(block) for block in mine]]
    entry[1] = leave_rows(middles[0], after(pieces, *mine[3:]))

    blocks = gather_x(entry[1])
    outputs = [blocks, None]
    pieces, attn_saved[1] = attention_forward(blocks, tables, weights, gains_a, place, 1)
    pieces = arrivals(pieces)
    middles[1], copies, shapeds[1], gates_own[1] = middle_rows(
        entry[1], pieces, gains_m, names_own, routers, place, 1, sequences
    )
    arrived[1] = exchange_e(copies).reshape(-1, width)
    terms, back_pre, hidden = experts_both(
        arrived[1], names, top, routers, backs[1], expert_weights[1], place, 1
    )

    def start_ring(mines, others):
        half = width // 2
        two = sum_of([mines[2], others[2]])
        return shifted(two[:half], "tensor", 1), shifted(two[half:], "tensor", -1)

    def ring_parts(mines, others, low, high):
        half = width // 2
        return (
            jnp.concatenate(
                [sum_of([mines[1, :half], others[1, :half], low]), sum_of([mines[1, half:], others[1, half:]])]
            ),
            jnp.concatenate(
                [sum_of([mines[3, :half], others[3, :half]]), sum_of([mines[3, half:], others[3, half:], high])]
            ),
        )

    def end_ring(first, third):
        return shifted(first, "tensor", 1), shifted(third, "tensor", -1)

    in_blocks, smalls, grads_gain = ([None, None] for _ in range(3))
    pieces = exchange_e(terms.reshape(-1, share, width + BESIDE))
    mines, others = experts_grads(arrived[1], backs[1], back_pre, hidden)
    outs = experts_out(hidden, expert_weights[1])
    back_middle, rounded, smalls[1] = back_middle_rows(
        flow, after(pieces, mines, others, outs), middles[1], shapeds[1], gates_own[1], gains_m, routers, place, 1
    )
    others = sibling(after(others, rounded))
    out_pieces = exchange_e(after(outs, rounded).reshape(-1, share, width))
    partial, branch, back_qkv = attention_backward(
        gather_x(rounded), attn_saved[1], tables, weights, place, 1
    )
    flow, grads_gain[1], copies = back_entry_rows(
        back_middle, arrivals(partial), entry[1], gains_a, place, 1, sequences
    )
    copies = after(copies, out_pieces)
    backs[0] = exchange_e(copies).reshape(-1, width)
    last = leave_rows(middles[1], out_pieces, (flow,))
    mine_half, other_half = attention_grads(place, after(back_qkv, last), attn_saved[1], branch)
    mines = after(mines, last)
    twos = start_ring(mines, others)
    half_one = sum_of([mine_half, sibling(other_half)])
    backs[0] = after(backs[0], half_one, *twos)
    ends = end_ring(*ring_parts(mines, others, *twos))
    own = sum_of([mines[0], others[0]])

    piece = collect_e(after(half_one, backs[0]).reshape(sequences, -1, half_one.shape[1]))
    terms, back_pre, hidden = experts_backward(backs[0], pre, gates, expert_weights[0])
    terms = after(terms, piece)
    pieces = exchange_e(terms.reshape(-1, share, width + BESIDE))
    mines, others = experts_grads(arrived[0], backs[0], back_pre, hidden)
    sums = [None, sum_of([own, *ends])]
    piece_one = piece
    pieces = after(pieces, mines, others, sums[1])
    back_middle, rounded, smalls[0] = back_middle_rows(
        flow, pieces, middles[0], shapeds[0], gates_own[0], gains_m, routers, place, 0
    )
    others = sibling(after(others, rounded))

    def own_layer(of_first, of_second):
        own = jnp.where(first, of_first, of_second)
        return own + sibling(jnp.where(first, of_second, of_first).astype(BF)).astype(F32)

    small = own_layer(smalls[0], smalls[1]).astype(BF)
    gathered = after(gather_x(rounded), small)
    partial, branch, back_qkv = attention_backward(gathered, attn_saved[0], tables, weights, place, 0)
    mine_half, other_half = attention_grads(place, back_qkv, attn_saved[0], branch)
    pieces = arrivals(partial)
    final, grads_gain[0] = back_entry_rows(
        back_middle, pieces, entry[0], gains_a, place, 0, 0, (last,)
    )

    half_zero = jnp.concatenate([sum_of([mine_half, sibling(other_half)]), small], axis=1)
    finals = gather_x(final)
    twos = start_ring(after(mines, *finals[1:]), others)
    cut = half_zero.shape[1]
    both = exchange_e(
        jnp.concatenate(
            [
                half_zero.reshape(sequences, -1, cut),
                jnp.broadcast_to(piece_one[None], (sequences, *piece_one.shape)),
            ],
            axis=2,
        )
    )
    piece = jnp.sum(both[:, :, :cut].astype(F32), axis=0).astype(BF)
    done_one = both.reshape(half_one.shape[0], -1)[:, cut:]
    gain = own_layer(grads_gain[0], grads_gain[1]).reshape(width // 128, 128).astype(BF)
    gain = jnp.pad(gain, ((0, piece.shape[0] - width // 128), (0, 0)))
    piece = jnp.concatenate([piece, gain], axis=1)
    parts = ring_parts(mines, others, *twos)
    ends = end_ring(*parts)
    sums[0] = sum_of([mines[0], others[0], *ends])
    grad_gate, grad_up, grad_down = experts_finish(
        place, [*sums, to_core(sums[0], 0), to_core(sums[1], 1)]
    )
    mine, other = straight_rows(place, outputs[0], finals)
    activations, input_grads = by_batch(place, mine, sibling(other))
    spread = after(spread_e(piece), grad_gate, activations)
    gain = jnp.sum(spread[:, : width // 128, -128:].astype(F32), axis=0).astype(BF)
    done_zero = spread.reshape(half_one.shape[0], -1)
    small = jnp.concatenate([done_zero[:, -256:-128], gain], axis=0)
    blocks = gather_x(small)
    grad_query, grad_key, grad_value, grad_out = attention_finish(
        place,
        [done_zero, done_one, to_core(done_zero, 0), to_core(done_one, 1)],
        [w_query.shape[2], w_key.shape[2], w_value.shape[2]],
    )
    grad_router, grad_gain_m, gain = small_finish(after(blocks, grad_query), expert_count)
    return (
        activations,
        input_grads,
        gain,
        grad_query,
        grad_key,
        grad_value,
        grad_out,
        grad_gain_m,
        grad_router.T[None],
        grad_gate,
        grad_up,
        grad_down,
    )


def solution(mesh):
    in_specs = (
        P(None, "expert", None),
        P(None, "expert", None),
        P(None, "expert", None),
        P(None, "expert", None),
        P("section", None),
        P("section", None, "tensor"),
        P("section", None, "tensor"),
        P("section", None, "tensor"),
        P("section", "tensor", None),
        P("section", None),
        P("section", None, None),
        P("section", "expert", None, "tensor"),
        P("section", "expert", None, "tensor"),
        P("section", "expert", "tensor", None),
    )
    out_specs = (
        P("section", None, "expert", None),
        P("section", None, "expert", None),
        P("section", None),
        P("section", None, "tensor"),
        P("section", None, "tensor"),
        P("section", None, "tensor"),
        P("section", "tensor", None),
        P("section", None),
        P("section", None, None),
        P("section", "expert", None, "tensor"),
        P("section", "expert", None, "tensor"),
        P("section", "expert", "tensor", None),
    )
    return jax.shard_map(
        per_device, mesh=mesh, in_specs=in_specs, out_specs=out_specs, check_vma=False
    )
```

```python
import math

import jax
import jax.numpy as jnp
from jax import lax
from jax.experimental import pallas as pl
from jax.experimental.pallas import tpu as pltpu
from jax.sharding import PartitionSpec as P

HEADS = 24
KV_HEADS = 8
HEAD_DIM = 64
SHARING = HEADS // KV_HEADS
EPSILON = 1e-06
LOWEST = -1e30
BF = jnp.bfloat16
F32 = jnp.float32
ANY = pl.BlockSpec(memory_space=pl.ANY)
WHOLE = pl.BlockSpec(memory_space=pltpu.VMEM)
SCALARS = pl.BlockSpec(memory_space=pltpu.SMEM)
BESIDE = 128


def shifted(array, axis, by):
    length = lax.axis_size(axis)
    return lax.ppermute(array, axis, [(i, (i + by) % length) for i in range(length)])


def sibling(array):
    return shifted(array, "section", 1)


def to_core(array, core):
    return lax.ppermute(array, "section", [(1 - core, core)])


def after(value, *others):
    return lax.optimization_barrier((value, *others))[0]


def gather_x(block):
    ahead = {k: shifted(block, "tensor", -k) for k in (1, 3, 2)}
    return [block, ahead[1], ahead[2], ahead[3]]


def start_gather(upper, lower):
    return shifted(upper, "tensor", -1), shifted(lower, "tensor", 1)


def end_gather(block, one, three):
    width, sent = block.shape[0], one.shape[0]
    half = width // 2
    return (
        shifted(jnp.concatenate([block[sent:], one[:half]], axis=0), "tensor", -1),
        shifted(jnp.concatenate([block[: width - sent], three[sent - half :]], axis=0), "tensor", 1),
    )


def arrivals(blocks):
    return [blocks[0]] + [shifted(blocks[k], "tensor", k) for k in (1, 2, 3)]


def sum_of(blocks):
    return sum(block.astype(F32) for block in blocks).astype(BF)


def spread_e(block):
    return exchange_e(jnp.broadcast_to(block[None], (lax.axis_size("expert"), *block.shape)))


def exchange_e(blocks):
    return lax.all_to_all(blocks, "expert", 0, 0, tiled=True)


def collect_e(blocks):
    return jnp.sum(exchange_e(blocks).astype(F32), axis=0).astype(BF)


def dot(left, right):
    return jnp.dot(left, right, preferred_element_type=F32)


def contract_rows(left, right):
    return lax.dot_general(left, right, (((0,), (0,)), ((), ())), preferred_element_type=F32)


def contract_cols(left, right):
    return lax.dot_general(left, right, (((1,), (1,)), ((), ())), preferred_element_type=F32)


def call(kernel, outs, args, specs, scratch=(), grid=None, out_specs=None):
    extra = {} if grid is None else {"grid": grid}
    return pl.pallas_call(
        kernel,
        out_shape=[jax.ShapeDtypeStruct(shape, kind) for shape, kind in outs],
        in_specs=specs,
        out_specs=out_specs or [WHOLE] * len(outs),
        scratch_shapes=list(scratch),
        compiler_params=pltpu.CompilerParams(vmem_limit_bytes=60 * 2**20),
        cost_estimate=pl.CostEstimate(flops=1, bytes_accessed=1, transcendentals=0),
        **extra,
    )(*args)


def inverse_level(rows):
    return lax.rsqrt(jnp.mean(rows * rows, axis=-1, keepdims=True) + EPSILON)


def norm_back(back_scaled, rows, gain):
    inverse = inverse_level(rows)
    unit = rows * inverse
    back_unit = back_scaled * gain
    level = inverse * (back_unit - unit * jnp.mean(back_unit * unit, axis=-1, keepdims=True))
    return level, jnp.sum(back_scaled * unit, axis=0, keepdims=True)


def of_layer(layer, section, own, other):
    return jnp.where(section == layer, own[...].astype(F32), other[...].astype(F32))


def prepare_tables(place, documents, columns):
    rows = documents.shape[2]
    share = rows // 4

    def kernel(at, doc_ref, cos, sin, mask):
        turn = share * at[1]
        doc = pltpu.roll(doc_ref[at[0]].astype(F32), lax.rem(rows - turn, rows), 1)
        along = jnp.broadcast_to(doc, (rows, rows))
        down = along.T
        place_along = lax.rem(lax.broadcasted_iota(jnp.int32, (rows, rows), 1) + turn, rows)
        place_down = lax.rem(lax.broadcasted_iota(jnp.int32, (rows, rows), 0) + turn, rows)
        mask[...] = jnp.where((along == down) & (place_along <= place_down), 0.0, LOWEST)
        starts = jnp.sum(jnp.where(along < down, 1.0, 0.0), axis=1, keepdims=True)
        lane = lax.broadcasted_iota(jnp.int32, (rows, 128), 1)
        frequency = jnp.exp(lax.rem(lane, HEAD_DIM // 2).astype(F32) * (-2.0 * math.log(10000.0) / HEAD_DIM))
        offset = place_down[:, :1].astype(F32) - starts
        angle = offset * frequency
        for ref, table in ((cos, jnp.cos(angle)), (sin, jnp.sin(angle))):
            for a in range(0, columns, 128):
                ref[:, a : a + 128] = table

    return call(
        kernel,
        [((rows, columns), F32), ((rows, columns), F32), ((rows, rows), F32)],
        [place, documents],
        [SCALARS, WHOLE],
    )


def half_turn(values):
    lane = lax.broadcasted_iota(jnp.int32, values.shape, 1)
    width = values.shape[1]
    behind = pltpu.roll(values, width - HEAD_DIM // 2, 1)
    before = pltpu.roll(values, HEAD_DIM // 2, 1)
    return jnp.where(lane % HEAD_DIM < HEAD_DIM // 2, -behind, before)


def pick(layer, section, own, other, target, sem, start):
    for here, source in ((True, own), (False, other)):

        @pl.when((section == layer) == here)
        def _():
            copy = pltpu.make_async_copy(source, target, sem)
            copy.start() if start else copy.wait()


def pick_all(layer, section, weights, qkv, out, sems, which, start):
    at = 0
    for i in range(4):
        width = weights[i].shape[1]
        target = out if i == 3 else qkv.at[:, at : at + width]
        at += width
        if i in which:
            pick(layer, section, weights[i], weights[4 + i], target, sems.at[i], start)


def attention_forward(source, tables, weights, gains, place, layer):
    width, q_cols = weights[0].shape
    kv_cols = weights[1].shape[1]
    all_cols = q_cols + 2 * kv_cols
    heads = q_cols // HEAD_DIM
    rows = tables[0].shape[0]
    share = rows // 4
    entries = len(source)

    def kernel(at, *refs):
        entry, refs = refs[:entries], refs[entries:]
        (cos, sin, allowed, gain_own, gain_other), refs = refs[:5], refs[5:]
        parts, refs = refs[:8], refs[8:]
        (p0, p1, p2, p3, normed, qkv, lse, attended, w_qkv, w_out, staged, sems) = refs
        section = at[0]
        if entries == 1:
            copies = [
                pltpu.make_async_copy(
                    entry[0].at[section, pl.ds(pl.multiple_of(share * lax.rem(at[1] + k, 4), share), share)],
                    staged.at[share * k : share * (k + 1)],
                    sems.at[4 + k],
                )
                for k in range(4)
            ]
            for copy in copies:
                copy.start()
        pick_all(layer, section, parts, w_qkv, w_out, sems, range(4), True)
        gain = of_layer(layer, section, gain_own, gain_other)
        for k in range(4):
            if entries == 1:
                copies[k].wait()
                x = staged[share * k : share * (k + 1), :].astype(F32)
            else:
                x = entry[k][...].astype(F32)
            normed[share * k : share * (k + 1), :] = (x * inverse_level(x) * gain).astype(BF)
        pick_all(layer, section, parts, w_qkv, w_out, sems, range(3), False)
        raw = dot(normed[...], w_qkv[...])
        turned = raw[:, : q_cols + kv_cols]
        turned = turned * cos[...] + half_turn(turned) * sin[...]
        qkv[:, : q_cols + kv_cols] = turned.astype(BF)
        qkv[:, q_cols + kv_cols :] = raw[:, q_cols + kv_cols :].astype(BF)
        sums = jnp.zeros((rows, 128), F32)
        lane = lax.broadcasted_iota(jnp.int32, (rows, 128), 1)
        for h in range(heads):
            g = h // SHARING
            q = qkv[:, HEAD_DIM * h : HEAD_DIM * (h + 1)]
            key = qkv[:, q_cols + HEAD_DIM * g : q_cols + HEAD_DIM * (g + 1)]
            value = qkv[:, q_cols + kv_cols + HEAD_DIM * g : q_cols + kv_cols + HEAD_DIM * (g + 1)]
            scores = contract_cols(q, key) * HEAD_DIM**-0.5 + allowed[...]
            peak = jnp.max(scores, axis=-1, keepdims=True)
            raised = jnp.exp(scores - peak)
            total = jnp.sum(raised, axis=-1, keepdims=True)
            sums = jnp.where(lane == h, peak + jnp.log(total), sums)
            probability = (raised / total).astype(BF)
            attended[:, HEAD_DIM * h : HEAD_DIM * (h + 1)] = dot(probability, value).astype(BF)
        lse[...] = sums
        pick_all(layer, section, parts, w_qkv, w_out, sems, (3,), False)
        partial = dot(attended[...], w_out[...]).astype(BF)
        for k, ref in enumerate((p0, p1, p2, p3)):
            ref[...] = partial[share * k : share * (k + 1), :]

    results = call(
        kernel,
        [((share, width), BF)] * 4
        + [((rows, width), BF), ((rows, all_cols), BF), ((rows, 128), F32), ((rows, q_cols), BF)],
        [place, *source, *tables, *gains, *weights],
        [SCALARS] + [ANY if entries == 1 else WHOLE] * entries + [WHOLE] * 5 + [ANY] * 8,
        [
            pltpu.VMEM((width, all_cols), BF),
            pltpu.VMEM((q_cols, width), BF),
            pltpu.VMEM((rows, width), BF),
            pltpu.SemaphoreType.DMA((8,)),
        ],
    )
    return results[:4], results[4:]


def attention_backward(blocks, saved, tables, weights, place, layer):
    normed, qkv, lse, attended = saved
    rows, width = normed.shape
    q_cols = weights[0].shape[1]
    kv_cols = weights[1].shape[1]
    all_cols = q_cols + 2 * kv_cols
    groups = kv_cols // HEAD_DIM
    share = rows // 4

    def kernel(at, b0, b1, b2, b3, qkv_ref, lse_ref, cos, sin, allowed, *refs):
        parts, refs = refs[:8], refs[8:]
        p0, p1, p2, p3, branch, back_qkv, w_qkv, w_out, back_o, back_qk, sems = refs
        section = at[0]
        pick_all(layer, section, parts, w_qkv, w_out, sems, (3, 0, 1, 2), True)
        for k, ref in enumerate((b0, b1, b2, b3)):
            branch[share * k : share * (k + 1), :] = ref[...]
        pick_all(layer, section, parts, w_qkv, w_out, sems, (3,), False)
        back_o[...] = contract_cols(branch[...], w_out[...]).astype(BF)
        for g in range(groups):
            at_k = q_cols + HEAD_DIM * g
            at_v = q_cols + kv_cols + HEAD_DIM * g
            key = qkv_ref[:, at_k : at_k + HEAD_DIM]
            value = qkv_ref[:, at_v : at_v + HEAD_DIM]
            back_value = jnp.zeros((rows, HEAD_DIM), F32)
            back_key = jnp.zeros((rows, HEAD_DIM), F32)
            for h in range(SHARING * g, SHARING * (g + 1)):
                q = qkv_ref[:, HEAD_DIM * h : HEAD_DIM * (h + 1)]
                back = back_o[:, HEAD_DIM * h : HEAD_DIM * (h + 1)]
                scores = contract_cols(q, key) * HEAD_DIM**-0.5 + allowed[...]
                probability = jnp.exp(scores - lse_ref[:, h : h + 1])
                back_p = contract_cols(back, value)
                back_value = back_value + contract_rows(probability.astype(BF), back)
                delta = jnp.sum(back_p * probability, axis=-1, keepdims=True)
                back_s = (probability * (back_p - delta)).astype(BF)
                back_qk[:, HEAD_DIM * h : HEAD_DIM * (h + 1)] = dot(back_s, key)
                back_key = back_key + contract_rows(back_s, q)
            back_qk[:, at_k : at_k + HEAD_DIM] = back_key
            back_qkv[:, at_v : at_v + HEAD_DIM] = back_value.astype(BF)
        scaled = back_qk[...] * HEAD_DIM**-0.5
        turned = scaled * cos[...] - half_turn(scaled * sin[...])
        back_qkv[:, : q_cols + kv_cols] = turned.astype(BF)
        pick_all(layer, section, parts, w_qkv, w_out, sems, range(3), False)
        partial = contract_cols(back_qkv[...], w_qkv[...]).astype(BF)
        for k, ref in enumerate((p0, p1, p2, p3)):
            ref[...] = partial[share * k : share * (k + 1), :]

    results = call(
        kernel,
        [((share, width), BF)] * 4 + [((rows, width), BF), ((rows, all_cols), BF)],
        [place, *blocks, qkv, lse, *tables, *weights],
        [SCALARS] + [WHOLE] * 9 + [ANY] * 8,
        [
            pltpu.VMEM((width, all_cols), BF),
            pltpu.VMEM((q_cols, width), BF),
            pltpu.VMEM((rows, q_cols), BF),
            pltpu.VMEM((rows, q_cols + kv_cols), F32),
            pltpu.SemaphoreType.DMA((4,)),
        ],
    )
    return results[:4], results[4], results[5]


def attention_grads(place, back_qkv, saved, branch):
    normed, attended = saved[0], saved[3]
    rows, width = normed.shape
    all_cols, q_cols = back_qkv.shape[1], attended.shape[1]
    half = width // 2

    def kernel(at, back_ref, normed_ref, attended_ref, branch_ref, mine, other):
        for out, which in ((other, 1 - at[0]), (mine, at[0])):
            for a in range(0, half, 256):
                columns = pl.ds(pl.multiple_of(half * which + a, 256), 256)
                out[a : a + 256, :all_cols] = contract_rows(normed_ref[:, columns], back_ref[...]).astype(BF)
                out[a : a + 256, all_cols:] = contract_rows(branch_ref[:, columns], attended_ref[...]).astype(BF)

    return call(
        kernel,
        [((half, all_cols + q_cols), BF)] * 2,
        [place, back_qkv, normed, attended, branch],
        [SCALARS] + [WHOLE] * 4,
    )


def attention_finish(place, of_first, of_second, widths, theirs, begun=()):
    half, q_cols = of_first.shape[0], widths[0]
    ends = [sum(widths[:k]) for k in range(4)]
    known = len(begun)

    def kernel(at, h0, h1, *refs):
        *grads, rows, turned, sems = refs[known:]
        which = 1 - at[0] if theirs else at[0]

        def store(ref):
            rows[...] = ref[:, : ends[3]].astype(F32)
            turned[...] = ref[:, ends[3] : ends[3] + q_cols].astype(F32).T

        pl.when(at[0] == 0)(lambda: store(h0))
        pl.when(at[0] == 1)(lambda: store(h1))
        spot = pl.ds(pl.multiple_of(half * which, half), half)
        copies = [
            pltpu.make_async_copy(rows.at[:, start : start + width], grad.at[0, spot, :], sems.at[k])
            for k, (grad, start, width) in enumerate(zip(grads, ends, widths))
        ]
        copies.append(pltpu.make_async_copy(turned, grads[3].at[0, :, spot], sems.at[3]))
        for copy in copies:
            copy.start()
        for copy in copies:
            copy.wait()

    shapes = [(1, 2 * half, w) for w in widths] + [(1, q_cols, 2 * half)]
    return pl.pallas_call(
        kernel,
        out_shape=[jax.ShapeDtypeStruct(shape, F32) for shape in shapes],
        in_specs=[SCALARS, WHOLE, WHOLE] + [ANY] * known,
        out_specs=[ANY] * 4,
        scratch_shapes=[
            pltpu.VMEM((half, ends[3]), F32),
            pltpu.VMEM((q_cols, half), F32),
            pltpu.SemaphoreType.DMA((4,)),
        ],
        input_output_aliases={3 + k: k for k in range(known)},
        compiler_params=pltpu.CompilerParams(vmem_limit_bytes=60 * 2**20),
        cost_estimate=pl.CostEstimate(flops=1, bytes_accessed=1, transcendentals=0),
    )(place, of_first, of_second, *begun)


def small_finish(blocks, count):
    chunks = blocks[0].shape[0] // 65
    width = chunks * 128

    def kernel(a, b, c, d, router, gain_m, gain_a):
        total = a[...].astype(F32) + b[...].astype(F32) + c[...].astype(F32) + d[...].astype(F32)
        for i in range(chunks):
            columns = slice(128 * i, 128 * (i + 1))
            router[:, columns] = total[64 * i : 64 * i + count, :]
            gain_m[:, columns] = total[64 * i + count : 64 * i + count + 1, :]
            gain_a[:, columns] = total[64 * chunks + i : 64 * chunks + i + 1, :]

    return call(
        kernel,
        [((count, width), F32), ((1, width), F32), ((1, width), F32)],
        blocks,
        [WHOLE] * 4,
    )


def prepare_experts(place, w_gate, w_up, w_down):
    _, width, deep = w_gate.shape

    def kernel(at, gate, up, down, kept, given):
        for out, which in ((given, 1 - at[0]), (kept, at[0])):
            out[:, :deep] = gate[which]
            out[:, deep : 2 * deep] = up[which]
            out[:, 2 * deep :] = down[which].T

    return call(
        kernel,
        [((width, 3 * deep), BF)] * 2,
        [place, w_gate, w_up, w_down],
        [SCALARS] + [WHOLE] * 3,
    )


def choose_experts(place, kept, given, layer, sent):
    width, cols = kept.shape

    def kernel(at, kept_ref, given_ref, whole, upper, lower):
        def store(ref):
            whole[...] = ref[...]
            upper[...] = ref[:sent, :]
            lower[...] = ref[width - sent :, :]

        pl.when(at[0] == layer)(lambda: store(kept_ref))
        pl.when(at[0] != layer)(lambda: store(given_ref))

    return call(
        kernel,
        [((width, cols), BF), ((sent, cols), BF), ((sent, cols), BF)],
        [place, kept, given],
        [SCALARS] + [WHOLE] * 2,
    )


def load_experts(refs, gate_up, down, sems):
    each = len(refs) // 2
    width, deep = down.shape[0], refs[0].shape[1] // 3
    half, sent = width // 2, refs[1].shape[0]
    rest = width - sent
    spots = [
        [(0, (0, width), 0)],
        [(1, (0, sent), 0)],
        [(3, (rest, sent), 0)],
        [(1, (sent, rest), 0), (2, (0, half), rest)],
        [(3, (0, rest), 0), (2, (half, half), rest)],
    ]
    up_copies, down_copies = [[], []], [[], []]
    sem = 0
    for k in range(2):
        for ref, pieces in zip(refs[each * k : each * (k + 1)], spots):
            for block, (start, count), source in pieces:
                at = 4 * k + block
                rows, taken = slice(start, start + count), slice(source, source + count)
                if gate_up is not None:
                    target = gate_up.at[rows, 2 * deep * at : 2 * deep * (at + 1)]
                    up_copies[k].append(
                        pltpu.make_async_copy(ref.at[taken, : 2 * deep], target, sems.at[sem])
                    )
                target = down.at[rows, deep * at : deep * (at + 1)]
                down_copies[k].append(
                    pltpu.make_async_copy(ref.at[taken, 2 * deep :], target, sems.at[sem + 1])
                )
                sem += 2
    return up_copies, down_copies


def start_all(*groups):
    for group in groups:
        for copies in group:
            for copy in copies:
                copy.start()


def wait_all(copies):
    for copy in copies:
        copy.wait()


def gate_table(rows, names, router):
    count, width = rows.shape[0], router.shape[0]
    number = lax.broadcasted_iota(jnp.int32, (count, width), 1).astype(F32)
    chosen = jnp.zeros((count, width), F32)
    for j in range(names.shape[1]):
        chosen = jnp.where(number == names[:, j : j + 1], 1.0, chosen)
    logits = jnp.where(chosen > 0, contract_cols(rows, router), LOWEST)
    raised = jnp.where(chosen > 0, jnp.exp(logits - jnp.max(logits, axis=-1, keepdims=True)), 0.0)
    return raised / jnp.sum(raised, axis=-1, keepdims=True)


def expert_gates(x, names, router, at):
    table = gate_table(x, names, router)
    number = lax.broadcasted_iota(jnp.int32, table.shape, 1)
    wanted = (2 * at[2] + at[0], 2 * at[2] + 1 - at[0])
    return [jnp.sum(jnp.where(number == e, table, 0.0), axis=-1, keepdims=True) for e in wanted]


def keep_gates(gates, own):
    lane = lax.broadcasted_iota(jnp.int32, gates.shape, 1)
    gates[...] = jnp.where(lane == 0, own[0], jnp.where(lane == 1, own[1], 0.0))


def expert_down(hidden, down, out):
    width = down.shape[0]
    for a in range(0, width, 256):
        out[:, a : a + 256] = contract_cols(hidden[...], down[a : a + 256, :]).astype(BF)


def leave(pairs, sems):
    copies = [pltpu.make_async_copy(a, b, sems.at[k]) for k, (a, b) in enumerate(pairs)]
    for copy in copies:
        copy.start()
    return copies


def expert_backs(back, gate_up, down, waits, pre, gates, out, back_pre, hidden, kept, sems):
    count, width = back.shape
    deep = hidden.shape[1] // 8
    lane = lax.broadcasted_iota(jnp.int32, (count, BESIDE), 1)
    beside = jnp.zeros((count, BESIDE), F32)
    for k in range(2):
        wait_all(waits[0][k])
        gate_weight = gates[:, k : k + 1]
        inner = jnp.zeros((count, 1), F32)
        for b in range(0, 4, 2):
            first = deep * (4 * k + b)
            raw = dot(back[...], down[:, first : first + 2 * deep])
            for c in range(2):
                gate, up = pre(k, b + c)
                piece = raw[:, deep * c : deep * (c + 1)]
                sigma = 1.0 / (1.0 + jnp.exp(-gate))
                smooth = gate * sigma
                full = smooth * up
                inner = inner + jnp.sum(piece * full, axis=-1, keepdims=True)
                at = first + deep * c
                hidden[:, at : at + deep] = (gate_weight * full).astype(BF)
                flow = gate_weight * piece
                back_pre[:, 2 * at : 2 * at + deep] = (
                    flow * up * sigma * (1.0 + gate * (1.0 - sigma))
                ).astype(BF)
                back_pre[:, 2 * at + deep : 2 * at + 2 * deep] = (flow * smooth).astype(BF)
        high = inner.astype(BF).astype(F32)
        beside = jnp.where(lane == 2 * k, high, jnp.where(lane == 2 * k + 1, inner - high, beside))
    out[:, width:] = beside.astype(BF)
    copies = leave([(back_pre, kept[0]), (hidden, kept[1])], sems)
    for k in range(2):
        wait_all(waits[1][k])
    for a in range(0, width, 256):
        out[:, a : a + 256] = contract_cols(back_pre[...], gate_up[a : a + 256, :]).astype(BF)
    wait_all(copies)


def experts_forward(rows, top, router, weights, place, layer):
    count, width = rows.shape[0], rows.shape[1] - BESIDE
    deep = weights[0].shape[1] // 3
    used = len(weights)

    def kernel(at, x, router_own, router_other, *refs):
        parts, outs, scratch = refs[:used], refs[used : used + 4], refs[used + 4 :]
        (out, kept, gates, names), (gate_up, down, hidden, pre, sems, leave_sems) = outs, scratch
        up_copies, down_copies = load_experts(parts, gate_up, down, sems)
        start_all(up_copies, down_copies)
        table = of_layer(layer, at[0], router_own, router_other).astype(BF)
        names[...] = x[:, width:]
        numbers = x[:, width:].astype(F32)[:, :top]
        keep_gates(gates, expert_gates(x[:, :width], numbers, table, at))
        for k in range(2):
            wait_all(up_copies[k])
            for b in range(4):
                at_b = deep * (4 * k + b)
                both = dot(x[:, :width], gate_up[:, 2 * at_b : 2 * at_b + 2 * deep])
                pre[:, 2 * at_b : 2 * at_b + 2 * deep] = both.astype(BF)
                gate, up = both[:, :deep], both[:, deep:]
                value = gates[:, k : k + 1] * gate * up / (1.0 + jnp.exp(-gate))
                hidden[:, at_b : at_b + deep] = value.astype(BF)
        leaving = leave([(pre, kept)], leave_sems)
        for k in range(2):
            wait_all(down_copies[k])
        expert_down(hidden, down, out)
        wait_all(leaving)

    return call(
        kernel,
        [((count, width), BF), ((count, 16 * deep), BF), ((count, 128), F32), ((count, BESIDE), BF)],
        [place, rows, *router, *weights],
        [SCALARS] + [WHOLE] * 3 + [ANY] * used,
        [
            pltpu.VMEM((width, 16 * deep), BF),
            pltpu.VMEM((width, 8 * deep), BF),
            pltpu.VMEM((count, 8 * deep), BF),
            pltpu.VMEM((count, 16 * deep), BF),
            pltpu.SemaphoreType.DMA((28,)),
            pltpu.SemaphoreType.DMA((1,)),
        ],
        out_specs=[WHOLE, ANY, WHOLE, WHOLE],
    )


def experts_backward(back, pre, gates, weights):
    count, width = back.shape
    deep = weights[0].shape[1] // 3
    used = len(weights)

    def kernel(back_ref, pre_ref, gates_ref, *refs):
        parts, (out, *kept), scratch = refs[:used], refs[used : used + 3], refs[used + 3 :]
        gate_up, down, back_pre, hidden, sems, leave_sems = scratch
        up_copies, down_copies = load_experts(parts, gate_up, down, sems)
        start_all(down_copies, up_copies)

        def acts(k, b):
            at = 2 * deep * (4 * k + b)
            both = pre_ref[:, at : at + 2 * deep].astype(F32)
            return both[:, :deep], both[:, deep:]

        expert_backs(
            back_ref, gate_up, down, (down_copies, up_copies), acts, gates_ref, out, back_pre, hidden, kept, leave_sems
        )

    return call(
        kernel,
        [((count, width + BESIDE), BF), ((count, 16 * deep), BF), ((count, 8 * deep), BF)],
        [back, pre, gates, *weights],
        [WHOLE] * 3 + [ANY] * used,
        [
            pltpu.VMEM((width, 16 * deep), BF),
            pltpu.VMEM((width, 8 * deep), BF),
            pltpu.VMEM((count, 16 * deep), BF),
            pltpu.VMEM((count, 8 * deep), BF),
            pltpu.SemaphoreType.DMA((28,)),
            pltpu.SemaphoreType.DMA((2,)),
        ],
        out_specs=[WHOLE, ANY, ANY],
    )


def experts_both(rows, names, top, router, back, weights, place, layer):
    count, width = rows.shape
    deep = weights[0].shape[1] // 3
    used = len(weights)

    def kernel(at, x, names_ref, router_own, router_other, back_ref, *refs):
        parts, (out, *kept), scratch = refs[:used], refs[used : used + 3], refs[used + 3 :]
        gate_up, down, pre, gates, back_pre, hidden, sems, leave_sems = scratch
        up_copies, down_copies = load_experts(parts, gate_up, down, sems)
        start_all(up_copies, down_copies)
        table = of_layer(layer, at[0], router_own, router_other).astype(BF)
        numbers = names_ref[...].astype(F32)[:, :top]
        keep_gates(gates, expert_gates(x[...], numbers, table, at))
        for k in range(2):
            wait_all(up_copies[k])
            for b in range(4):
                at_b = 2 * deep * (4 * k + b)
                pre[:, at_b : at_b + 2 * deep] = dot(x[...], gate_up[:, at_b : at_b + 2 * deep])

        def acts(k, b):
            at_b = 2 * deep * (4 * k + b)
            return pre[:, at_b : at_b + deep], pre[:, at_b + deep : at_b + 2 * deep]

        expert_backs(
            back_ref, gate_up, down, (down_copies, ([], [])), acts, gates, out, back_pre, hidden, kept, leave_sems
        )

    return call(
        kernel,
        [((count, width + BESIDE), BF), ((count, 16 * deep), BF), ((count, 8 * deep), BF)],
        [place, rows, names, *router, back, *weights],
        [SCALARS] + [WHOLE] * 5 + [ANY] * used,
        [
            pltpu.VMEM((width, 16 * deep), BF),
            pltpu.VMEM((width, 8 * deep), BF),
            pltpu.VMEM((count, 16 * deep), F32),
            pltpu.VMEM((count, 128), F32),
            pltpu.VMEM((count, 16 * deep), BF),
            pltpu.VMEM((count, 8 * deep), BF),
            pltpu.SemaphoreType.DMA((28,)),
            pltpu.SemaphoreType.DMA((2,)),
        ],
        out_specs=[WHOLE, ANY, ANY],
    )


def experts_out(hidden, weights):
    count = hidden.shape[0]
    width, deep = weights[0].shape[0], weights[0].shape[1] // 3
    used = len(weights)

    def kernel(hidden_ref, *refs):
        parts, out, down, sems = refs[:used], *refs[used:]
        _, down_copies = load_experts(parts, None, down, sems)
        start_all(down_copies)
        wait_all(down_copies[0] + down_copies[1])
        expert_down(hidden_ref, down, out)

    return call(
        kernel,
        [((count, width), BF)],
        [hidden, *weights],
        [WHOLE] + [ANY] * used,
        [pltpu.VMEM((width, 8 * deep), BF), pltpu.SemaphoreType.DMA((28,))],
    )[0]


def experts_grads(rows, back, back_pre, hidden):
    count, width = back.shape
    deep = hidden.shape[1] // 8

    def kernel(x, back_ref, pre_ref, hidden_ref, mine, other, rows_turned, back_turned):
        step = pl.program_id(0)

        @pl.when(step == 0)
        def _():
            rows_turned[...] = x[:, :width].T
            back_turned[...] = back_ref[...].T

        def store(out):
            for a in range(0, width, 512):
                out[0, a : a + 512, : 2 * deep] = dot(rows_turned[a : a + 512, :], pre_ref[...]).astype(BF)
                out[0, a : a + 512, 2 * deep :] = dot(back_turned[a : a + 512, :], hidden_ref[...]).astype(BF)

        pl.when(step < 4)(lambda: store(other))
        pl.when(step >= 4)(lambda: store(mine))

    return call(
        kernel,
        [((4, width, 3 * deep), BF)] * 2,
        [rows, back, back_pre, hidden],
        [
            WHOLE,
            WHOLE,
            pl.BlockSpec((count, 2 * deep), lambda i: (0, (i + 4) % 8)),
            pl.BlockSpec((count, deep), lambda i: (0, (i + 4) % 8)),
        ],
        [pltpu.VMEM((width, count), BF)] * 2,
        grid=(8,),
        out_specs=[
            pl.BlockSpec((1, width, 3 * deep), lambda i: (jnp.maximum(i - 4, 0), 0, 0)),
            pl.BlockSpec((1, width, 3 * deep), lambda i: (jnp.minimum(i, 3), 0, 0)),
        ],
    )


def experts_finish(place, sums):
    width, deep = sums[0].shape[0], sums[0].shape[1] // 3

    def kernel(at, s0, s1, s2, s3, grad_gate, grad_up, grad_down):
        def store(ref, which):
            grad_gate[0, which] = ref[:, :deep].astype(F32)
            grad_up[0, which] = ref[:, deep : 2 * deep].astype(F32)
            grad_down[0, which] = ref[:, 2 * deep :].astype(F32).T

        @pl.when(at[0] == 0)
        def _():
            store(s0, 0)
            store(s2, 1)

        @pl.when(at[0] == 1)
        def _():
            store(s1, 1)
            store(s3, 0)

    return call(
        kernel,
        [((1, 2, width, deep), F32)] * 2 + [((1, 2, deep, width), F32)],
        [place, *sums],
        [SCALARS] + [WHOLE] * 4,
    )


def middle_rows(entry, pieces, gain, names, router, place, layer, copies):
    share, width = entry.shape
    top = names.shape[1]
    beside = 0 if layer else BESIDE
    count = router[0].shape[0]

    def kernel(at, entry_ref, a, b, c, d, gain_own, gain_other, names_ref, router_own, router_other,
               middle, out, shaped, gates):
        total = entry_ref[...].astype(F32)
        for ref in (a, b, c, d):
            total = total + ref[...].astype(F32)
        middle[...] = total
        rows = (total * inverse_level(total) * of_layer(layer, at[0], gain_own, gain_other)).astype(BF)
        shaped[...] = rows
        numbers = names_ref[...].astype(F32)
        lane = lax.broadcasted_iota(jnp.int32, (share, BESIDE), 1)
        extra = jnp.zeros((share, BESIDE), F32)
        for j in range(top):
            extra = jnp.where(lane == j, numbers[:, j : j + 1], extra)
        for k in range(copies):
            out[k, :, :width] = rows
            if beside:
                out[k, :, width:] = extra.astype(BF)
        table = of_layer(layer, at[0], router_own, router_other).astype(BF)
        gates[...] = gate_table(rows, numbers, table)

    return call(
        kernel,
        [((share, width), F32), ((copies, share, width + beside), BF), ((share, width), BF), ((share, count), F32)],
        [place, entry, *pieces, *gain, names, *router],
        [SCALARS] + [WHOLE] * 10,
    )


def leave_rows(middle, pieces, beside=()):
    share, width = middle.shape
    extra = len(beside)

    def kernel(middle_ref, pieces_ref, *refs):
        total = middle_ref[...]
        for k in range(pieces_ref.shape[0]):
            total = total + pieces_ref[k].astype(F32)
        refs[-1][:share, :] = total.astype(BF)
        for k in range(extra):
            refs[-1][share * (k + 1) : share * (k + 2), :] = refs[k][...]

    return call(
        kernel, [((share * (1 + extra), width), BF)], [middle, pieces, *beside], [WHOLE] * (2 + extra)
    )[0]


def back_middle_rows(flow, pieces, middle, shaped, gates, gain, router, place, layer):
    share, width = middle.shape
    count = gates.shape[1]

    def kernel(at, flow_ref, pieces_ref, middle_ref, shaped_ref, gates_ref, gain_own, gain_other, router_own,
               router_other, back, rounded, small):
        total = jnp.zeros((share, width), F32)
        inner = jnp.zeros((share, count), F32)
        number = lax.broadcasted_iota(jnp.int32, (share, count), 1)
        for p in range(pieces_ref.shape[0]):
            total = total + pieces_ref[p, :, :width].astype(F32)
            beside = pieces_ref[p, :, width:].astype(F32)
            for k, e in enumerate((2 * p + at[0], 2 * p + 1 - at[0])):
                value = beside[:, 2 * k : 2 * k + 1] + beside[:, 2 * k + 1 : 2 * k + 2]
                inner = jnp.where(number == e, value, inner)
        own = gates_ref[...]
        slope = jnp.sum(own * inner, axis=-1, keepdims=True)
        logits = (own * (inner - slope)).astype(BF)
        table = of_layer(layer, at[0], router_own, router_other).astype(BF)
        total = total + dot(logits, table)
        gain_row = of_layer(layer, at[0], gain_own, gain_other)
        level, grad = norm_back(total, middle_ref[...], gain_row)
        total = flow_ref[...].astype(F32) + level
        back[...] = total
        rounded[...] = total.astype(BF)
        grad_router = contract_rows(logits, shaped_ref[...])
        row = lax.broadcasted_iota(jnp.int32, (64 - count, 128), 0)
        for i in range(width // 128):
            columns = slice(128 * i, 128 * (i + 1))
            small[64 * i : 64 * i + count, :] = grad_router[:, columns]
            small[64 * i + count : 64 * (i + 1), :] = jnp.where(row == 0, grad[:, columns], 0.0)

    return call(
        kernel,
        [((share, width), F32), ((share, width), BF), ((width // 2, 128), F32)],
        [place, flow, pieces, middle, shaped, gates, *gain, *router],
        [SCALARS] + [WHOLE] * 9,
    )


def back_entry_rows(back, pieces, entry, gain, place, layer, copies, beside=()):
    share, width = back.shape
    extra = sum(rows.shape[0] for rows in beside)

    def kernel(at, back_ref, a, b, c, d, entry_ref, gain_own, gain_other, *refs):
        more, (out, grad_gain, *spread) = refs[: len(beside)], refs[len(beside) :]
        total = a[...].astype(F32) + b[...].astype(F32) + c[...].astype(F32) + d[...].astype(F32)
        level, grad = norm_back(
            total, entry_ref[...].astype(F32), of_layer(layer, at[0], gain_own, gain_other)
        )
        flow = (back_ref[...] + level).astype(BF)
        out[:share, :] = flow
        start = share
        for ref in more:
            out[start : start + ref.shape[0], :] = ref[...]
            start += ref.shape[0]
        grad_gain[...] = grad
        for ref in spread:
            for k in range(copies):
                ref[k] = flow

    outs = [((share + extra, width), BF), ((1, width), F32)]
    if copies:
        outs.append(((copies, share, width), BF))
    return call(
        kernel,
        outs,
        [place, back, *pieces, entry, *gain, *beside],
        [SCALARS] + [WHOLE] * (8 + len(beside)),
    )


def straight_rows(place, entered, final):
    share, width = entered[0].shape
    rows = 4 * share

    def kernel(at, *refs):
        blocks, finals, (own, other) = refs[:4], refs[4:8], refs[8:]
        here = at[0] == 0
        for k in range(4):
            start = share * lax.rem(at[1] + k, 4)
            values = blocks[k][...].astype(F32), finals[k][...].astype(F32)
            pairs = (
                (values[0], values[1][share : 2 * share]),
                (values[1][:share], values[1][2 * share :]),
            )
            for n, (zero, one) in enumerate(pairs):
                spot = pl.ds(pl.multiple_of(rows * n + start, share), share)
                own[spot, :] = jnp.where(here, zero, one).astype(BF)
                other[spot, :] = jnp.where(here, one, zero).astype(BF)

    return call(
        kernel,
        [((2 * rows, width), BF)] * 2,
        [place, *entered, *final],
        [SCALARS] + [WHOLE] * 8,
    )


def by_batch(place, own, other):
    rows, width = own.shape[0] // 2, own.shape[1]

    def kernel(at, own_ref, other_ref, activations, input_grads):
        for n, out in enumerate((activations, input_grads)):
            out[0, at[0]] = own_ref[rows * n : rows * (n + 1), :]
            out[0, 1 - at[0]] = other_ref[rows * n : rows * (n + 1), :]

    return call(
        kernel, [((1, 2, rows, width), BF)] * 2, [place, own, other], [SCALARS] + [WHOLE] * 2
    )


def per_device(
    inputs,
    cotangent,
    documents,
    routes,
    gain_attn,
    w_query,
    w_key,
    w_value,
    w_out,
    gain_moe,
    w_router,
    w_gate,
    w_up,
    w_down,
):
    section = lax.axis_index("section")
    expert = lax.axis_index("expert")
    tensor = lax.axis_index("tensor")
    sequences = lax.axis_size("expert")
    first = section == 0
    place = jnp.stack([section, tensor, expert]).astype(jnp.int32)
    rows, width = inputs.shape[1:]
    share = rows // 4
    expert_count = w_router.shape[2]
    own_weights = [w_query[0], w_key[0], w_value[0], w_out[0]]

    def own_rows(array):
        start = (section, share * tensor, 0)
        return lax.dynamic_slice(array, start, (1, share, array.shape[2]))[0]

    kept, given = prepare_experts(place, w_gate[0], w_up[0], w_down[0])
    given = sibling(given)
    quarter, *parts = choose_experts(place, kept, given, 0, width // 2)
    sides = start_gather(*parts)
    weights = own_weights + [sibling(w) for w in own_weights]

    gains_a = [gain_attn, sibling(gain_attn)]
    gains_m = [gain_moe, sibling(gain_moe)]
    routers = [w_router[0].T, sibling(w_router[0].T)]
    tables = prepare_tables(place, documents, w_query.shape[2] + w_key.shape[2])
    names_own = own_rows(routes)
    top = routes.shape[2]
    flow = own_rows(cotangent)

    entry = [own_rows(inputs), None]
    attn_saved, middles, shapeds, gates_own, arrived = ([None, None] for _ in range(5))
    pieces, attn_saved[0] = attention_forward([after(inputs, quarter)], tables, weights, gains_a, place, 0)
    quarter_one, *parts = choose_experts(
        place, kept, after(given, pieces[0]), 1, width // 4 * 3
    )
    pieces = arrivals(after(pieces, *sides, quarter_one))
    middles[0], copies, shapeds[0], gates_own[0] = middle_rows(
        entry[0], pieces, gains_m, names_own, routers, place, 0, sequences
    )
    mine = [quarter, *sides, *end_gather(after(quarter, *pieces), *sides)]
    expert_weights = [[*mine, *[sibling(block) for block in mine]], None]
    arrived[0] = exchange_e(copies).reshape(-1, width + BESIDE)
    backs = [None, spread_e(after(flow, copies)).reshape(-1, width)]
    arrived[0] = after(arrived[0], *mine[3:])
    parts = after(tuple(parts), *mine[3:])
    sides = start_gather(*parts)
    terms, pre, gates, names = experts_forward(arrived[0], top, routers, expert_weights[0], place, 0)
    terms = after(terms, backs[1])
    pieces = exchange_e(terms.reshape(-1, share, width))
    mine = [quarter_one, *sides, *end_gather(quarter_one, *sides)]
    expert_weights[1] = [*mine, *[sibling(block) for block in mine]]
    entry[1] = leave_rows(middles[0], after(pieces, *mine[3:]))

    blocks = gather_x(entry[1])
    outputs = [blocks, None]
    pieces, attn_saved[1] = attention_forward(blocks, tables, weights, gains_a, place, 1)
    pieces = arrivals(pieces)
    middles[1], copies, shapeds[1], gates_own[1] = middle_rows(
        entry[1], pieces, gains_m, names_own, routers, place, 1, sequences
    )
    arrived[1] = exchange_e(copies).reshape(-1, width)
    terms, back_pre, hidden = experts_both(
        arrived[1], names, top, routers, backs[1], expert_weights[1], place, 1
    )

    def start_ring(mines, others):
        half = width // 2
        two = sum_of([mines[2], others[2]])
        return shifted(two[:half], "tensor", 1), shifted(two[half:], "tensor", -1)

    def ring_parts(mines, others, low, high):
        half = width // 2
        return (
            jnp.concatenate(
                [sum_of([mines[1, :half], others[1, :half], low]), sum_of([mines[1, half:], others[1, half:]])]
            ),
            jnp.concatenate(
                [sum_of([mines[3, :half], others[3, :half]]), sum_of([mines[3, half:], others[3, half:], high])]
            ),
        )

    def end_ring(first, third):
        return shifted(first, "tensor", 1), shifted(third, "tensor", -1)

    in_blocks, smalls, grads_gain = ([None, None] for _ in range(3))
    pieces = exchange_e(terms.reshape(-1, share, width + BESIDE))
    mines, others = experts_grads(arrived[1], backs[1], back_pre, hidden)
    outs = experts_out(hidden, expert_weights[1])
    back_middle, rounded, smalls[1] = back_middle_rows(
        flow, after(pieces, mines, others, outs), middles[1], shapeds[1], gates_own[1], gains_m, routers, place, 1
    )
    others = sibling(after(others, rounded))
    out_pieces = exchange_e(after(outs, rounded).reshape(-1, share, width))
    partial, branch, back_qkv = attention_backward(
        gather_x(rounded), attn_saved[1], tables, weights, place, 1
    )
    flow, grads_gain[1], copies = back_entry_rows(
        back_middle, arrivals(partial), entry[1], gains_a, place, 1, sequences
    )
    copies = after(copies, out_pieces)
    backs[0] = exchange_e(copies).reshape(-1, width)
    last = leave_rows(middles[1], out_pieces, (flow,))
    mine_half, other_half = attention_grads(place, after(back_qkv, last), attn_saved[1], branch)
    mines = after(mines, last)
    twos = start_ring(mines, others)
    half_one = sum_of([mine_half, sibling(other_half)])
    backs[0] = after(backs[0], half_one, *twos)
    ends = end_ring(*ring_parts(mines, others, *twos))
    own = sum_of([mines[0], others[0]])

    piece = collect_e(after(half_one, backs[0]).reshape(sequences, -1, half_one.shape[1]))
    terms, back_pre, hidden = experts_backward(backs[0], pre, gates, expert_weights[0])
    terms = after(terms, piece)
    pieces = exchange_e(terms.reshape(-1, share, width + BESIDE))
    mines, others = experts_grads(arrived[0], backs[0], back_pre, hidden)
    sums = [None, sum_of([own, *ends])]
    piece_one = piece
    pieces = after(pieces, mines, others, sums[1])
    back_middle, rounded, smalls[0] = back_middle_rows(
        flow, pieces, middles[0], shapeds[0], gates_own[0], gains_m, routers, place, 0
    )
    others = sibling(after(others, rounded))

    def own_layer(of_first, of_second):
        own = jnp.where(first, of_first, of_second)
        return own + sibling(jnp.where(first, of_second, of_first).astype(BF)).astype(F32)

    small = own_layer(smalls[0], smalls[1]).astype(BF)
    gathered = after(gather_x(rounded), small)
    partial, branch, back_qkv = attention_backward(gathered, attn_saved[0], tables, weights, place, 0)
    mine_half, other_half = attention_grads(place, back_qkv, attn_saved[0], branch)
    half_zero = jnp.concatenate([sum_of([mine_half, sibling(other_half)]), small], axis=1)
    cut = half_zero.shape[1]
    both = jnp.concatenate(
        [
            half_zero.reshape(sequences, -1, cut),
            jnp.broadcast_to(piece_one[None], (sequences, *piece_one.shape)),
        ],
        axis=2,
    )
    pieces = after(arrivals(partial), both)
    both = exchange_e(both)
    final, grads_gain[0] = back_entry_rows(
        back_middle, pieces, entry[0], gains_a, place, 0, 0, (last,)
    )

    finals = gather_x(final)
    twos = start_ring(after(mines, *finals[1:]), others)
    piece = jnp.sum(both[:, :, :cut].astype(F32), axis=0).astype(BF)
    done_one = both.reshape(half_one.shape[0], -1)[:, cut:]
    gain = own_layer(grads_gain[0], grads_gain[1]).reshape(width // 128, 128).astype(BF)
    gain = jnp.pad(gain, ((0, piece.shape[0] - width // 128), (0, 0)))
    piece = jnp.concatenate([piece, gain], axis=1)
    mine, other = straight_rows(place, outputs[0], finals)
    activations, input_grads = by_batch(place, mine, sibling(other))
    parts = ring_parts(after(mines, activations), others, *twos)
    ends = end_ring(*parts)
    sums[0] = sum_of([mines[0], others[0], *ends])
    grad_gate, grad_up, grad_down = experts_finish(
        place, [*sums, to_core(sums[0], 0), to_core(sums[1], 1)]
    )
    spread = after(spread_e(piece), grad_gate)
    gain = jnp.sum(spread[:, : width // 128, -128:].astype(F32), axis=0).astype(BF)
    done_zero = spread.reshape(half_one.shape[0], -1)
    small = jnp.concatenate([done_zero[:, -256:-128], gain], axis=0)
    blocks = gather_x(small)
    widths = [w_query.shape[2], w_key.shape[2], w_value.shape[2]]
    begun = attention_finish(place, done_zero, done_one, widths, False)
    grad_query, grad_key, grad_value, grad_out = attention_finish(
        place, to_core(done_zero, 0), to_core(done_one, 1), widths, True, begun
    )
    grad_router, grad_gain_m, gain = small_finish(after(blocks, grad_query), expert_count)
    return (
        activations,
        input_grads,
        gain,
        grad_query,
        grad_key,
        grad_value,
        grad_out,
        grad_gain_m,
        grad_router.T[None],
        grad_gate,
        grad_up,
        grad_down,
    )


def solution(mesh):
    in_specs = (
        P(None, "expert", None),
        P(None, "expert", None),
        P(None, "expert", None),
        P(None, "expert", None),
        P("section", None),
        P("section", None, "tensor"),
        P("section", None, "tensor"),
        P("section", None, "tensor"),
        P("section", "tensor", None),
        P("section", None),
        P("section", None, None),
        P("section", "expert", None, "tensor"),
        P("section", "expert", None, "tensor"),
        P("section", "expert", "tensor", None),
    )
    out_specs = (
        P("section", None, "expert", None),
        P("section", None, "expert", None),
        P("section", None),
        P("section", None, "tensor"),
        P("section", None, "tensor"),
        P("section", None, "tensor"),
        P("section", "tensor", None),
        P("section", None),
        P("section", None, None),
        P("section", "expert", None, "tensor"),
        P("section", "expert", None, "tensor"),
        P("section", "expert", "tensor", None),
    )
    return jax.shard_map(
        per_device, mesh=mesh, in_specs=in_specs, out_specs=out_specs, check_vma=False
    )
```

```python
import math

import jax
import jax.numpy as jnp
from jax import lax
from jax.experimental import pallas as pl
from jax.experimental.pallas import tpu as pltpu
from jax.sharding import PartitionSpec as P

HEADS = 24
KV_HEADS = 8
HEAD_DIM = 64
SHARING = HEADS // KV_HEADS
EPSILON = 1e-06
LOWEST = -1e30
BF = jnp.bfloat16
F32 = jnp.float32
ANY = pl.BlockSpec(memory_space=pl.ANY)
WHOLE = pl.BlockSpec(memory_space=pltpu.VMEM)
SCALARS = pl.BlockSpec(memory_space=pltpu.SMEM)
BESIDE = 128


def shifted(array, axis, by):
    length = lax.axis_size(axis)
    return lax.ppermute(array, axis, [(i, (i + by) % length) for i in range(length)])


def sibling(array):
    return shifted(array, "section", 1)


def to_core(array, core):
    return lax.ppermute(array, "section", [(1 - core, core)])


def after(value, *others):
    return lax.optimization_barrier((value, *others))[0]


def gather_x(block):
    ahead = {k: shifted(block, "tensor", -k) for k in (1, 3, 2)}
    return [block, ahead[1], ahead[2], ahead[3]]


def start_gather(upper, lower):
    return shifted(upper, "tensor", -1), shifted(lower, "tensor", 1)


def end_gather(block, one, three):
    width, sent = block.shape[0], one.shape[0]
    half = width // 2
    return (
        shifted(jnp.concatenate([block[sent:], one[:half]], axis=0), "tensor", -1),
        shifted(jnp.concatenate([block[: width - sent], three[sent - half :]], axis=0), "tensor", 1),
    )


def arrivals(blocks):
    return [blocks[0]] + [shifted(blocks[k], "tensor", k) for k in (1, 2, 3)]


def sum_of(blocks):
    return sum(block.astype(F32) for block in blocks).astype(BF)


def spread_e(block):
    return exchange_e(jnp.broadcast_to(block[None], (lax.axis_size("expert"), *block.shape)))


def exchange_e(blocks):
    return lax.all_to_all(blocks, "expert", 0, 0, tiled=True)


def collect_e(blocks):
    return jnp.sum(exchange_e(blocks).astype(F32), axis=0).astype(BF)


def dot(left, right):
    return jnp.dot(left, right, preferred_element_type=F32)


def contract_rows(left, right):
    return lax.dot_general(left, right, (((0,), (0,)), ((), ())), preferred_element_type=F32)


def contract_cols(left, right):
    return lax.dot_general(left, right, (((1,), (1,)), ((), ())), preferred_element_type=F32)


def call(kernel, outs, args, specs, scratch=(), grid=None, out_specs=None):
    extra = {} if grid is None else {"grid": grid}
    return pl.pallas_call(
        kernel,
        out_shape=[jax.ShapeDtypeStruct(shape, kind) for shape, kind in outs],
        in_specs=specs,
        out_specs=out_specs or [WHOLE] * len(outs),
        scratch_shapes=list(scratch),
        compiler_params=pltpu.CompilerParams(vmem_limit_bytes=60 * 2**20),
        cost_estimate=pl.CostEstimate(flops=1, bytes_accessed=1, transcendentals=0),
        **extra,
    )(*args)


def inverse_level(rows):
    return lax.rsqrt(jnp.mean(rows * rows, axis=-1, keepdims=True) + EPSILON)


def norm_back(back_scaled, rows, gain):
    inverse = inverse_level(rows)
    unit = rows * inverse
    back_unit = back_scaled * gain
    level = inverse * (back_unit - unit * jnp.mean(back_unit * unit, axis=-1, keepdims=True))
    return level, jnp.sum(back_scaled * unit, axis=0, keepdims=True)


def of_layer(layer, section, own, other):
    return jnp.where(section == layer, own[...].astype(F32), other[...].astype(F32))


def prepare_tables(place, documents, columns):
    rows = documents.shape[2]
    share = rows // 4

    def kernel(at, doc_ref, cos, sin, mask):
        turn = share * at[1]
        doc = pltpu.roll(doc_ref[at[0]].astype(F32), lax.rem(rows - turn, rows), 1)
        along = jnp.broadcast_to(doc, (rows, rows))
        down = along.T
        place_along = lax.rem(lax.broadcasted_iota(jnp.int32, (rows, rows), 1) + turn, rows)
        place_down = lax.rem(lax.broadcasted_iota(jnp.int32, (rows, rows), 0) + turn, rows)
        mask[...] = jnp.where((along == down) & (place_along <= place_down), 0.0, LOWEST)
        starts = jnp.sum(jnp.where(along < down, 1.0, 0.0), axis=1, keepdims=True)
        lane = lax.broadcasted_iota(jnp.int32, (rows, 128), 1)
        frequency = jnp.exp(lax.rem(lane, HEAD_DIM // 2).astype(F32) * (-2.0 * math.log(10000.0) / HEAD_DIM))
        offset = place_down[:, :1].astype(F32) - starts
        angle = offset * frequency
        for ref, table in ((cos, jnp.cos(angle)), (sin, jnp.sin(angle))):
            for a in range(0, columns, 128):
                ref[:, a : a + 128] = table

    return call(
        kernel,
        [((rows, columns), F32), ((rows, columns), F32), ((rows, rows), F32)],
        [place, documents],
        [SCALARS, WHOLE],
    )


def half_turn(values):
    lane = lax.broadcasted_iota(jnp.int32, values.shape, 1)
    width = values.shape[1]
    behind = pltpu.roll(values, width - HEAD_DIM // 2, 1)
    before = pltpu.roll(values, HEAD_DIM // 2, 1)
    return jnp.where(lane % HEAD_DIM < HEAD_DIM // 2, -behind, before)


def pick(layer, section, own, other, target, sem, start):
    for here, source in ((True, own), (False, other)):

        @pl.when((section == layer) == here)
        def _():
            copy = pltpu.make_async_copy(source, target, sem)
            copy.start() if start else copy.wait()


def pick_all(layer, section, weights, qkv, out, sems, which, start):
    at = 0
    for i in range(4):
        width = weights[i].shape[1]
        target = out if i == 3 else qkv.at[:, at : at + width]
        at += width
        if i in which:
            pick(layer, section, weights[i], weights[4 + i], target, sems.at[i], start)


def attention_forward(source, tables, weights, gains, place, layer):
    width, q_cols = weights[0].shape
    kv_cols = weights[1].shape[1]
    all_cols = q_cols + 2 * kv_cols
    heads = q_cols // HEAD_DIM
    rows = tables[0].shape[0]
    share = rows // 4
    entries = len(source)

    def kernel(at, *refs):
        entry, refs = refs[:entries], refs[entries:]
        (cos, sin, allowed, gain_own, gain_other), refs = refs[:5], refs[5:]
        parts, refs = refs[:8], refs[8:]
        (p0, p1, p2, p3, normed, qkv, lse, attended, w_qkv, w_out, staged, sems) = refs
        section = at[0]
        if entries == 1:
            copies = [
                pltpu.make_async_copy(
                    entry[0].at[section, pl.ds(pl.multiple_of(share * lax.rem(at[1] + k, 4), share), share)],
                    staged.at[share * k : share * (k + 1)],
                    sems.at[4 + k],
                )
                for k in range(4)
            ]
            for copy in copies:
                copy.start()
        pick_all(layer, section, parts, w_qkv, w_out, sems, range(4), True)
        gain = of_layer(layer, section, gain_own, gain_other)
        for k in range(4):
            if entries == 1:
                copies[k].wait()
                x = staged[share * k : share * (k + 1), :].astype(F32)
            else:
                x = entry[k][...].astype(F32)
            normed[share * k : share * (k + 1), :] = (x * inverse_level(x) * gain).astype(BF)
        pick_all(layer, section, parts, w_qkv, w_out, sems, range(3), False)
        raw = dot(normed[...], w_qkv[...])
        turned = raw[:, : q_cols + kv_cols]
        turned = turned * cos[...] + half_turn(turned) * sin[...]
        qkv[:, : q_cols + kv_cols] = turned.astype(BF)
        qkv[:, q_cols + kv_cols :] = raw[:, q_cols + kv_cols :].astype(BF)
        sums = jnp.zeros((rows, 128), F32)
        lane = lax.broadcasted_iota(jnp.int32, (rows, 128), 1)
        for h in range(heads):
            g = h // SHARING
            q = qkv[:, HEAD_DIM * h : HEAD_DIM * (h + 1)]
            key = qkv[:, q_cols + HEAD_DIM * g : q_cols + HEAD_DIM * (g + 1)]
            value = qkv[:, q_cols + kv_cols + HEAD_DIM * g : q_cols + kv_cols + HEAD_DIM * (g + 1)]
            scores = contract_cols(q, key) * HEAD_DIM**-0.5 + allowed[...]
            peak = jnp.max(scores, axis=-1, keepdims=True)
            raised = jnp.exp(scores - peak)
            total = jnp.sum(raised, axis=-1, keepdims=True)
            sums = jnp.where(lane == h, peak + jnp.log(total), sums)
            probability = (raised / total).astype(BF)
            attended[:, HEAD_DIM * h : HEAD_DIM * (h + 1)] = dot(probability, value).astype(BF)
        lse[...] = sums
        pick_all(layer, section, parts, w_qkv, w_out, sems, (3,), False)
        partial = dot(attended[...], w_out[...]).astype(BF)
        for k, ref in enumerate((p0, p1, p2, p3)):
            ref[...] = partial[share * k : share * (k + 1), :]

    results = call(
        kernel,
        [((share, width), BF)] * 4
        + [((rows, width), BF), ((rows, all_cols), BF), ((rows, 128), F32), ((rows, q_cols), BF)],
        [place, *source, *tables, *gains, *weights],
        [SCALARS] + [ANY if entries == 1 else WHOLE] * entries + [WHOLE] * 5 + [ANY] * 8,
        [
            pltpu.VMEM((width, all_cols), BF),
            pltpu.VMEM((q_cols, width), BF),
            pltpu.VMEM((rows, width), BF),
            pltpu.SemaphoreType.DMA((8,)),
        ],
    )
    return results[:4], results[4:]


def attention_backward(blocks, saved, tables, weights, place, layer):
    normed, qkv, lse, attended = saved
    rows, width = normed.shape
    q_cols = weights[0].shape[1]
    kv_cols = weights[1].shape[1]
    all_cols = q_cols + 2 * kv_cols
    groups = kv_cols // HEAD_DIM
    share = rows // 4

    def kernel(at, b0, b1, b2, b3, qkv_ref, lse_ref, cos, sin, allowed, *refs):
        parts, refs = refs[:8], refs[8:]
        p0, p1, p2, p3, branch, back_qkv, w_qkv, w_out, back_o, back_qk, sems = refs
        section = at[0]
        pick_all(layer, section, parts, w_qkv, w_out, sems, (3, 0, 1, 2), True)
        for k, ref in enumerate((b0, b1, b2, b3)):
            branch[share * k : share * (k + 1), :] = ref[...]
        pick_all(layer, section, parts, w_qkv, w_out, sems, (3,), False)
        back_o[...] = contract_cols(branch[...], w_out[...]).astype(BF)
        for g in range(groups):
            at_k = q_cols + HEAD_DIM * g
            at_v = q_cols + kv_cols + HEAD_DIM * g
            key = qkv_ref[:, at_k : at_k + HEAD_DIM]
            value = qkv_ref[:, at_v : at_v + HEAD_DIM]
            back_value = jnp.zeros((rows, HEAD_DIM), F32)
            back_key = jnp.zeros((rows, HEAD_DIM), F32)
            for h in range(SHARING * g, SHARING * (g + 1)):
                q = qkv_ref[:, HEAD_DIM * h : HEAD_DIM * (h + 1)]
                back = back_o[:, HEAD_DIM * h : HEAD_DIM * (h + 1)]
                scores = contract_cols(q, key) * HEAD_DIM**-0.5 + allowed[...]
                probability = jnp.exp(scores - lse_ref[:, h : h + 1])
                back_p = contract_cols(back, value)
                back_value = back_value + contract_rows(probability.astype(BF), back)
                delta = jnp.sum(back_p * probability, axis=-1, keepdims=True)
                back_s = (probability * (back_p - delta)).astype(BF)
                back_qk[:, HEAD_DIM * h : HEAD_DIM * (h + 1)] = dot(back_s, key)
                back_key = back_key + contract_rows(back_s, q)
            back_qk[:, at_k : at_k + HEAD_DIM] = back_key
            back_qkv[:, at_v : at_v + HEAD_DIM] = back_value.astype(BF)
        scaled = back_qk[...] * HEAD_DIM**-0.5
        turned = scaled * cos[...] - half_turn(scaled * sin[...])
        back_qkv[:, : q_cols + kv_cols] = turned.astype(BF)
        pick_all(layer, section, parts, w_qkv, w_out, sems, range(3), False)
        partial = contract_cols(back_qkv[...], w_qkv[...]).astype(BF)
        for k, ref in enumerate((p0, p1, p2, p3)):
            ref[...] = partial[share * k : share * (k + 1), :]

    results = call(
        kernel,
        [((share, width), BF)] * 4 + [((rows, width), BF), ((rows, all_cols), BF)],
        [place, *blocks, qkv, lse, *tables, *weights],
        [SCALARS] + [WHOLE] * 9 + [ANY] * 8,
        [
            pltpu.VMEM((width, all_cols), BF),
            pltpu.VMEM((q_cols, width), BF),
            pltpu.VMEM((rows, q_cols), BF),
            pltpu.VMEM((rows, q_cols + kv_cols), F32),
            pltpu.SemaphoreType.DMA((4,)),
        ],
    )
    return results[:4], results[4], results[5]


def attention_grads(place, back_qkv, saved, branch):
    normed, attended = saved[0], saved[3]
    rows, width = normed.shape
    all_cols, q_cols = back_qkv.shape[1], attended.shape[1]
    half = width // 2

    def kernel(at, back_ref, normed_ref, attended_ref, branch_ref, mine, other):
        for out, which in ((other, 1 - at[0]), (mine, at[0])):
            for a in range(0, half, 256):
                columns = pl.ds(pl.multiple_of(half * which + a, 256), 256)
                out[a : a + 256, :all_cols] = contract_rows(normed_ref[:, columns], back_ref[...]).astype(BF)
                out[a : a + 256, all_cols:] = contract_rows(branch_ref[:, columns], attended_ref[...]).astype(BF)

    return call(
        kernel,
        [((half, all_cols + q_cols), BF)] * 2,
        [place, back_qkv, normed, attended, branch],
        [SCALARS] + [WHOLE] * 4,
    )


def attention_finish(place, of_first, of_second, widths, theirs, begun=()):
    half, q_cols = of_first.shape[0], widths[0]
    ends = [sum(widths[:k]) for k in range(4)]
    known = len(begun)

    def kernel(at, h0, h1, *refs):
        *grads, rows, turned, sems = refs[known:]
        which = 1 - at[0] if theirs else at[0]

        def store(ref):
            rows[...] = ref[:, : ends[3]].astype(F32)
            turned[...] = ref[:, ends[3] : ends[3] + q_cols].astype(F32).T

        pl.when(at[0] == 0)(lambda: store(h0))
        pl.when(at[0] == 1)(lambda: store(h1))
        spot = pl.ds(pl.multiple_of(half * which, half), half)
        copies = [
            pltpu.make_async_copy(rows.at[:, start : start + width], grad.at[0, spot, :], sems.at[k])
            for k, (grad, start, width) in enumerate(zip(grads, ends, widths))
        ]
        copies.append(pltpu.make_async_copy(turned, grads[3].at[0, :, spot], sems.at[3]))
        for copy in copies:
            copy.start()
        for copy in copies:
            copy.wait()

    shapes = [(1, 2 * half, w) for w in widths] + [(1, q_cols, 2 * half)]
    return pl.pallas_call(
        kernel,
        out_shape=[jax.ShapeDtypeStruct(shape, F32) for shape in shapes],
        in_specs=[SCALARS, WHOLE, WHOLE] + [ANY] * known,
        out_specs=[ANY] * 4,
        scratch_shapes=[
            pltpu.VMEM((half, ends[3]), F32),
            pltpu.VMEM((q_cols, half), F32),
            pltpu.SemaphoreType.DMA((4,)),
        ],
        input_output_aliases={3 + k: k for k in range(known)},
        compiler_params=pltpu.CompilerParams(vmem_limit_bytes=60 * 2**20),
        cost_estimate=pl.CostEstimate(flops=1, bytes_accessed=1, transcendentals=0),
    )(place, of_first, of_second, *begun)


def small_finish(blocks, count):
    chunks = blocks[0].shape[0] // 65
    width = chunks * 128

    def kernel(a, b, c, d, router, gain_m, gain_a):
        total = a[...].astype(F32) + b[...].astype(F32) + c[...].astype(F32) + d[...].astype(F32)
        for i in range(chunks):
            columns = slice(128 * i, 128 * (i + 1))
            router[:, columns] = total[64 * i : 64 * i + count, :]
            gain_m[:, columns] = total[64 * i + count : 64 * i + count + 1, :]
            gain_a[:, columns] = total[64 * chunks + i : 64 * chunks + i + 1, :]

    return call(
        kernel,
        [((count, width), F32), ((1, width), F32), ((1, width), F32)],
        blocks,
        [WHOLE] * 4,
    )


def prepare_experts(place, w_gate, w_up, w_down):
    _, width, deep = w_gate.shape

    def kernel(at, gate, up, down, kept, given):
        for out, which in ((given, 1 - at[0]), (kept, at[0])):
            out[:, :deep] = gate[which]
            out[:, deep : 2 * deep] = up[which]
            out[:, 2 * deep :] = down[which].T

    return call(
        kernel,
        [((width, 3 * deep), BF)] * 2,
        [place, w_gate, w_up, w_down],
        [SCALARS] + [WHOLE] * 3,
    )


def choose_experts(place, kept, given, layer, sent):
    width, cols = kept.shape

    def kernel(at, kept_ref, given_ref, whole, upper, lower):
        def store(ref):
            whole[...] = ref[...]
            upper[...] = ref[:sent, :]
            lower[...] = ref[width - sent :, :]

        pl.when(at[0] == layer)(lambda: store(kept_ref))
        pl.when(at[0] != layer)(lambda: store(given_ref))

    return call(
        kernel,
        [((width, cols), BF), ((sent, cols), BF), ((sent, cols), BF)],
        [place, kept, given],
        [SCALARS] + [WHOLE] * 2,
    )


def load_experts(refs, gate_up, down, sems):
    each = len(refs) // 2
    width, deep = down.shape[0], refs[0].shape[1] // 3
    half, sent = width // 2, refs[1].shape[0]
    rest = width - sent
    spots = [
        [(0, (0, width), 0)],
        [(1, (0, sent), 0)],
        [(3, (rest, sent), 0)],
        [(1, (sent, rest), 0), (2, (0, half), rest)],
        [(3, (0, rest), 0), (2, (half, half), rest)],
    ]
    up_copies, down_copies = [[], []], [[], []]
    sem = 0
    for k in range(2):
        for ref, pieces in zip(refs[each * k : each * (k + 1)], spots):
            for block, (start, count), source in pieces:
                at = 4 * k + block
                rows, taken = slice(start, start + count), slice(source, source + count)
                if gate_up is not None:
                    target = gate_up.at[rows, 2 * deep * at : 2 * deep * (at + 1)]
                    up_copies[k].append(
                        pltpu.make_async_copy(ref.at[taken, : 2 * deep], target, sems.at[sem])
                    )
                target = down.at[rows, deep * at : deep * (at + 1)]
                down_copies[k].append(
                    pltpu.make_async_copy(ref.at[taken, 2 * deep :], target, sems.at[sem + 1])
                )
                sem += 2
    return up_copies, down_copies


def start_all(*groups):
    for group in groups:
        for copies in group:
            for copy in copies:
                copy.start()


def wait_all(copies):
    for copy in copies:
        copy.wait()


def gate_table(rows, names, router):
    count, width = rows.shape[0], router.shape[0]
    number = lax.broadcasted_iota(jnp.int32, (count, width), 1).astype(F32)
    chosen = jnp.zeros((count, width), F32)
    for j in range(names.shape[1]):
        chosen = jnp.where(number == names[:, j : j + 1], 1.0, chosen)
    logits = jnp.where(chosen > 0, contract_cols(rows, router), LOWEST)
    raised = jnp.where(chosen > 0, jnp.exp(logits - jnp.max(logits, axis=-1, keepdims=True)), 0.0)
    return raised / jnp.sum(raised, axis=-1, keepdims=True)


def expert_gates(x, names, router, at):
    table = gate_table(x, names, router)
    number = lax.broadcasted_iota(jnp.int32, table.shape, 1)
    wanted = (2 * at[2] + at[0], 2 * at[2] + 1 - at[0])
    return [jnp.sum(jnp.where(number == e, table, 0.0), axis=-1, keepdims=True) for e in wanted]


def keep_gates(gates, own):
    lane = lax.broadcasted_iota(jnp.int32, gates.shape, 1)
    gates[...] = jnp.where(lane == 0, own[0], jnp.where(lane == 1, own[1], 0.0))


def expert_down(hidden, down, out):
    width = down.shape[0]
    for a in range(0, width, 256):
        out[:, a : a + 256] = contract_cols(hidden[...], down[a : a + 256, :]).astype(BF)


def leave(pairs, sems):
    copies = [pltpu.make_async_copy(a, b, sems.at[k]) for k, (a, b) in enumerate(pairs)]
    for copy in copies:
        copy.start()
    return copies


def expert_backs(back, gate_up, down, waits, pre, gates, out, back_pre, hidden, kept, sems):
    count, width = back.shape
    deep = hidden.shape[1] // 8
    lane = lax.broadcasted_iota(jnp.int32, (count, BESIDE), 1)
    beside = jnp.zeros((count, BESIDE), F32)
    for k in range(2):
        wait_all(waits[0][k])
        gate_weight = gates[:, k : k + 1]
        inner = jnp.zeros((count, 1), F32)
        for b in range(0, 4, 2):
            first = deep * (4 * k + b)
            raw = dot(back[...], down[:, first : first + 2 * deep])
            for c in range(2):
                gate, up = pre(k, b + c)
                piece = raw[:, deep * c : deep * (c + 1)]
                sigma = 1.0 / (1.0 + jnp.exp(-gate))
                smooth = gate * sigma
                full = smooth * up
                inner = inner + jnp.sum(piece * full, axis=-1, keepdims=True)
                at = first + deep * c
                hidden[:, at : at + deep] = (gate_weight * full).astype(BF)
                flow = gate_weight * piece
                back_pre[:, 2 * at : 2 * at + deep] = (
                    flow * up * sigma * (1.0 + gate * (1.0 - sigma))
                ).astype(BF)
                back_pre[:, 2 * at + deep : 2 * at + 2 * deep] = (flow * smooth).astype(BF)
        high = inner.astype(BF).astype(F32)
        beside = jnp.where(lane == 2 * k, high, jnp.where(lane == 2 * k + 1, inner - high, beside))
    out[:, width:] = beside.astype(BF)
    copies = leave([(back_pre, kept[0]), (hidden, kept[1])], sems)
    for k in range(2):
        wait_all(waits[1][k])
    for a in range(0, width, 256):
        out[:, a : a + 256] = contract_cols(back_pre[...], gate_up[a : a + 256, :]).astype(BF)
    wait_all(copies)


def experts_forward(rows, top, router, weights, place, layer):
    count, width = rows.shape[0], rows.shape[1] - BESIDE
    deep = weights[0].shape[1] // 3
    used = len(weights)

    def kernel(at, x, router_own, router_other, *refs):
        parts, outs, scratch = refs[:used], refs[used : used + 4], refs[used + 4 :]
        (out, kept, gates, names), (gate_up, down, hidden, pre, sems, leave_sems) = outs, scratch
        up_copies, down_copies = load_experts(parts, gate_up, down, sems)
        start_all(up_copies, down_copies)
        table = of_layer(layer, at[0], router_own, router_other).astype(BF)
        names[...] = x[:, width:]
        numbers = x[:, width:].astype(F32)[:, :top]
        keep_gates(gates, expert_gates(x[:, :width], numbers, table, at))
        for k in range(2):
            wait_all(up_copies[k])
            for b in range(4):
                at_b = deep * (4 * k + b)
                both = dot(x[:, :width], gate_up[:, 2 * at_b : 2 * at_b + 2 * deep])
                pre[:, 2 * at_b : 2 * at_b + 2 * deep] = both.astype(BF)
                gate, up = both[:, :deep], both[:, deep:]
                value = gates[:, k : k + 1] * gate * up / (1.0 + jnp.exp(-gate))
                hidden[:, at_b : at_b + deep] = value.astype(BF)
        leaving = leave([(pre, kept)], leave_sems)
        for k in range(2):
            wait_all(down_copies[k])
        expert_down(hidden, down, out)
        wait_all(leaving)

    return call(
        kernel,
        [((count, width), BF), ((count, 16 * deep), BF), ((count, 128), F32), ((count, BESIDE), BF)],
        [place, rows, *router, *weights],
        [SCALARS] + [WHOLE] * 3 + [ANY] * used,
        [
            pltpu.VMEM((width, 16 * deep), BF),
            pltpu.VMEM((width, 8 * deep), BF),
            pltpu.VMEM((count, 8 * deep), BF),
            pltpu.VMEM((count, 16 * deep), BF),
            pltpu.SemaphoreType.DMA((28,)),
            pltpu.SemaphoreType.DMA((1,)),
        ],
        out_specs=[WHOLE, ANY, WHOLE, WHOLE],
    )


def experts_backward(back, pre, gates, weights):
    count, width = back.shape
    deep = weights[0].shape[1] // 3
    used = len(weights)

    def kernel(back_ref, pre_ref, gates_ref, *refs):
        parts, (out, *kept), scratch = refs[:used], refs[used : used + 3], refs[used + 3 :]
        gate_up, down, back_pre, hidden, sems, leave_sems = scratch
        up_copies, down_copies = load_experts(parts, gate_up, down, sems)
        start_all(down_copies, up_copies)

        def acts(k, b):
            at = 2 * deep * (4 * k + b)
            both = pre_ref[:, at : at + 2 * deep].astype(F32)
            return both[:, :deep], both[:, deep:]

        expert_backs(
            back_ref, gate_up, down, (down_copies, up_copies), acts, gates_ref, out, back_pre, hidden, kept, leave_sems
        )

    return call(
        kernel,
        [((count, width + BESIDE), BF), ((count, 16 * deep), BF), ((count, 8 * deep), BF)],
        [back, pre, gates, *weights],
        [WHOLE] * 3 + [ANY] * used,
        [
            pltpu.VMEM((width, 16 * deep), BF),
            pltpu.VMEM((width, 8 * deep), BF),
            pltpu.VMEM((count, 16 * deep), BF),
            pltpu.VMEM((count, 8 * deep), BF),
            pltpu.SemaphoreType.DMA((28,)),
            pltpu.SemaphoreType.DMA((2,)),
        ],
        out_specs=[WHOLE, ANY, ANY],
    )


def experts_both(rows, names, top, router, back, weights, place, layer):
    count, width = rows.shape
    deep = weights[0].shape[1] // 3
    used = len(weights)

    def kernel(at, x, names_ref, router_own, router_other, back_ref, *refs):
        parts, (out, *kept), scratch = refs[:used], refs[used : used + 3], refs[used + 3 :]
        gate_up, down, pre, gates, back_pre, hidden, sems, leave_sems = scratch
        up_copies, down_copies = load_experts(parts, gate_up, down, sems)
        start_all(up_copies, down_copies)
        table = of_layer(layer, at[0], router_own, router_other).astype(BF)
        numbers = names_ref[...].astype(F32)[:, :top]
        keep_gates(gates, expert_gates(x[...], numbers, table, at))
        for k in range(2):
            wait_all(up_copies[k])
            for b in range(4):
                at_b = 2 * deep * (4 * k + b)
                pre[:, at_b : at_b + 2 * deep] = dot(x[...], gate_up[:, at_b : at_b + 2 * deep])

        def acts(k, b):
            at_b = 2 * deep * (4 * k + b)
            return pre[:, at_b : at_b + deep], pre[:, at_b + deep : at_b + 2 * deep]

        expert_backs(
            back_ref, gate_up, down, (down_copies, ([], [])), acts, gates, out, back_pre, hidden, kept, leave_sems
        )

    return call(
        kernel,
        [((count, width + BESIDE), BF), ((count, 16 * deep), BF), ((count, 8 * deep), BF)],
        [place, rows, names, *router, back, *weights],
        [SCALARS] + [WHOLE] * 5 + [ANY] * used,
        [
            pltpu.VMEM((width, 16 * deep), BF),
            pltpu.VMEM((width, 8 * deep), BF),
            pltpu.VMEM((count, 16 * deep), F32),
            pltpu.VMEM((count, 128), F32),
            pltpu.VMEM((count, 16 * deep), BF),
            pltpu.VMEM((count, 8 * deep), BF),
            pltpu.SemaphoreType.DMA((28,)),
            pltpu.SemaphoreType.DMA((2,)),
        ],
        out_specs=[WHOLE, ANY, ANY],
    )


def experts_out(hidden, weights):
    count = hidden.shape[0]
    width, deep = weights[0].shape[0], weights[0].shape[1] // 3
    used = len(weights)

    def kernel(hidden_ref, *refs):
        parts, out, down, sems = refs[:used], *refs[used:]
        _, down_copies = load_experts(parts, None, down, sems)
        start_all(down_copies)
        wait_all(down_copies[0] + down_copies[1])
        expert_down(hidden_ref, down, out)

    return call(
        kernel,
        [((count, width), BF)],
        [hidden, *weights],
        [WHOLE] + [ANY] * used,
        [pltpu.VMEM((width, 8 * deep), BF), pltpu.SemaphoreType.DMA((28,))],
    )[0]


def experts_grads(rows, back, back_pre, hidden):
    count, width = back.shape
    deep = hidden.shape[1] // 8

    def kernel(x, back_ref, pre_ref, hidden_ref, mine, other, rows_turned, back_turned):
        step = pl.program_id(0)

        @pl.when(step == 0)
        def _():
            rows_turned[...] = x[:, :width].T
            back_turned[...] = back_ref[...].T

        def store(out):
            for a in range(0, width, 512):
                out[0, a : a + 512, : 2 * deep] = dot(rows_turned[a : a + 512, :], pre_ref[...]).astype(BF)
                out[0, a : a + 512, 2 * deep :] = dot(back_turned[a : a + 512, :], hidden_ref[...]).astype(BF)

        pl.when(step < 4)(lambda: store(other))
        pl.when(step >= 4)(lambda: store(mine))

    return call(
        kernel,
        [((4, width, 3 * deep), BF)] * 2,
        [rows, back, back_pre, hidden],
        [
            WHOLE,
            WHOLE,
            pl.BlockSpec((count, 2 * deep), lambda i: (0, (i + 4) % 8)),
            pl.BlockSpec((count, deep), lambda i: (0, (i + 4) % 8)),
        ],
        [pltpu.VMEM((width, count), BF)] * 2,
        grid=(8,),
        out_specs=[
            pl.BlockSpec((1, width, 3 * deep), lambda i: (jnp.maximum(i - 4, 0), 0, 0)),
            pl.BlockSpec((1, width, 3 * deep), lambda i: (jnp.minimum(i, 3), 0, 0)),
        ],
    )


def experts_finish(place, sums):
    width, deep = sums[0].shape[0], sums[0].shape[1] // 3

    def kernel(at, s0, s1, s2, s3, grad_gate, grad_up, grad_down):
        def store(ref, which):
            grad_gate[0, which] = ref[:, :deep].astype(F32)
            grad_up[0, which] = ref[:, deep : 2 * deep].astype(F32)
            grad_down[0, which] = ref[:, 2 * deep :].astype(F32).T

        @pl.when(at[0] == 0)
        def _():
            store(s0, 0)
            store(s2, 1)

        @pl.when(at[0] == 1)
        def _():
            store(s1, 1)
            store(s3, 0)

    return call(
        kernel,
        [((1, 2, width, deep), F32)] * 2 + [((1, 2, deep, width), F32)],
        [place, *sums],
        [SCALARS] + [WHOLE] * 4,
    )


def middle_rows(entry, pieces, gain, names, router, place, layer, copies):
    share, width = entry.shape
    top = names.shape[1]
    beside = 0 if layer else BESIDE
    count = router[0].shape[0]

    def kernel(at, entry_ref, a, b, c, d, gain_own, gain_other, names_ref, router_own, router_other,
               middle, out, shaped, gates):
        total = entry_ref[...].astype(F32)
        for ref in (a, b, c, d):
            total = total + ref[...].astype(F32)
        middle[...] = total
        rows = (total * inverse_level(total) * of_layer(layer, at[0], gain_own, gain_other)).astype(BF)
        shaped[...] = rows
        numbers = names_ref[...].astype(F32)
        lane = lax.broadcasted_iota(jnp.int32, (share, BESIDE), 1)
        extra = jnp.zeros((share, BESIDE), F32)
        for j in range(top):
            extra = jnp.where(lane == j, numbers[:, j : j + 1], extra)
        for k in range(copies):
            out[k, :, :width] = rows
            if beside:
                out[k, :, width:] = extra.astype(BF)
        table = of_layer(layer, at[0], router_own, router_other).astype(BF)
        gates[...] = gate_table(rows, numbers, table)

    return call(
        kernel,
        [((share, width), F32), ((copies, share, width + beside), BF), ((share, width), BF), ((share, count), F32)],
        [place, entry, *pieces, *gain, names, *router],
        [SCALARS] + [WHOLE] * 10,
    )


def leave_rows(middle, pieces, beside=()):
    share, width = middle.shape
    extra = len(beside)

    def kernel(middle_ref, pieces_ref, *refs):
        total = middle_ref[...]
        for k in range(pieces_ref.shape[0]):
            total = total + pieces_ref[k].astype(F32)
        refs[-1][:share, :] = total.astype(BF)
        for k in range(extra):
            refs[-1][share * (k + 1) : share * (k + 2), :] = refs[k][...]

    return call(
        kernel, [((share * (1 + extra), width), BF)], [middle, pieces, *beside], [WHOLE] * (2 + extra)
    )[0]


def back_middle_rows(flow, pieces, middle, shaped, gates, gain, router, place, layer):
    share, width = middle.shape
    count = gates.shape[1]

    def kernel(at, flow_ref, pieces_ref, middle_ref, shaped_ref, gates_ref, gain_own, gain_other, router_own,
               router_other, back, rounded, small):
        total = jnp.zeros((share, width), F32)
        inner = jnp.zeros((share, count), F32)
        number = lax.broadcasted_iota(jnp.int32, (share, count), 1)
        for p in range(pieces_ref.shape[0]):
            total = total + pieces_ref[p, :, :width].astype(F32)
            beside = pieces_ref[p, :, width:].astype(F32)
            for k, e in enumerate((2 * p + at[0], 2 * p + 1 - at[0])):
                value = beside[:, 2 * k : 2 * k + 1] + beside[:, 2 * k + 1 : 2 * k + 2]
                inner = jnp.where(number == e, value, inner)
        own = gates_ref[...]
        slope = jnp.sum(own * inner, axis=-1, keepdims=True)
        logits = (own * (inner - slope)).astype(BF)
        table = of_layer(layer, at[0], router_own, router_other).astype(BF)
        total = total + dot(logits, table)
        gain_row = of_layer(layer, at[0], gain_own, gain_other)
        level, grad = norm_back(total, middle_ref[...], gain_row)
        total = flow_ref[...].astype(F32) + level
        back[...] = total
        rounded[...] = total.astype(BF)
        grad_router = contract_rows(logits, shaped_ref[...])
        row = lax.broadcasted_iota(jnp.int32, (64 - count, 128), 0)
        for i in range(width // 128):
            columns = slice(128 * i, 128 * (i + 1))
            small[64 * i : 64 * i + count, :] = grad_router[:, columns]
            small[64 * i + count : 64 * (i + 1), :] = jnp.where(row == 0, grad[:, columns], 0.0)

    return call(
        kernel,
        [((share, width), F32), ((share, width), BF), ((width // 2, 128), F32)],
        [place, flow, pieces, middle, shaped, gates, *gain, *router],
        [SCALARS] + [WHOLE] * 9,
    )


def back_entry_rows(back, pieces, entry, gain, place, layer, copies, beside=()):
    share, width = back.shape
    extra = sum(rows.shape[0] for rows in beside)

    def kernel(at, back_ref, a, b, c, d, entry_ref, gain_own, gain_other, *refs):
        more, (out, grad_gain, *spread) = refs[: len(beside)], refs[len(beside) :]
        total = a[...].astype(F32) + b[...].astype(F32) + c[...].astype(F32) + d[...].astype(F32)
        level, grad = norm_back(
            total, entry_ref[...].astype(F32), of_layer(layer, at[0], gain_own, gain_other)
        )
        flow = (back_ref[...] + level).astype(BF)
        out[:share, :] = flow
        start = share
        for ref in more:
            out[start : start + ref.shape[0], :] = ref[...]
            start += ref.shape[0]
        grad_gain[...] = grad
        for ref in spread:
            for k in range(copies):
                ref[k] = flow

    outs = [((share + extra, width), BF), ((1, width), F32)]
    if copies:
        outs.append(((copies, share, width), BF))
    return call(
        kernel,
        outs,
        [place, back, *pieces, entry, *gain, *beside],
        [SCALARS] + [WHOLE] * (8 + len(beside)),
    )


def straight_rows(place, entered, final):
    share, width = entered[0].shape
    rows = 4 * share

    def kernel(at, *refs):
        blocks, finals, (own, other) = refs[:4], refs[4:8], refs[8:]
        here = at[0] == 0
        for k in range(4):
            start = share * lax.rem(at[1] + k, 4)
            values = blocks[k][...].astype(F32), finals[k][...].astype(F32)
            pairs = (
                (values[0], values[1][share : 2 * share]),
                (values[1][:share], values[1][2 * share :]),
            )
            for n, (zero, one) in enumerate(pairs):
                spot = pl.ds(pl.multiple_of(rows * n + start, share), share)
                own[spot, :] = jnp.where(here, zero, one).astype(BF)
                other[spot, :] = jnp.where(here, one, zero).astype(BF)

    return call(
        kernel,
        [((2 * rows, width), BF)] * 2,
        [place, *entered, *final],
        [SCALARS] + [WHOLE] * 8,
    )


def by_batch(place, own, other):
    rows, width = own.shape[0] // 2, own.shape[1]

    def kernel(at, own_ref, other_ref, activations, input_grads):
        for n, out in enumerate((activations, input_grads)):
            out[0, at[0]] = own_ref[rows * n : rows * (n + 1), :]
            out[0, 1 - at[0]] = other_ref[rows * n : rows * (n + 1), :]

    return call(
        kernel, [((1, 2, rows, width), BF)] * 2, [place, own, other], [SCALARS] + [WHOLE] * 2
    )


def per_device(
    inputs,
    cotangent,
    documents,
    routes,
    gain_attn,
    w_query,
    w_key,
    w_value,
    w_out,
    gain_moe,
    w_router,
    w_gate,
    w_up,
    w_down,
):
    section = lax.axis_index("section")
    expert = lax.axis_index("expert")
    tensor = lax.axis_index("tensor")
    sequences = lax.axis_size("expert")
    first = section == 0
    place = jnp.stack([section, tensor, expert]).astype(jnp.int32)
    rows, width = inputs.shape[1:]
    share = rows // 4
    expert_count = w_router.shape[2]
    own_weights = [w_query[0], w_key[0], w_value[0], w_out[0]]

    def own_rows(array):
        start = (section, share * tensor, 0)
        return lax.dynamic_slice(array, start, (1, share, array.shape[2]))[0]

    kept, given = prepare_experts(place, w_gate[0], w_up[0], w_down[0])
    given = sibling(given)
    quarter, *parts = choose_experts(place, kept, given, 0, width // 2)
    sides = start_gather(*parts)
    weights = own_weights + [sibling(w) for w in own_weights]

    gains_a = [gain_attn, sibling(gain_attn)]
    gains_m = [gain_moe, sibling(gain_moe)]
    routers = [w_router[0].T, sibling(w_router[0].T)]
    tables = prepare_tables(place, documents, w_query.shape[2] + w_key.shape[2])
    names_own = own_rows(routes)
    top = routes.shape[2]
    flow = own_rows(cotangent)

    entry = [own_rows(inputs), None]
    attn_saved, middles, shapeds, gates_own, arrived = ([None, None] for _ in range(5))
    pieces, attn_saved[0] = attention_forward([after(inputs, quarter)], tables, weights, gains_a, place, 0)
    quarter_one, *parts = choose_experts(
        place, kept, after(given, pieces[0]), 1, width // 8 * 7
    )
    pieces = arrivals(after(pieces, *sides, quarter_one))
    middles[0], copies, shapeds[0], gates_own[0] = middle_rows(
        entry[0], pieces, gains_m, names_own, routers, place, 0, sequences
    )
    mine = [quarter, *sides, *end_gather(after(quarter, *pieces), *sides)]
    expert_weights = [[*mine, *[sibling(block) for block in mine]], None]
    arrived[0] = exchange_e(copies).reshape(-1, width + BESIDE)
    backs = [None, spread_e(after(flow, copies)).reshape(-1, width)]
    arrived[0] = after(arrived[0], *mine[3:])
    parts = after(tuple(parts), *mine[3:])
    sides = start_gather(*parts)
    terms, pre, gates, names = experts_forward(arrived[0], top, routers, expert_weights[0], place, 0)
    terms = after(terms, backs[1])
    pieces = exchange_e(terms.reshape(-1, share, width))
    mine = [quarter_one, *sides, *end_gather(quarter_one, *sides)]
    expert_weights[1] = [*mine, *[sibling(block) for block in mine]]
    entry[1] = leave_rows(middles[0], after(pieces, *mine[3:]))

    blocks = gather_x(entry[1])
    outputs = [blocks, None]
    pieces, attn_saved[1] = attention_forward(blocks, tables, weights, gains_a, place, 1)
    pieces = arrivals(pieces)
    middles[1], copies, shapeds[1], gates_own[1] = middle_rows(
        entry[1], pieces, gains_m, names_own, routers, place, 1, sequences
    )
    arrived[1] = exchange_e(copies).reshape(-1, width)
    terms, back_pre, hidden = experts_both(
        arrived[1], names, top, routers, backs[1], expert_weights[1], place, 1
    )

    def start_ring(mines, others):
        half = width // 2
        two = sum_of([mines[2], others[2]])
        return shifted(two[:half], "tensor", 1), shifted(two[half:], "tensor", -1)

    def ring_parts(mines, others, low, high):
        half = width // 2
        return (
            jnp.concatenate(
                [sum_of([mines[1, :half], others[1, :half], low]), sum_of([mines[1, half:], others[1, half:]])]
            ),
            jnp.concatenate(
                [sum_of([mines[3, :half], others[3, :half]]), sum_of([mines[3, half:], others[3, half:], high])]
            ),
        )

    def end_ring(first, third):
        return shifted(first, "tensor", 1), shifted(third, "tensor", -1)

    in_blocks, smalls, grads_gain = ([None, None] for _ in range(3))
    pieces = exchange_e(terms.reshape(-1, share, width + BESIDE))
    mines, others = experts_grads(arrived[1], backs[1], back_pre, hidden)
    outs = experts_out(hidden, expert_weights[1])
    back_middle, rounded, smalls[1] = back_middle_rows(
        flow, after(pieces, mines, others, outs), middles[1], shapeds[1], gates_own[1], gains_m, routers, place, 1
    )
    others = sibling(after(others, rounded))
    out_pieces = exchange_e(after(outs, rounded).reshape(-1, share, width))
    partial, branch, back_qkv = attention_backward(
        gather_x(rounded), attn_saved[1], tables, weights, place, 1
    )
    flow, grads_gain[1], copies = back_entry_rows(
        back_middle, arrivals(partial), entry[1], gains_a, place, 1, sequences
    )
    copies = after(copies, out_pieces)
    backs[0] = exchange_e(copies).reshape(-1, width)
    last = leave_rows(middles[1], out_pieces, (flow,))
    mine_half, other_half = attention_grads(place, after(back_qkv, last), attn_saved[1], branch)
    mines = after(mines, last)
    twos = start_ring(mines, others)
    half_one = sum_of([mine_half, sibling(other_half)])
    backs[0] = after(backs[0], half_one, *twos)
    ends = end_ring(*ring_parts(mines, others, *twos))
    own = sum_of([mines[0], others[0]])

    piece = collect_e(after(half_one, backs[0]).reshape(sequences, -1, half_one.shape[1]))
    terms, back_pre, hidden = experts_backward(backs[0], pre, gates, expert_weights[0])
    terms = after(terms, piece)
    pieces = exchange_e(terms.reshape(-1, share, width + BESIDE))
    mines, others = experts_grads(arrived[0], backs[0], back_pre, hidden)
    sums = [None, sum_of([own, *ends])]
    piece_one = piece
    pieces = after(pieces, mines, others, sums[1])
    back_middle, rounded, smalls[0] = back_middle_rows(
        flow, pieces, middles[0], shapeds[0], gates_own[0], gains_m, routers, place, 0
    )
    others = sibling(after(others, rounded))

    def own_layer(of_first, of_second):
        own = jnp.where(first, of_first, of_second)
        return own + sibling(jnp.where(first, of_second, of_first).astype(BF)).astype(F32)

    small = own_layer(smalls[0], smalls[1]).astype(BF)
    gathered = after(gather_x(rounded), small)
    partial, branch, back_qkv = attention_backward(gathered, attn_saved[0], tables, weights, place, 0)
    mine_half, other_half = attention_grads(place, back_qkv, attn_saved[0], branch)
    half_zero = jnp.concatenate([sum_of([mine_half, sibling(other_half)]), small], axis=1)
    cut = half_zero.shape[1]
    both = jnp.concatenate(
        [
            half_zero.reshape(sequences, -1, cut),
            jnp.broadcast_to(piece_one[None], (sequences, *piece_one.shape)),
        ],
        axis=2,
    )
    pieces = after(arrivals(partial), both)
    both = exchange_e(both)
    final, grads_gain[0] = back_entry_rows(
        back_middle, pieces, entry[0], gains_a, place, 0, 0, (last,)
    )

    finals = gather_x(final)
    twos = start_ring(after(mines, *finals[1:]), others)
    piece = jnp.sum(both[:, :, :cut].astype(F32), axis=0).astype(BF)
    done_one = both.reshape(half_one.shape[0], -1)[:, cut:]
    gain = own_layer(grads_gain[0], grads_gain[1]).reshape(width // 128, 128).astype(BF)
    gain = jnp.pad(gain, ((0, piece.shape[0] - width // 128), (0, 0)))
    piece = jnp.concatenate([piece, gain], axis=1)
    mine, other = straight_rows(place, outputs[0], finals)
    activations, input_grads = by_batch(place, mine, sibling(other))
    parts = ring_parts(after(mines, activations), others, *twos)
    ends = end_ring(*parts)
    sums[0] = sum_of([mines[0], others[0], *ends])
    grad_gate, grad_up, grad_down = experts_finish(
        place, [*sums, to_core(sums[0], 0), to_core(sums[1], 1)]
    )
    moved_one = to_core(done_one, 1)
    spread = after(spread_e(piece), grad_gate, moved_one)
    gain = jnp.sum(spread[:, : width // 128, -128:].astype(F32), axis=0).astype(BF)
    done_zero = spread.reshape(half_one.shape[0], -1)
    small = jnp.concatenate([done_zero[:, -256:-128], gain], axis=0)
    blocks = gather_x(small)
    widths = [w_query.shape[2], w_key.shape[2], w_value.shape[2]]
    begun = attention_finish(place, done_zero, done_one, widths, False)
    grad_query, grad_key, grad_value, grad_out = attention_finish(
        place, to_core(done_zero, 0), moved_one, widths, True, begun
    )
    grad_router, grad_gain_m, gain = small_finish(after(blocks, grad_query), expert_count)
    return (
        activations,
        input_grads,
        gain,
        grad_query,
        grad_key,
        grad_value,
        grad_out,
        grad_gain_m,
        grad_router.T[None],
        grad_gate,
        grad_up,
        grad_down,
    )


def solution(mesh):
    in_specs = (
        P(None, "expert", None),
        P(None, "expert", None),
        P(None, "expert", None),
        P(None, "expert", None),
        P("section", None),
        P("section", None, "tensor"),
        P("section", None, "tensor"),
        P("section", None, "tensor"),
        P("section", "tensor", None),
        P("section", None),
        P("section", None, None),
        P("section", "expert", None, "tensor"),
        P("section", "expert", None, "tensor"),
        P("section", "expert", "tensor", None),
    )
    out_specs = (
        P("section", None, "expert", None),
        P("section", None, "expert", None),
        P("section", None),
        P("section", None, "tensor"),
        P("section", None, "tensor"),
        P("section", None, "tensor"),
        P("section", "tensor", None),
        P("section", None),
        P("section", None, None),
        P("section", "expert", None, "tensor"),
        P("section", "expert", None, "tensor"),
        P("section", "expert", "tensor", None),
    )
    return jax.shard_map(
        per_device, mesh=mesh, in_specs=in_specs, out_specs=out_specs, check_vma=False
    )
```
